32 devices in a mesh: node: 16 (over z, x, core), head: 2 (over y).
Axes of the slice: x: 2, y: 2, z: 4, core: 2. Of those that a mesh axis runs over, the one named last changes fastest.
Arguments:
- features: bfloat16 [65536, 512], P(('node', 'head')), may hold values from -8 to 8
- w_query: bfloat16 [512, 512], replicated, may hold values from -0.25 to 0.25
- w_key_value: bfloat16 [512, 2, 512], replicated, may hold values from -0.25 to 0.25
- edge_local: float32 [512], P('head'), may hold values from 0.5 to 2
- edge_expand: float32 [512], P('head'), may hold values from 0.5 to 2
- local_cols: int32 [512, 8], P('node'), may hold values from 0 to 35, as said below
- exp_rows: int32 [16, 4, 16], P('node'), may hold values from 0 to 31
- exp_cols: int32 [16, 4, 16], P('node'), may hold values from 0 to 31
Outputs:
- attention: bfloat16 [65536, 512], P(('node', 'head'))
The draws below stay inside these ranges and needn't reach their ends.
Inputs may be any that keep to these rules, and one draw needn't show every extreme that they name: `local_cols`: the first slot of every row names a tile of the row's own node block, a value from 2 to 33.
All inputs are finite; a program needn't handle non-finite values.
Results may differ from the reference program's by a relative error of at most 0.009.
Values may be sent and summed in bfloat16 or wider, within the bound.
No kernel may reach another device: no remote copies, remote signals or barrier semaphores. Data moves between devices by JAX's collectives and lax.ppermute only.
A program may use at most 128 MiB of HBM per device.

```python
import math
import jax
import jax.numpy as jnp
from jax import lax

D = 512
HEADS = 8
HDIM = 64
TILE = 128
RT = 32
HT = 2
LPR = 8
MATCH = 4
ET = 16
ROWS = 4096
NODES = 65536
N_NODE = 16


def draw_local_cols(key, part):
    key = jax.random.fold_in(key, 11)
    first_key, rest_key = jax.random.split(key)
    first = jax.random.randint(first_key, (NODES // TILE, 1), HT, HT + RT)
    rest = jax.random.randint(rest_key, (NODES // TILE, LPR - 1), 0, RT + 2 * HT)
    return jnp.concatenate([first, rest], axis=1).astype(jnp.int32)


def with_ends(entries, own_key, smallest, high):
    shape = entries.shape
    spot = [jax.random.randint(jax.random.fold_in(own_key, axis), (), 0, shape[axis]) for axis in range(len(shape))]
    entries = entries.at[tuple(spot)].set(smallest)
    longest = shape.index(max(shape))
    spot[longest] = (spot[longest] + 1) % shape[longest]
    return entries.at[tuple(spot)].set(high)


def shard_levels(stream_key, extent, cuts, smallest, top_value):
    factor_of, own = 1.0, jax.random.fold_in(stream_key, 6)
    for position, parts in cuts:
        heights = jnp.exp(jax.random.uniform(jax.random.fold_in(own, position), (parts,), jnp.float32, smallest / len(cuts), top_value / len(cuts)))
        factor_of = factor_of * jnp.repeat(heights, extent[position] // parts).reshape([-1 if axis == position else 1 for axis in range(len(extent))])
    return factor_of


def gaussian(own_key, shape, width, most, cuts=(), kind=jnp.bfloat16):
    values = jax.random.normal(own_key, shape, jnp.float32) * width
    if len(cuts) > 0:
        values = shard_levels(own_key, shape, cuts, -0.22, 0.18) * values
    return jnp.clip(values, min=-most, max=most).astype(kind)


def setup_inputs(seed: int = 0) -> dict:
    key_list = jax.random.split(jax.random.key(seed), 9)
    return {
        "features": gaussian(key_list[0], (NODES, D), 1.0, 8.0, ((0, 32),)),
        "w_query": gaussian(key_list[1], (D, D), D ** -0.5, 0.25),
        "w_key_value": gaussian(key_list[2], (D, 2, D), D ** -0.5, 0.25),
        "edge_local": jnp.clip(jnp.exp(math.log(2.0) - 1.3862944 * jax.random.uniform(key_list[3], (D,), jnp.float32) ** shard_levels(key_list[3], (D,), ((0, 2),), -0.2, 0.2)), 0.5, 2.0),
        "edge_expand": jnp.clip(jnp.exp(math.log(2.0) - 1.3862944 * jax.random.uniform(key_list[4], (D,), jnp.float32) ** shard_levels(key_list[4], (D,), ((0, 2),), -0.2, 0.2)), 0.5, 2.0),
        "local_cols": draw_local_cols(jax.random.fold_in(key_list[8], 71), 0),
        "exp_rows": with_ends(jax.random.randint(key_list[6], (N_NODE, MATCH, ET), 0, RT), jax.random.fold_in(key_list[6], 1), 0, RT - 1).astype(jnp.int32),
        "exp_cols": with_ends(jax.random.randint(key_list[7], (N_NODE, MATCH, ET), 0, RT), jax.random.fold_in(key_list[7], 1), 0, RT - 1).astype(jnp.int32),
    }


highest = lax.Precision.HIGHEST

def attend(queries, key_block, value_block, usable):
    scores = jnp.einsum('gqhe,gkhe->ghqk', queries.astype(jnp.float32), key_block.astype(jnp.float32), precision=highest)
    weights = jnp.exp(jnp.clip(scores, -5.0, 5.0))
    weights = jnp.where(usable[:, None, None, :], weights, jnp.zeros_like(weights))
    denominator = lax.optimization_barrier(jnp.sum(weights, axis=3))
    rounded = lax.optimization_barrier(weights.astype(jnp.bfloat16)).astype(jnp.float32)
    numerator = jnp.einsum('ghqk,gkhe->gqhe', rounded, value_block.astype(jnp.float32), precision=highest)
    return (numerator, jnp.transpose(denominator, (0, 2, 1)))

def local_part(queries, extended, columns, first_tile, tile_count, tile_rows, halo_tiles):
    row_count, head_count, head_width = queries.shape
    row_tiles = row_count // tile_rows
    group_size = min(row_tiles, max(1, 512 // tile_rows))
    group_count = row_tiles // group_size
    ext_tiles = extended.reshape(-1, tile_rows, extended.shape[1])
    grouped_queries = queries.reshape(group_count, group_size, tile_rows, head_count, head_width)
    grouped_columns = columns.reshape(group_count, group_size, columns.shape[1])

    def one_group(pair):
        block_queries, block_columns = pair
        picked = ext_tiles[block_columns].reshape(group_size, -1, 2, head_count, head_width)
        global_tile = first_tile + block_columns - halo_tiles
        usable = jnp.logical_and(global_tile >= 0, global_tile < tile_count)
        usable = jnp.repeat(usable, tile_rows, axis=1)
        return attend(block_queries, picked[:, :, 0], picked[:, :, 1], usable)
    numerator, denominator = lax.map(one_group, (grouped_queries, grouped_columns))
    return (numerator.reshape(row_count, head_count, head_width), denominator.reshape(row_count, head_count))

def expander_part(queries, key_tiles, row_index):
    row_count, head_count, head_width = queries.shape
    tile_rows = key_tiles.shape[1]
    row_tiles = row_count // tile_rows
    pair_count = key_tiles.shape[0]
    chosen = queries.reshape(row_tiles, tile_rows, head_count, head_width)[row_index]
    pairs = key_tiles.reshape(pair_count, tile_rows, 2, head_count, head_width)
    usable = jnp.ones((pair_count, tile_rows), dtype=jnp.bool_)
    numerator, denominator = attend(chosen, pairs[:, :, 0], pairs[:, :, 1], usable)
    selector = (row_index[None, :] == jnp.arange(row_tiles, dtype=jnp.int32)[:, None]).astype(jnp.float32)
    numerator = jnp.einsum('te,eqhw->tqhw', selector, numerator, precision=highest)
    denominator = jnp.einsum('te,eqh->tqh', selector, denominator, precision=highest)
    return (numerator.reshape(row_count, head_count, head_width), denominator.reshape(row_count, head_count))

def reference(features, w_query, w_key_value, edge_local, edge_expand, local_cols, exp_rows, exp_cols):
    scale = 1.0 / math.sqrt(HDIM)
    queries = jnp.dot(features, w_query, preferred_element_type=jnp.float32).astype(jnp.bfloat16)
    key_values = jnp.dot(features, w_key_value.reshape(D, 2 * D), preferred_element_type=jnp.float32).astype(jnp.bfloat16)
    query_wide = lax.optimization_barrier(queries).astype(jnp.float32)
    local_q = (query_wide * edge_local * scale).astype(jnp.bfloat16).reshape(NODES, HEADS, HDIM)
    expand_q = (query_wide * edge_expand * scale).astype(jnp.bfloat16).reshape(NODES, HEADS, HDIM)
    margin = HT * TILE
    padded = jnp.pad(key_values, ((margin, margin), (0, 0)))
    log_count = N_NODE.bit_length() - 1
    tile_count = N_NODE * RT

    def one_block(block):
        start = block * ROWS
        block_local = lax.dynamic_slice_in_dim(local_q, start, ROWS, 0)
        block_expand = lax.dynamic_slice_in_dim(expand_q, start, ROWS, 0)
        extended = lax.dynamic_slice_in_dim(padded, start, ROWS + 2 * margin, 0)
        columns = lax.dynamic_slice_in_dim(local_cols, block * RT, RT, 0)
        numerator, denominator = local_part(block_local, extended, columns, block * RT, tile_count, TILE, HT)
        tile_list = []
        row_list = []
        for matching in range(MATCH):
            partner = jnp.bitwise_xor(block, jnp.int32(1 << matching * log_count // 4))
            partner_block = lax.dynamic_slice_in_dim(key_values, partner * ROWS, ROWS, 0).reshape(RT, TILE, 2 * D)
            tile_list.append(partner_block[exp_cols[block, matching]])
            row_list.append(exp_rows[block, matching])
        extra_num, extra_den = expander_part(block_expand, jnp.concatenate(tile_list, axis=0), jnp.concatenate(row_list, axis=0))
        result = (numerator + extra_num) / (denominator + extra_den)[:, :, None]
        return result.astype(jnp.bfloat16).reshape(ROWS, D)
    blocks = lax.map(one_block, jnp.arange(N_NODE, dtype=jnp.int32))
    return blocks.reshape(NODES, D)
```

```python
import functools
import math

import jax
import jax.numpy as jnp
from jax import lax
from jax.experimental import pallas as pl
from jax.experimental.pallas import tpu as pltpu
from jax.sharding import PartitionSpec as P

HEADS = 8
TILE = 128
HT = 2
MATCH = 4
LANES = 128
GROUP = 4
MIB = 1024 * 1024

ANY = pl.BlockSpec(memory_space=pl.ANY)
SMEM = pl.BlockSpec(memory_space=pltpu.SMEM)
VMEM = pl.BlockSpec(memory_space=pltpu.VMEM)
HBM = pl.BlockSpec(memory_space=pltpu.HBM)


def piece_copies(pieces, target, sems):
    copies = []
    start = 0
    for index, piece in enumerate(pieces):
        size = piece.shape[0]
        copies.append(
            pltpu.make_async_copy(piece, target.at[pl.ds(start, size)], sems.at[index])
        )
        start += size
    return copies


def lane_masks():
    lane = lax.broadcasted_iota(jnp.int32, (TILE, LANES), 1)
    return lane < LANES // 2, lane % (LANES // 2)


def pack_denominators(pieces):
    _, within = lane_masks()
    size = LANES // 2 // len(pieces)
    packed = pieces[-1]
    for pair in range(len(pieces) - 2, -1, -1):
        packed = jnp.where(within < (pair + 1) * size, pieces[pair], packed)
    return packed


def spread_denominators(packed, pairs):
    size = LANES // 2 // pairs
    inverse = 1.0 / packed
    coarse = inverse.astype(jnp.bfloat16)
    fine = (inverse - coarse.astype(jnp.float32)).astype(jnp.bfloat16)
    shape = (2 * LANES, pairs * LANES)
    source = lax.broadcasted_iota(jnp.int32, shape, 0) % LANES
    target = lax.broadcasted_iota(jnp.int32, shape, 1)
    wanted = target // LANES * size + (target % LANES) // (LANES // 2) * (LANES // 2)
    chooser = jnp.where(source == wanted, 1.0, 0.0).astype(jnp.bfloat16)
    return jnp.dot(
        jnp.concatenate([coarse, fine], axis=1), chooser, preferred_element_type=jnp.float32
    )


def project(rows, w, keys, values, first):
    new_keys = jnp.dot(rows, w[0], preferred_element_type=jnp.float32).astype(jnp.bfloat16).T
    new_values = jnp.dot(rows, w[1], preferred_element_type=jnp.float32).astype(jnp.bfloat16)
    for index in range(rows.shape[0] // TILE):
        span = slice(index * TILE, (index + 1) * TILE)
        keys[first + index] = new_keys[:, span]
        values[first + index] = new_values[span, :]


def attend_row(queries, keys, values, ones, tiles):
    low, _ = lane_masks()
    low_mask = jnp.where(low, 1.0, 0.0).astype(jnp.bfloat16)
    high_mask = jnp.where(low, 0.0, 1.0).astype(jnp.bfloat16)
    results = []
    for pair in range(queries.shape[1] // LANES):
        part = slice(pair * LANES, (pair + 1) * LANES)
        both = jnp.concatenate([queries[:, part] * low_mask, queries[:, part] * high_mask], axis=0)
        weights = []
        for start in range(0, len(tiles), 2):
            slab = jnp.concatenate([keys[tile, part, :] for tile in tiles[start : start + 2]], axis=1)
            scores = jnp.dot(both, slab, preferred_element_type=jnp.float32)
            weights.append(jnp.exp(jnp.clip(scores, -5.0, 5.0)).astype(jnp.bfloat16))
        weights = jnp.concatenate(weights, axis=1)
        wide = jnp.concatenate(
            [
                jnp.concatenate([values[tile, :, part], ones[0]], axis=1) for tile in tiles[:-1]
            ]
            + [jnp.concatenate([values[tiles[-1], :, part] * ones[1], ones[1]], axis=1)],
            axis=0,
        )
        sums = jnp.dot(weights, wide, preferred_element_type=jnp.float32)
        results.append(
            (
                jnp.where(low, sums[:TILE, :LANES], sums[TILE:, :LANES]),
                jnp.where(low, sums[:TILE, LANES:], sums[TILE:, LANES:]),
            )
        )
    return results


def attend_units(queries, keys, values, num, den, units):
    low_lanes, _ = lane_masks()
    low = jnp.where(low_lanes, 1.0, 0.0).astype(jnp.bfloat16)
    high = jnp.where(low_lanes, 0.0, 1.0).astype(jnp.bfloat16)
    nothing = jnp.zeros((LANES // 2, TILE), jnp.bfloat16)
    rows = [pl.ds(pl.multiple_of(row * TILE, TILE), TILE) for row, _ in units]
    last = queries.shape[0] // TILE - 1
    query_rows = [
        pl.ds(pl.multiple_of(jnp.minimum(row, last) * TILE, TILE), TILE) for row, _ in units
    ]
    denominators = [[] for _ in units]
    for pair in range(queries.shape[1] // LANES):
        part = slice(pair * LANES, (pair + 1) * LANES)
        middle = pair * LANES + LANES // 2
        weights = []
        for row, (_, tile) in zip(query_rows, units):
            first = jnp.concatenate([keys[tile, pair * LANES : middle, :], nothing], axis=0)
            second = jnp.concatenate([nothing, keys[tile, middle : (pair + 1) * LANES, :]], axis=0)
            scores = jnp.dot(
                queries[row, part],
                jnp.concatenate([first, second], axis=1),
                preferred_element_type=jnp.float32,
            )
            weights.append(jnp.exp(jnp.clip(scores, -5.0, 5.0)).astype(jnp.bfloat16))
        sums = []
        for weight, (_, tile) in zip(weights, units):
            value = values[tile, :, part]
            wide = jnp.concatenate(
                [
                    jnp.concatenate([value * low, low], axis=1),
                    jnp.concatenate([value * high, high], axis=1),
                ],
                axis=0,
            )
            sums.append(jnp.dot(weight, wide, preferred_element_type=jnp.float32))
        for row, both, listed in zip(rows, sums, denominators):
            num[row, part] += both[:, :LANES]
            listed.append(both[:, LANES:])
    for row, listed in zip(rows, denominators):
        den[row, :] += pack_denominators(listed)


def sums_copies(num, den, num_out, den_out, sems, inward):
    rows = num_out.shape[0]
    copies = []
    for index, (here, there) in enumerate([(num, num_out), (den, den_out)]):
        here = here.at[pl.ds(0, rows)]
        source, target = (there, here) if inward else (here, there)
        copies.append(pltpu.make_async_copy(source, target, sems.at[index]))
    return copies


def project_pieces(pieces, w, keys, values, at):
    for piece in pieces:
        tiles = piece.shape[0] // TILE
        size = math.gcd(tiles, GROUP)

        def some_tiles(index, carry, piece=piece, at=at, size=size):
            some = piece[pl.ds(pl.multiple_of(index * size * TILE, TILE), size * TILE), :]
            project(some, w, keys, values, at + index * size)
            return carry

        lax.fori_loop(0, tiles // size, some_tiles, 0)
        at += tiles


def attend_rows(span, fresh, place_ref, cols_ref, where_ref, local_ref, keys, values, sums, scratch):
    num, den, num_out, den_out = sums
    ones, list_ref, sems = scratch
    width = num.shape[1]
    tiles_here = local_ref.shape[0] // TILE
    slots = cols_ref.shape[1]
    ones[0] = jnp.ones(ones.shape[1:], ones.dtype)
    ones[1] = jnp.zeros(ones.shape[1:], ones.dtype)

    def one_row(row, carry):
        target = pl.ds(pl.multiple_of(row * TILE, TILE), TILE)
        half = row // (tiles_here // 2)
        found = jnp.int32(0)
        for slot in range(slots):
            tile = where_ref[half, cols_ref[place_ref[0] * tiles_here + row, slot]]
            list_ref[found] = tile
            found = found + (tile >= 0).astype(jnp.int32)
        list_ref[found] = 0
        odd = lax.rem(found, 2)
        if fresh:

            @pl.when(found == 0)
            def _():
                num[target, :] = jnp.zeros((TILE, width), jnp.float32)
                den[target, :] = jnp.zeros((TILE, LANES), jnp.float32)

        for chunks in range(1, slots // 2 + 1):

            @pl.when((found + 1) // 2 == chunks)
            def _():
                tiles = [list_ref[index] for index in range(2 * chunks)]
                units = (ones[0], ones[odd])
                results = attend_row(local_ref[target, :], keys, values, units, tiles)
                packed = pack_denominators([denominator for _, denominator in results])
                for pair, (numerator, _) in enumerate(results):
                    part = slice(pair * LANES, (pair + 1) * LANES)
                    num[target, part] = numerator if fresh else num[target, part] + numerator
                den[target, :] = packed if fresh else den[target, :] + packed

        for index, (here, there) in enumerate([(num, num_out), (den, den_out)]):
            pltpu.make_async_copy(here.at[target], there.at[target], sems.at[index]).start()
        return carry

    lax.fori_loop(*span, one_row, 0)
    every = pl.ds(span[0] * TILE, (span[1] - span[0]) * TILE)
    for index, (here, there) in enumerate([(num, num_out), (den, den_out)]):
        pltpu.make_async_copy(here.at[every], there.at[every], sems.at[index]).wait()


def own_kernel(span, place_ref, cols_ref, where_ref, rows, w, wq, scales, *refs):
    (num_out, den_out, keys, values, local_ref, expand_ref, num, den, *scratch) = refs
    width = rows.shape[1]
    tiles = rows.shape[0] // TILE
    size = min(GROUP, tiles)
    project_pieces([rows], w, keys, values, 0)

    def some_queries(index, carry):
        target = pl.ds(pl.multiple_of(index * size * TILE, TILE), size * TILE)
        queries = jnp.dot(rows[target, :], wq[...], preferred_element_type=jnp.float32)
        queries = queries.astype(jnp.bfloat16).astype(jnp.float32)
        scale = 1.0 / math.sqrt(width // HEADS)
        local_ref[target, :] = (queries * scales[0:1, :] * scale).astype(jnp.bfloat16)
        expand_ref[target, :] = (queries * scales[1:2, :] * scale).astype(jnp.bfloat16)
        return carry

    lax.fori_loop(0, tiles // size, some_queries, 0)
    sums = (num, den, num_out, den_out)
    attend_rows(span, True, place_ref, cols_ref, where_ref, local_ref, keys, values, sums, scratch)


def near_kernel(span, count, place_ref, cols_ref, where_ref, *refs):
    pieces = refs[:count]
    (w, local_ref, own_keys, own_values, _, _, num_out, den_out) = refs[count : count + 8]
    (num, den, ones, list_ref, sems, keys, values, own_sems) = refs[count + 8 :]
    tiles = own_keys.shape[0]
    copies = [
        pltpu.make_async_copy(own_keys, keys.at[pl.ds(0, tiles)], own_sems.at[0]),
        pltpu.make_async_copy(own_values, values.at[pl.ds(0, tiles)], own_sems.at[1]),
    ]
    for copy in copies:
        copy.start()
    project_pieces(pieces, w, keys, values, tiles)
    for copy in copies:
        copy.wait()
    sums = (num, den, num_out, den_out)
    scratch = (ones, list_ref, sems)
    attend_rows(span, True, place_ref, cols_ref, where_ref, local_ref, keys, values, sums, scratch)


def rest_kernel(span, count, place_ref, cols_ref, where_ref, *refs):
    pieces = refs[:count]
    (w, local_ref, num_in, den_in, num_out, den_out) = refs[count : count + 6]
    (num, den, ones, list_ref, sems, keys, values, sums_sems) = refs[count + 6 :]
    incoming = sums_copies(num, den, num_in, den_in, sums_sems, True)
    for copy in incoming:
        copy.start()
    project_pieces(pieces, w, keys, values, 0)
    for copy in incoming:
        copy.wait()
    sums = (num, den, num_out, den_out)
    scratch = (ones, list_ref, sems)
    attend_rows(span, False, place_ref, cols_ref, where_ref, local_ref, keys, values, sums, scratch)


def local_call(kernel, tables, pieces, extra, extra_specs, span, sums, more_outs, scratch, limit, flops):
    own_rows, width = extra[1].shape if kernel is not own_kernel else pieces[0].shape
    shapes = [
        jax.ShapeDtypeStruct((own_rows, width), jnp.float32),
        jax.ShapeDtypeStruct((own_rows, LANES), jnp.float32),
    ]
    arguments = [*tables, *pieces, *extra, *(sums or ())]
    aliases = {}
    if sums:
        aliases = {len(arguments) - 2: 0, len(arguments) - 1: 1}
    bound = functools.partial(kernel, span)
    if kernel is not own_kernel:
        bound = functools.partial(kernel, span, len(pieces))
    return pl.pallas_call(
        bound,
        in_specs=[SMEM] * 3 + [VMEM] * len(pieces) + extra_specs + [HBM] * len(sums or ()),
        out_specs=[HBM, HBM] + [VMEM] * len(more_outs),
        out_shape=shapes + more_outs,
        input_output_aliases=aliases,
        scratch_shapes=[
            pltpu.VMEM((own_rows, width), jnp.float32),
            pltpu.VMEM((own_rows, LANES), jnp.float32),
            pltpu.VMEM((2, TILE, LANES), jnp.bfloat16),
            pltpu.SMEM((tables[1].shape[1] + 1,), jnp.int32),
            pltpu.SemaphoreType.DMA((2,)),
        ]
        + scratch,
        compiler_params=pltpu.CompilerParams(vmem_limit_bytes=limit * MIB),
        cost_estimate=pl.CostEstimate(flops=flops, bytes_accessed=10**5, transcendentals=0),
    )(*arguments)


def key_scratch(tiles, width):
    return [
        pltpu.VMEM((tiles, width, TILE), jnp.bfloat16),
        pltpu.VMEM((tiles, TILE, width), jnp.bfloat16),
        pltpu.SemaphoreType.DMA((2,)),
    ]


def own_attention(tables, rows, w, wq, scales, span):
    width = rows.shape[1]
    tiles = rows.shape[0] // TILE
    shapes = [(tiles, width, TILE), (tiles, TILE, width), rows.shape, rows.shape]
    outs = [jax.ShapeDtypeStruct(shape, jnp.bfloat16) for shape in shapes]
    return local_call(
        own_kernel, tables, [rows], [w, wq, scales], [VMEM] * 3, span, None, outs, [], 24, 10**8
    )


def near_attention(tables, pieces, w, local_q, keys, values, num, den, span):
    tiles = keys.shape[0] + sum(piece.shape[0] // TILE for piece in pieces)
    scratch = key_scratch(tiles, local_q.shape[1])
    extra = [w, local_q, keys, values]
    specs = [VMEM, VMEM, ANY, ANY]
    return local_call(
        near_kernel, tables, pieces, extra, specs, span, (num, den), [], scratch, 24, 10**12
    )


def rest_attention(tables, pieces, w, local_q, num, den, span):
    scratch = key_scratch(sum(piece.shape[0] // TILE for piece in pieces), local_q.shape[1])
    extra = [w, local_q]
    return local_call(
        rest_kernel, tables, pieces, extra, [VMEM] * 2, span, (num, den), [], scratch, 24, 10**8
    )


def expand_kernel(count, last, place_ref, rows_ref, spots_ref, *refs):
    sources = refs[:count]
    (expand_q, num_in, den_in, w) = refs[count : count + 4]
    refs = refs[count + 4 :]
    if last:
        (out_ref, features, keys, values, num, den, row_list, tile_list, sems) = refs
    else:
        (num_out, den_out, features, keys, values, num, den, row_list, tile_list, sems) = refs
    own_rows, width = num_in.shape
    tiles_here = own_rows // TILE
    matchings, edges = rows_ref.shape
    copies = piece_copies(sources, features, sems)
    for copy in copies:
        copy.start()

    def clear(tile, carry):
        target = pl.ds(pl.multiple_of(tile * TILE, TILE), TILE)
        num[target, :] = jnp.zeros((TILE, width), jnp.float32)
        den[target, :] = jnp.zeros((TILE, LANES), jnp.float32)
        return carry

    lax.fori_loop(0, tiles_here + 1, clear, 0)

    def visit(edge, found):
        for matching in range(matchings):
            row = rows_ref[matching, edge] - place_ref[0] * tiles_here
            spot = spots_ref[matching, edge]
            mine = jnp.logical_and(jnp.logical_and(row >= 0, row < tiles_here), spot >= 0)
            row_list[found] = row
            tile_list[found] = spot
            found = found + mine.astype(jnp.int32)
        return found

    found = lax.fori_loop(0, edges, visit, jnp.int32(0))
    for inner in range(GROUP):
        row_list[found + inner] = tiles_here
        tile_list[found + inner] = 0
    for copy in copies:
        copy.wait()

    def group(index, carry):
        first = index * GROUP
        some = jnp.concatenate(
            [
                features[pl.ds(pl.multiple_of(tile_list[first + i] * TILE, TILE), TILE), :]
                for i in range(GROUP)
            ],
            axis=0,
        )
        project(some, w, keys, values, 0)
        units = [(row_list[first + i], i) for i in range(GROUP)]
        attend_units(expand_q, keys, values, num, den, units)
        return carry

    lax.fori_loop(0, (found + GROUP - 1) // GROUP, group, 0)

    def finish(tile, carry):
        target = pl.ds(pl.multiple_of(tile * TILE, TILE), TILE)
        total = num_in[target, :] + num[target, :]
        count = den_in[target, :] + den[target, :]
        if last:
            inverse = spread_denominators(count, width // LANES)
            out_ref[target, :] = (total * inverse).astype(jnp.bfloat16)
        else:
            num_out[target, :] = total
            den_out[target, :] = count
        return carry

    lax.fori_loop(0, tiles_here, finish, 0)


def expand_attention(place, exp_rows, spots, sources, expand_q, num, den, w, last):
    own_rows, width = num.shape
    most = exp_rows.shape[0] * exp_rows.shape[1] + GROUP
    tiles = sum(source.shape[0] for source in sources) // TILE
    sums = [jax.ShapeDtypeStruct(num.shape, num.dtype), jax.ShapeDtypeStruct(den.shape, den.dtype)]
    return pl.pallas_call(
        functools.partial(expand_kernel, len(sources), last),
        in_specs=[SMEM] * 3 + [ANY] * len(sources) + [VMEM] * 4,
        out_specs=VMEM if last else [VMEM, VMEM],
        out_shape=jax.ShapeDtypeStruct((own_rows, width), jnp.bfloat16) if last else sums,
        scratch_shapes=[
            pltpu.VMEM((tiles * TILE, width), jnp.bfloat16),
            pltpu.VMEM((GROUP, width, TILE), jnp.bfloat16),
            pltpu.VMEM((GROUP, TILE, width), jnp.bfloat16),
            pltpu.VMEM((own_rows + TILE, width), jnp.float32),
            pltpu.VMEM((own_rows + TILE, LANES), jnp.float32),
            pltpu.SMEM((most,), jnp.int32),
            pltpu.SMEM((most,), jnp.int32),
            pltpu.SemaphoreType.DMA((len(sources),)),
        ],
        compiler_params=pltpu.CompilerParams(vmem_limit_bytes=36 * MIB),
        cost_estimate=pl.CostEstimate(
            flops=own_rows * width * 256, bytes_accessed=own_rows * width, transcendentals=0
        ),
    )(place, exp_rows, spots, *sources, expand_q, num, den, w)


def cut_kernel(margin, here_ref, features, lower, edge, sems):
    start = pl.multiple_of(here_ref[0] * (features.shape[0] - margin), TILE)
    copies = [
        pltpu.make_async_copy(features.at[pl.ds(0, lower.shape[0])], lower, sems.at[0]),
        pltpu.make_async_copy(features.at[pl.ds(start, margin)], edge, sems.at[1]),
    ]
    for copy in copies:
        copy.start()
    for copy in copies:
        copy.wait()


def cut(here, features, margin):
    rows, width = features.shape
    return pl.pallas_call(
        functools.partial(cut_kernel, margin),
        in_specs=[SMEM, ANY],
        out_specs=[VMEM, VMEM],
        out_shape=[
            jax.ShapeDtypeStruct((rows // 2, width), jnp.bfloat16),
            jax.ShapeDtypeStruct((margin, width), jnp.bfloat16),
        ],
        scratch_shapes=[pltpu.SemaphoreType.DMA((2,))],
        compiler_params=pltpu.CompilerParams(vmem_limit_bytes=8 * MIB),
    )(here, features)


def select_kernel(jobs, share, sources, place_ref, *refs):
    matchings = len(refs) - sources - len(jobs)
    wanted = refs[:matchings]
    parts = refs[matchings : matchings + sources]
    outs = refs[matchings + sources :]
    here = place_ref[0]
    even = lax.rem(place_ref[1], 2) == 0
    quarter = parts[1].shape[0] // TILE
    per_part = 2 * quarter
    flat = []
    for (of_even, of_odd, lines), out in zip(jobs, outs):
        at = 0
        for line in lines:
            start = (here if line == 0 else 1 - here) * share
            for slot in range(share):
                tile = wanted[of_even][0, start + slot]
                if of_odd != of_even:
                    tile = jnp.where(even, tile, wanted[of_odd][0, start + slot])
                flat.append((tile, out, at))
                at += 1
    for tile, out, slot in flat:
        own = tile // per_part == here
        lower = lax.rem(tile // quarter, 2) == 0
        target = slice(slot * TILE, (slot + 1) * TILE)

        @pl.when(own)
        def _():
            start = pl.multiple_of(lax.rem(tile, per_part) * TILE, TILE)
            out[target, :] = parts[0][pl.ds(start, TILE), :]

        start = pl.multiple_of(lax.rem(tile, quarter) * TILE, TILE)

        @pl.when(jnp.logical_and(jnp.logical_not(own), lower))
        def _():
            out[target, :] = parts[1][pl.ds(start, TILE), :]

        if sources > 2:

            @pl.when(jnp.logical_not(jnp.logical_or(own, lower)))
            def _():
                out[target, :] = parts[2][pl.ds(start, TILE), :]


def select(place, jobs, share, wanted, parts):
    width = parts[0].shape[1]
    sizes = [share * len(lines) for _, _, lines in jobs]
    return pl.pallas_call(
        functools.partial(select_kernel, jobs, share, len(parts)),
        in_specs=[SMEM] * (1 + len(wanted)) + [VMEM] * len(parts),
        out_specs=[VMEM] * len(jobs),
        out_shape=[jax.ShapeDtypeStruct((size * TILE, width), jnp.bfloat16) for size in sizes],
        compiler_params=pltpu.CompilerParams(vmem_limit_bytes=16 * MIB),
    )(place, *wanted, *parts)


def distinct_kernel(tiles, lines, place_ref, cols_ref, near_ref, last_ref, *refs):
    wanted_refs = refs[:-2]
    mark, rank_of = refs[-2:]
    matchings, edges = cols_ref.shape
    share = edges // lines
    here = place_ref[0]
    odd = lax.rem(place_ref[1], 2)
    every = range(matchings)

    def clear(tile, carry):
        for matching in every:
            mark[matching, tile] = 0
        return carry

    def count(edge, missing):
        left = []
        for matching in every:
            tile = cols_ref[matching, edge]
            left.append(missing[matching] - (1 - mark[matching, tile]))
            mark[matching, tile] = 1
        return tuple(left)

    def place(at, carry):
        quarter = tiles // 4
        tile = jnp.where(at < quarter, at + quarter, jnp.where(at < 2 * quarter, at - quarter, at))
        ranks, left = [], []
        for matching, (rank, missing) in enumerate(zip(*carry)):
            present = mark[matching, tile]
            added = jnp.where(jnp.logical_and(present == 0, missing > 0), 1, 0)
            wanted_refs[matching][0, rank] = tile
            rank_of[matching, tile] = rank
            ranks.append(rank + present + added)
            left.append(missing - added)
        return tuple(ranks), tuple(left)

    def look_up(edge, carry):
        for matching in every:
            slot = rank_of[matching, cols_ref[matching, edge]]
            away = jnp.where(slot // share == here, 0, 1)
            within = lax.rem(slot, share)
            if matching < matchings - 2:
                near_ref[matching, edge] = (2 * matching + away) * share + within
                last_ref[matching, edge] = -1
            else:
                second = odd if matching == matchings - 1 else 1 - odd
                third = 2 * (matchings - 2)
                near = jnp.where(away == 0, third + second, third + 2)
                later = jnp.logical_and(away == 1, second == 1)
                near_ref[matching, edge] = jnp.where(later, -1, near * share + within)
                last_ref[matching, edge] = jnp.where(later, within, -1)
        return carry

    zero = jnp.int32(0)
    lax.fori_loop(0, tiles, clear, 0)
    missing = lax.fori_loop(0, edges, count, (jnp.int32(edges),) * matchings)
    lax.fori_loop(0, tiles, place, ((zero,) * matchings, missing))
    lax.fori_loop(0, edges, look_up, 0)


def distinct_slots(place, cols, tiles, lines):
    matchings, edges = cols.shape
    wanted = jax.ShapeDtypeStruct((1, 2 * edges), jnp.int32)
    spots = jax.ShapeDtypeStruct(cols.shape, jnp.int32)
    near, last, *wanted = pl.pallas_call(
        functools.partial(distinct_kernel, tiles, lines),
        in_specs=[SMEM, SMEM],
        out_specs=[SMEM] * (2 + matchings),
        out_shape=[spots, spots] + [wanted] * matchings,
        scratch_shapes=[pltpu.SMEM((matchings, tiles), jnp.int32)] * 2,
        cost_estimate=pl.CostEstimate(flops=10**11, bytes_accessed=4096, transcendentals=0),
    )(place, cols)
    return near, last, wanted


def local(features, w_query, w_key_value, edge_local, edge_expand, local_cols, exp_rows, exp_cols):
    groups = lax.axis_size("head")
    blocks = lax.axis_size("node")
    own_rows, width = features.shape
    here = lax.axis_index("head")
    block = lax.axis_index("node")
    edges = exp_cols.shape[2]
    tiles = local_cols.shape[0]
    own_tiles = own_rows // TILE
    margin = HT * TILE
    exp_rows, exp_cols = exp_rows[0], exp_cols[0]
    log_count = blocks.bit_length() - 1
    flips = [1 << matching * log_count // MATCH for matching in range(MATCH)]

    def swap(x, matching, of_odd=None):
        flip = [flips[matching], flips[matching if of_odd is None else of_odd]]
        return lax.ppermute(x, "node", [(i, i ^ flip[i % 2]) for i in range(blocks)])

    def other(x):
        return lax.ppermute(x, "head", [(0, 1), (1, 0)])

    scales = jnp.stack([edge_local, edge_expand])
    two = groups == 2 and min(flips[2:]) > 1
    if two:
        lower, edge_rows = cut(jnp.reshape(here, (1,)).astype(jnp.int32), features, margin)
        beside = other(scales)
        lower, edge_rows, exp_cols, beside, w_query, w_key_value, block, here = (
            lax.optimization_barrier(
                (lower, edge_rows, exp_cols, beside, w_query, w_key_value, block, here)
            )
        )
    place = jnp.stack([here, block]).astype(jnp.int32)
    column = jnp.arange(tiles + 2 * HT, dtype=jnp.int32) - HT
    usable = block * tiles + column
    usable = jnp.logical_and(usable >= 0, usable < blocks * tiles)
    own = column // own_tiles == here
    own_place = column - here * own_tiles
    split = own_tiles // 2

    if two:
        half = own_rows // 2
        quarter = own_tiles // 2
        lower_here = column // quarter % 2 == 0
        inside = jnp.logical_and(column >= 0, column < tiles)
        after = column >= tiles
        in_halo = jnp.where(after, column - tiles, column + HT)
        in_halo += jnp.where(after == (here == 0), 2 * quarter + HT, 2 * quarter)
        place_in = jnp.where(lower_here, column % quarter, quarter + column % quarter)
        rest = jnp.where(inside, place_in, in_halo)
        near = jnp.where(own, own_place, own_tiles + place_in)
        near = jnp.where(jnp.logical_and(inside, jnp.logical_or(own, lower_here)), near, -1)
        rest_low = jnp.where(jnp.logical_and(usable, jnp.logical_not(own)), rest, -1)
        rest_high = jnp.where(jnp.logical_and(usable, near < 0), rest, -1)
        where_own = jnp.where(own, own_place, -1)
        tables = jnp.stack([where_own, where_own, near, near, rest_low, rest_high])
        w = jnp.transpose(w_key_value, (1, 0, 2))
        lower = other(lower)
        near_spots, last_spots, wanted = distinct_slots(place, exp_cols, tiles, groups)
        edge_rows, *wanted = lax.optimization_barrier((edge_rows, *wanted))
        route = [(2 * i, 2 * i - 2) for i in range(1, blocks)]
        route += [(2 * i + 1, 2 * i + 3) for i in range(blocks - 1)]
        halo = lax.ppermute(edge_rows, ("node", "head"), route)
        wanted = [swap(wanted[m], m) for m in range(MATCH)]
        upper = jnp.concatenate([features[half:], halo], axis=0)
        scales = jnp.where(
            here == 0,
            jnp.concatenate([scales, beside], axis=1),
            jnp.concatenate([beside, scales], axis=1),
        )
        num, den, keys, values, local_q, expand_q = own_attention(
            (place, local_cols, tables[:2]), features, w, w_query, scales, (0, split)
        )
        where_near, where_rest = tables[2:4], tables[4:]
        lower, upper, num, den, where_near, where_rest = lax.optimization_barrier(
            (lower, upper, num, den, where_near, where_rest)
        )
        upper = other(upper)
        share = edges // groups
        sources = [features, lower]
        chosen = select(place, ((3, 2, (0,)), (2, 3, (0,)), (1, 1, (0,))), share, wanted, sources)
        where_near, *chosen = lax.optimization_barrier((where_near, *chosen))
        first = swap(chosen[0], 3, 2)
        second = swap(chosen[1], 2, 3)
        early = swap(chosen[2], 1)
        num, den = near_attention(
            (place, local_cols, where_near),
            [lower],
            w,
            local_q,
            keys,
            values,
            num,
            den,
            (split, own_tiles),
        )
        upper, num, den = lax.optimization_barrier((upper, num, den))
        sources = [features, lower, upper]
        chosen = select(place, ((1, 1, (1,)), (0, 0, (0, 1))), share, wanted, sources)
        where_rest, first, early, *chosen = lax.optimization_barrier(
            (where_rest, first, early, *chosen)
        )
        first_beside = other(first)
        late = swap(chosen[0], 1)
        pair = swap(chosen[1], 0)
        num, den = rest_attention(
            (place, local_cols, where_rest),
            [lower, upper, halo],
            w,
            local_q,
            num,
            den,
            (0, own_tiles),
        )
        second, num, den = lax.optimization_barrier((second, num, den))
        last_sources = [other(second)]
        near_sources = [pair, early, late, first, second, first_beside]
    else:
        w = jnp.transpose(w_key_value, (1, 0, 2))
        gather = lambda x: lax.all_gather(x, "head", axis=0, tiled=True)
        scales = lax.all_gather(scales, "head", axis=1, tiled=True)
        full = gather(features)
        before = lax.ppermute(full[-margin:], "node", [(i, i + 1) for i in range(blocks - 1)])
        after = lax.ppermute(full[:margin], "node", [(i + 1, i) for i in range(blocks - 1)])
        received = [gather(swap(features, m)) for m in range(MATCH)]
        near_sources, last_sources = received[:2], received[2:]
        matching = jnp.arange(MATCH, dtype=jnp.int32)[:, None]
        near_spots = jnp.where(matching < 2, matching * tiles + exp_cols, -1)
        last_spots = jnp.where(matching < 2, -1, (matching - 2) * tiles + exp_cols)
        where_own = jnp.where(own, own_place, -1)
        where_own = jnp.stack([where_own, where_own])
        where_rest = jnp.where(jnp.logical_and(usable, jnp.logical_not(own)), column + HT, -1)
        where_rest = jnp.stack([where_rest, where_rest])
        num, den, keys, values, local_q, expand_q = own_attention(
            (place, local_cols, where_own), features, w, w_query, scales, (0, own_tiles)
        )
        num, den = rest_attention(
            (place, local_cols, where_rest),
            [before, full, after],
            w,
            local_q,
            num,
            den,
            (0, own_tiles),
        )
    num, den = expand_attention(
        place, exp_rows, near_spots, near_sources, expand_q, num, den, w, False
    )
    return expand_attention(
        place, exp_rows, last_spots, last_sources, expand_q, num, den, w, True
    )


def solution(mesh):
    return jax.shard_map(
        local,
        mesh=mesh,
        in_specs=(
            P(("node", "head"), None),
            P(),
            P(),
            P("head"),
            P("head"),
            P("node", None),
            P("node", None, None),
            P("node", None, None),
        ),
        out_specs=P(("node", "head"), None),
        check_vma=False,
    )
```

```python
import functools
import math

import jax
import jax.numpy as jnp
from jax import lax
from jax.experimental import pallas as pl
from jax.experimental.pallas import tpu as pltpu
from jax.sharding import PartitionSpec as P

HEADS = 8
TILE = 128
HT = 2
MATCH = 4
LANES = 128
GROUP = 4
MIB = 1024 * 1024

ANY = pl.BlockSpec(memory_space=pl.ANY)
SMEM = pl.BlockSpec(memory_space=pltpu.SMEM)
VMEM = pl.BlockSpec(memory_space=pltpu.VMEM)
HBM = pl.BlockSpec(memory_space=pltpu.HBM)


def piece_copies(pieces, target, sems):
    copies = []
    start = 0
    for index, piece in enumerate(pieces):
        size = piece.shape[0] // TILE * TILE
        copies.append(
            pltpu.make_async_copy(
                piece.at[pl.ds(0, size)], target.at[pl.ds(start, size)], sems.at[index]
            )
        )
        start += size
    return copies


def lane_masks():
    lane = lax.broadcasted_iota(jnp.int32, (TILE, LANES), 1)
    return lane < LANES // 2, lane % (LANES // 2)


def pack_denominators(pieces):
    _, within = lane_masks()
    size = LANES // 2 // len(pieces)
    packed = pieces[-1]
    for pair in range(len(pieces) - 2, -1, -1):
        packed = jnp.where(within < (pair + 1) * size, pieces[pair], packed)
    return packed


def spread_denominators(packed, pairs):
    size = LANES // 2 // pairs
    inverse = 1.0 / packed
    coarse = inverse.astype(jnp.bfloat16)
    fine = (inverse - coarse.astype(jnp.float32)).astype(jnp.bfloat16)
    shape = (2 * LANES, pairs * LANES)
    source = lax.broadcasted_iota(jnp.int32, shape, 0) % LANES
    target = lax.broadcasted_iota(jnp.int32, shape, 1)
    wanted = target // LANES * size + (target % LANES) // (LANES // 2) * (LANES // 2)
    chooser = jnp.where(source == wanted, 1.0, 0.0).astype(jnp.bfloat16)
    return jnp.dot(
        jnp.concatenate([coarse, fine], axis=1), chooser, preferred_element_type=jnp.float32
    )


def project(rows, w, keys, values, first):
    new_keys = jnp.dot(rows, w[0], preferred_element_type=jnp.float32).astype(jnp.bfloat16).T
    new_values = jnp.dot(rows, w[1], preferred_element_type=jnp.float32).astype(jnp.bfloat16)
    for index in range(rows.shape[0] // TILE):
        span = slice(index * TILE, (index + 1) * TILE)
        keys[first + index] = new_keys[:, span]
        values[first + index] = new_values[span, :]


def attend_row(queries, keys, values, ones, tiles):
    low, _ = lane_masks()
    low_mask = jnp.where(low, 1.0, 0.0).astype(jnp.bfloat16)
    high_mask = jnp.where(low, 0.0, 1.0).astype(jnp.bfloat16)
    results = []
    for pair in range(queries.shape[1] // LANES):
        part = slice(pair * LANES, (pair + 1) * LANES)
        both = jnp.concatenate([queries[:, part] * low_mask, queries[:, part] * high_mask], axis=0)
        weights = []
        for start in range(0, len(tiles), 2):
            slab = jnp.concatenate([keys[tile, part, :] for tile in tiles[start : start + 2]], axis=1)
            scores = jnp.dot(both, slab, preferred_element_type=jnp.float32)
            weights.append(jnp.exp(jnp.clip(scores, -5.0, 5.0)).astype(jnp.bfloat16))
        weights = jnp.concatenate(weights, axis=1)
        wide = jnp.concatenate(
            [
                jnp.concatenate([values[tile, :, part], ones[0]], axis=1) for tile in tiles[:-1]
            ]
            + [jnp.concatenate([values[tiles[-1], :, part] * ones[1], ones[1]], axis=1)],
            axis=0,
        )
        sums = jnp.dot(weights, wide, preferred_element_type=jnp.float32)
        results.append(
            (
                jnp.where(low, sums[:TILE, :LANES], sums[TILE:, :LANES]),
                jnp.where(low, sums[:TILE, LANES:], sums[TILE:, LANES:]),
            )
        )
    return results


def attend_units(queries, keys, values, num, den, units):
    low_lanes, _ = lane_masks()
    low = jnp.where(low_lanes, 1.0, 0.0).astype(jnp.bfloat16)
    high = jnp.where(low_lanes, 0.0, 1.0).astype(jnp.bfloat16)
    nothing = jnp.zeros((LANES // 2, TILE), jnp.bfloat16)
    rows = [pl.ds(pl.multiple_of(row * TILE, TILE), TILE) for row, _ in units]
    last = queries.shape[0] // TILE - 1
    query_rows = [
        pl.ds(pl.multiple_of(jnp.minimum(row, last) * TILE, TILE), TILE) for row, _ in units
    ]
    denominators = [[] for _ in units]
    for pair in range(queries.shape[1] // LANES):
        part = slice(pair * LANES, (pair + 1) * LANES)
        middle = pair * LANES + LANES // 2
        weights = []
        for row, (_, tile) in zip(query_rows, units):
            first = jnp.concatenate([keys[tile, pair * LANES : middle, :], nothing], axis=0)
            second = jnp.concatenate([nothing, keys[tile, middle : (pair + 1) * LANES, :]], axis=0)
            scores = jnp.dot(
                queries[row, part],
                jnp.concatenate([first, second], axis=1),
                preferred_element_type=jnp.float32,
            )
            weights.append(jnp.exp(jnp.clip(scores, -5.0, 5.0)).astype(jnp.bfloat16))
        sums = []
        for weight, (_, tile) in zip(weights, units):
            value = values[tile, :, part]
            wide = jnp.concatenate(
                [
                    jnp.concatenate([value * low, low], axis=1),
                    jnp.concatenate([value * high, high], axis=1),
                ],
                axis=0,
            )
            sums.append(jnp.dot(weight, wide, preferred_element_type=jnp.float32))
        for row, both, listed in zip(rows, sums, denominators):
            num[row, part] += both[:, :LANES]
            listed.append(both[:, LANES:])
    for row, listed in zip(rows, denominators):
        den[row, :] += pack_denominators(listed)


def project_pieces(pieces, w, keys, values, at):
    for piece in pieces:
        tiles = piece.shape[0] // TILE
        size = math.gcd(tiles, GROUP)

        def some_tiles(index, carry, piece=piece, at=at, size=size):
            some = piece[pl.ds(pl.multiple_of(index * size * TILE, TILE), size * TILE), :]
            project(some, w, keys, values, at + index * size)
            return carry

        lax.fori_loop(0, tiles // size, some_tiles, 0)
        at += tiles


def attend_rows(fresh, place_ref, cols_ref, where_ref, local_ref, keys, values, sums, scratch):
    num, den, num_out, den_out = sums
    ones, list_ref, sems = scratch
    width = num.shape[1]
    tiles_here = local_ref.shape[0] // TILE
    slots = cols_ref.shape[1]
    ones[0] = jnp.ones(ones.shape[1:], ones.dtype)
    ones[1] = jnp.zeros(ones.shape[1:], ones.dtype)

    def one_row(row, carry):
        target = pl.ds(pl.multiple_of(row * TILE, TILE), TILE)
        found = jnp.int32(0)
        for slot in range(slots):
            tile = where_ref[cols_ref[place_ref[0] * tiles_here + row, slot]]
            list_ref[found] = tile
            found = found + (tile >= 0).astype(jnp.int32)
        list_ref[found] = 0
        odd = lax.rem(found, 2)
        if fresh:

            @pl.when(found == 0)
            def _():
                num[target, :] = jnp.zeros((TILE, width), jnp.float32)
                den[target, :] = jnp.zeros((TILE, LANES), jnp.float32)

        for chunks in range(1, slots // 2 + 1):

            @pl.when((found + 1) // 2 == chunks)
            def _():
                tiles = [list_ref[index] for index in range(2 * chunks)]
                units = (ones[0], ones[odd])
                results = attend_row(local_ref[target, :], keys, values, units, tiles)
                packed = pack_denominators([denominator for _, denominator in results])
                for pair, (numerator, _) in enumerate(results):
                    part = slice(pair * LANES, (pair + 1) * LANES)
                    num[target, part] = numerator if fresh else num[target, part] + numerator
                den[target, :] = packed if fresh else den[target, :] + packed

        for index, (here, there) in enumerate([(num, num_out), (den, den_out)]):
            pltpu.make_async_copy(here.at[target], there.at[target], sems.at[index]).start()
        return carry

    lax.fori_loop(0, tiles_here, one_row, 0)
    for index, (here, there) in enumerate([(num, num_out), (den, den_out)]):
        pltpu.make_async_copy(here, there, sems.at[index]).wait()


def own_kernel(rows, w, wq, scales, keys, values, local_ref, expand_ref):
    width = rows.shape[1]
    tiles = rows.shape[0] // TILE
    size = min(GROUP, tiles)
    project_pieces([rows], w, keys, values, 0)

    def some_queries(index, carry):
        target = pl.ds(pl.multiple_of(index * size * TILE, TILE), size * TILE)
        queries = jnp.dot(rows[target, :], wq[...], preferred_element_type=jnp.float32)
        queries = queries.astype(jnp.bfloat16).astype(jnp.float32)
        scale = 1.0 / math.sqrt(width // HEADS)
        local_ref[target, :] = (queries * scales[0:1, :] * scale).astype(jnp.bfloat16)
        expand_ref[target, :] = (queries * scales[1:2, :] * scale).astype(jnp.bfloat16)
        return carry

    lax.fori_loop(0, tiles // size, some_queries, 0)


def project_own(rows, w, wq, scales):
    width = rows.shape[1]
    tiles = rows.shape[0] // TILE
    shapes = [(tiles, width, TILE), (tiles, TILE, width), rows.shape, rows.shape]
    return pl.pallas_call(
        own_kernel,
        in_specs=[VMEM] * 4,
        out_specs=[VMEM] * 4,
        out_shape=[jax.ShapeDtypeStruct(shape, jnp.bfloat16) for shape in shapes],
        compiler_params=pltpu.CompilerParams(vmem_limit_bytes=24 * MIB),
        cost_estimate=pl.CostEstimate(flops=10**8, bytes_accessed=10**5, transcendentals=0),
    )(rows, w, wq, scales)


def local_kernel(count, begins, place_ref, cols_ref, where_ref, *refs):
    pieces = refs[:count]
    (w, local_ref, before, after, num_out, den_out) = refs[count : count + 6]
    (num, den, ones, list_ref, sems, keys, values, more_sems) = refs[count + 6 :]
    tiles = 0
    if begins:
        tiles = before.shape[0]
        copies = [
            pltpu.make_async_copy(before, keys.at[pl.ds(0, tiles)], more_sems.at[0]),
            pltpu.make_async_copy(after, values.at[pl.ds(0, tiles)], more_sems.at[1]),
        ]
    else:
        copies = [
            pltpu.make_async_copy(before, num, more_sems.at[0]),
            pltpu.make_async_copy(after, den, more_sems.at[1]),
        ]
    for copy in copies:
        copy.start()
    project_pieces(pieces, w, keys, values, tiles)
    for copy in copies:
        copy.wait()
    sums = (num, den, num_out, den_out)
    scratch = (ones, list_ref, sems)
    attend_rows(begins, place_ref, cols_ref, where_ref, local_ref, keys, values, sums, scratch)


def local_attention(tables, pieces, w, local_q, before, begins):
    own_rows, width = local_q.shape
    shapes = [
        jax.ShapeDtypeStruct((own_rows, width), jnp.float32),
        jax.ShapeDtypeStruct((own_rows, LANES), jnp.float32),
    ]
    arguments = [*tables, *pieces, w, local_q, *before]
    aliases = {} if begins else {len(arguments) - 2: 0, len(arguments) - 1: 1}
    tiles = sum(piece.shape[0] // TILE for piece in pieces)
    tiles += own_rows // TILE if begins else 0
    return pl.pallas_call(
        functools.partial(local_kernel, len(pieces), begins),
        in_specs=[SMEM] * 3 + [VMEM] * (len(pieces) + 2) + [HBM] * 2,
        out_specs=[HBM, HBM],
        out_shape=shapes,
        input_output_aliases=aliases,
        scratch_shapes=[
            pltpu.VMEM((own_rows, width), jnp.float32),
            pltpu.VMEM((own_rows, LANES), jnp.float32),
            pltpu.VMEM((2, TILE, LANES), jnp.bfloat16),
            pltpu.SMEM((tables[1].shape[1] + 1,), jnp.int32),
            pltpu.SemaphoreType.DMA((2,)),
            pltpu.VMEM((tiles, width, TILE), jnp.bfloat16),
            pltpu.VMEM((tiles, TILE, width), jnp.bfloat16),
            pltpu.SemaphoreType.DMA((2,)),
        ],
        compiler_params=pltpu.CompilerParams(vmem_limit_bytes=24 * MIB),
        cost_estimate=pl.CostEstimate(
            flops=10**12 if begins else 10**8, bytes_accessed=10**5, transcendentals=0
        ),
    )(*arguments)


def expand_kernel(count, last, place_ref, rows_ref, spots_ref, *refs):
    sources = refs[:count]
    (expand_q, num_in, den_in, w) = refs[count : count + 4]
    refs = refs[count + 4 :]
    if last:
        (_, out_ref, features, keys, values, num, den, row_list, tile_list, mark, sems) = refs[:-2]
        (results, result_sems) = refs[-2:]
    else:
        (num, den, out_ref, features, keys, values, row_list, tile_list, mark, sems) = refs
    own_rows, width = expand_q.shape
    tiles_here = own_rows // TILE
    matchings, edges = rows_ref.shape
    copies = piece_copies(sources, features, sems)
    for copy in copies:
        copy.start()
    for tile in range(tiles_here):
        mark[tile] = 0 if last else 1

    def visit(edge, found):
        for matching in range(matchings):
            row = rows_ref[matching, edge] - place_ref[0] * tiles_here
            spot = spots_ref[matching, edge]
            mine = jnp.logical_and(jnp.logical_and(row >= 0, row < tiles_here), spot >= 0)
            row_list[found] = row
            tile_list[found] = spot
            found = found + mine.astype(jnp.int32)
            if last:

                @pl.when(mine)
                def _():
                    mark[row] = 1

        return found

    found = lax.fori_loop(0, edges, visit, jnp.int32(0))
    for inner in range(GROUP):
        row_list[found + inner] = tiles_here
        tile_list[found + inner] = 0

    def each_marked(action):
        def visit_tile(tile, carry):
            target = pl.ds(pl.multiple_of(tile * TILE, TILE), TILE)
            pl.when(mark[tile] == 1)(lambda: action(tile, target))
            return carry

        lax.fori_loop(0, tiles_here, visit_tile, 0)

    def begin(tile, target):
        num[target, :] = num_in[target, :]
        den[target, :] = den_in[target, :]

    each_marked(begin)
    spare = pl.ds(own_rows, TILE)
    num[spare, :] = jnp.zeros((TILE, width), jnp.float32)
    den[spare, :] = jnp.zeros((TILE, LANES), jnp.float32)
    for copy in copies:
        copy.wait()

    def group(index, carry):
        first = index * GROUP
        some = jnp.concatenate(
            [
                features[pl.ds(pl.multiple_of(tile_list[first + i] * TILE, TILE), TILE), :]
                for i in range(GROUP)
            ],
            axis=0,
        )
        project(some, w, keys, values, 0)
        units = [(row_list[first + i], i) for i in range(GROUP)]
        attend_units(expand_q, keys, values, num, den, units)
        return carry

    lax.fori_loop(0, (found + GROUP - 1) // GROUP, group, 0)

    def finish(tile, target):
        inverse = spread_denominators(den[target, :], width // LANES)
        result = (num[target, :] * inverse).astype(jnp.bfloat16)
        if last:
            results[target, :] = result
            copy_out(tile, target).start()
        else:
            out_ref[target, :] = result

    def copy_out(tile, target):
        return pltpu.make_async_copy(results.at[target], out_ref.at[target], result_sems.at[tile])

    each_marked(finish)
    if last:
        each_marked(lambda tile, target: copy_out(tile, target).wait())


def expand_attention(place, exp_rows, spots, sources, expand_q, num, den, w, out):
    width = w.shape[2]
    own_rows = expand_q.shape[0]
    last = out is not None
    most = exp_rows.shape[0] * exp_rows.shape[1] + GROUP
    tiles = sum(source.shape[0] // TILE for source in sources)
    sums = [
        jax.ShapeDtypeStruct((own_rows + TILE, width), jnp.float32),
        jax.ShapeDtypeStruct((own_rows + TILE, LANES), jnp.float32),
    ]
    result = jax.ShapeDtypeStruct((own_rows, width), jnp.bfloat16)
    sums_scratch = [pltpu.VMEM(array.shape, array.dtype) for array in sums]
    arguments = [place, exp_rows, spots, *sources, expand_q, num, den, w]
    return pl.pallas_call(
        functools.partial(expand_kernel, len(sources), last),
        in_specs=[SMEM] * 3 + [ANY] * len(sources) + [VMEM] * 4 + [ANY] * last,
        out_specs=ANY if last else [VMEM] * 3,
        out_shape=result if last else sums + [result],
        input_output_aliases={len(arguments): 0} if last else {},
        scratch_shapes=[
            pltpu.VMEM((tiles * TILE, width), jnp.bfloat16),
            pltpu.VMEM((GROUP, width, TILE), jnp.bfloat16),
            pltpu.VMEM((GROUP, TILE, width), jnp.bfloat16),
        ]
        + (sums_scratch if last else [])
        + [
            pltpu.SMEM((most,), jnp.int32),
            pltpu.SMEM((most,), jnp.int32),
            pltpu.SMEM((own_rows // TILE,), jnp.int32),
            pltpu.SemaphoreType.DMA((len(sources),)),
        ]
        + (
            [
                pltpu.VMEM((own_rows, width), jnp.bfloat16),
                pltpu.SemaphoreType.DMA((own_rows // TILE,)),
            ]
            if last
            else []
        ),
        compiler_params=pltpu.CompilerParams(vmem_limit_bytes=24 * MIB),
        cost_estimate=pl.CostEstimate(
            flops=own_rows * width * 256, bytes_accessed=own_rows * width, transcendentals=0
        ),
    )(*arguments, *([out] if last else []))


def cut_kernel(here_ref, features, first, second, edge, sems):
    here = here_ref[0]
    half, margin = first.shape[0], edge.shape[0]
    copies = []
    for index, (start, target) in enumerate(
        [(here * half, first), ((1 - here) * half, second), (here * (2 * half - margin), edge)]
    ):
        rows = pl.ds(pl.multiple_of(start, TILE), target.shape[0])
        copies.append(pltpu.make_async_copy(features.at[rows], target, sems.at[index]))
    for copy in copies:
        copy.start()
    for copy in copies:
        copy.wait()


def cut(here, features, margin):
    rows, width = features.shape
    shapes = [(rows // 2, width), (rows // 2, width), (margin, width)]
    return pl.pallas_call(
        cut_kernel,
        in_specs=[SMEM, ANY],
        out_specs=[VMEM] * 3,
        out_shape=[jax.ShapeDtypeStruct(shape, jnp.bfloat16) for shape in shapes],
        scratch_shapes=[pltpu.SemaphoreType.DMA((3,))],
        compiler_params=pltpu.CompilerParams(vmem_limit_bytes=8 * MIB),
    )(here, features)


def select_kernel(jobs, share, sources, margin, place_ref, *refs):
    matchings = len(refs) - sources - len(jobs) - (margin > 0)
    wanted = refs[:matchings]
    parts = refs[matchings : matchings + sources]
    outs = refs[matchings + sources :]
    here = place_ref[0]
    even = lax.rem(place_ref[1], 2) == 0
    quarter = parts[1].shape[0] // TILE
    if margin:
        start = pl.multiple_of((1 - here) * (quarter * TILE - margin), TILE)
        outs[-1][...] = parts[1][pl.ds(start, margin), :]
    per_part = 2 * quarter
    flat = []
    for (of_even, of_odd, lines, _), out in zip(jobs, outs):
        at = 0
        for line in lines:
            start = (here if line == 0 else 1 - here) * share
            for slot in range(share):
                tile = wanted[of_even][0, start + slot]
                if of_odd != of_even:
                    tile = jnp.where(even, tile, wanted[of_odd][0, start + slot])
                flat.append((tile, out, at))
                at += 1
    for tile, out, slot in flat:
        own = tile // per_part == here
        place = tile // quarter
        end = jnp.logical_or(place == 0, place == 3)
        target = slice(slot * TILE, (slot + 1) * TILE)

        @pl.when(own)
        def _():
            start = pl.multiple_of(lax.rem(tile, per_part) * TILE, TILE)
            out[target, :] = parts[0][pl.ds(start, TILE), :]

        start = pl.multiple_of(lax.rem(tile, quarter) * TILE, TILE)

        @pl.when(jnp.logical_and(jnp.logical_not(own), end))
        def _():
            out[target, :] = parts[1][pl.ds(start, TILE), :]

        if sources > 2:

            @pl.when(jnp.logical_not(jnp.logical_or(own, end)))
            def _():
                out[target, :] = parts[2][pl.ds(start, TILE), :]


def select(place, jobs, share, wanted, parts, margin=0):
    width = parts[0].shape[1]
    sizes = [share * len(lines) * TILE + more for _, _, lines, more in jobs]
    sizes += [margin] * (margin > 0)
    return pl.pallas_call(
        functools.partial(select_kernel, jobs, share, len(parts), margin),
        in_specs=[SMEM] * (1 + len(wanted)) + [VMEM] * len(parts),
        out_specs=[VMEM] * len(sizes),
        out_shape=[jax.ShapeDtypeStruct((size, width), jnp.bfloat16) for size in sizes],
        compiler_params=pltpu.CompilerParams(vmem_limit_bytes=16 * MIB),
        cost_estimate=pl.CostEstimate(flops=1000, bytes_accessed=1000, transcendentals=0),
    )(place, *wanted, *parts)


def distinct_kernel(tiles, lines, place_ref, cols_ref, near_ref, last_ref, *refs):
    wanted_refs = refs[:-2]
    mark, rank_of = refs[-2:]
    matchings, edges = cols_ref.shape
    share = edges // lines
    here = place_ref[0]
    odd = lax.rem(place_ref[1], 2)
    every = range(matchings)

    def clear(tile, carry):
        for matching in every:
            mark[matching, tile] = 0
        return carry

    def count(edge, missing):
        left = []
        for matching in every:
            tile = cols_ref[matching, edge]
            left.append(missing[matching] - (1 - mark[matching, tile]))
            mark[matching, tile] = 1
        return tuple(left)

    def place(at, carry):
        quarter = tiles // 4
        tile = at + (quarter if at // quarter % 2 == 0 else -quarter)
        ranks, left = [], []
        for matching, (rank, missing) in enumerate(zip(*carry)):
            present = mark[matching, tile]
            added = jnp.where(jnp.logical_and(present == 0, missing > 0), 1, 0)
            wanted_refs[matching][0, rank] = tile
            rank_of[matching, tile] = rank
            ranks.append(rank + present + added)
            left.append(missing - added)
        return tuple(ranks), tuple(left)

    def look_up(edge, carry):
        for matching in every:
            slot = rank_of[matching, cols_ref[matching, edge]]
            away = jnp.where(slot // share == here, 0, 1)
            within = lax.rem(slot, share)
            if matching < matchings - 2:
                near_ref[matching, edge] = (2 * matching + away) * share + within
                last_ref[matching, edge] = -1
            else:
                second = odd if matching == matchings - 1 else 1 - odd
                third = 2 * (matchings - 2)
                near = jnp.where(away == 0, third + second, third + 2)
                later = jnp.logical_and(away == 1, second == 1)
                near_ref[matching, edge] = jnp.where(later, -1, near * share + within)
                last_ref[matching, edge] = jnp.where(later, within, -1)
        return carry

    for tile in range(tiles):
        clear(tile, 0)
    missing = (jnp.int32(edges),) * matchings
    for edge in range(edges):
        missing = count(edge, missing)
    carry = ((jnp.int32(0),) * matchings, missing)
    for at in range(tiles):
        carry = place(at, carry)
    for edge in range(edges):
        look_up(edge, 0)


def distinct_slots(place, cols, tiles, lines):
    matchings, edges = cols.shape
    wanted = jax.ShapeDtypeStruct((1, 2 * edges), jnp.int32)
    spots = jax.ShapeDtypeStruct(cols.shape, jnp.int32)
    near, last, *wanted = pl.pallas_call(
        functools.partial(distinct_kernel, tiles, lines),
        in_specs=[SMEM, SMEM],
        out_specs=[SMEM] * (2 + matchings),
        out_shape=[spots, spots] + [wanted] * matchings,
        scratch_shapes=[pltpu.SMEM((matchings, tiles), jnp.int32)] * 2,
        cost_estimate=pl.CostEstimate(flops=10**11, bytes_accessed=4096, transcendentals=0),
    )(place, cols)
    return near, last, wanted


def local(features, w_query, w_key_value, edge_local, edge_expand, local_cols, exp_rows, exp_cols):
    groups = lax.axis_size("head")
    blocks = lax.axis_size("node")
    own_rows, width = features.shape
    here = lax.axis_index("head")
    block = lax.axis_index("node")
    edges = exp_cols.shape[2]
    tiles = local_cols.shape[0]
    own_tiles = own_rows // TILE
    margin = HT * TILE
    exp_rows, exp_cols = exp_rows[0], exp_cols[0]
    log_count = blocks.bit_length() - 1
    flips = [1 << matching * log_count // MATCH for matching in range(MATCH)]

    def swap(x, matching, of_odd=None):
        flip = [flips[matching], flips[matching if of_odd is None else of_odd]]
        return lax.ppermute(x, "node", [(i, i ^ flip[i % 2]) for i in range(blocks)])

    def other(x):
        return lax.ppermute(x, "head", [(0, 1), (1, 0)])

    scales = jnp.stack([edge_local, edge_expand])
    two = groups == 2 and min(flips[2:]) > 1
    if two:
        cuts = cut(jnp.reshape(here, (1,)).astype(jnp.int32), features, margin)
        beside = other(scales)
        *cuts, exp_cols, beside, w_query, w_key_value, block, here = lax.optimization_barrier(
            (*cuts, exp_cols, beside, w_query, w_key_value, block, here)
        )
    place = jnp.stack([here, block]).astype(jnp.int32)
    column = jnp.arange(tiles + 2 * HT, dtype=jnp.int32) - HT
    usable = block * tiles + column
    usable = jnp.logical_and(usable >= 0, usable < blocks * tiles)
    own = column // own_tiles == here
    own_place = column - here * own_tiles

    if two:
        quarter = own_tiles // 2
        end = jnp.logical_or(column // quarter == 0, column // quarter == 3)
        inside = jnp.logical_and(column >= 0, column < tiles)
        after = column >= tiles
        in_halo = jnp.where(after, column - tiles, column + HT)
        in_halo += jnp.where(after == (here == 0), 2 * quarter, 2 * quarter + HT)
        place_in = jnp.where(end, column % quarter, quarter + column % quarter)
        rest = jnp.where(inside, place_in, in_halo)
        near = jnp.where(own, own_place, own_tiles + place_in)
        near = jnp.where(jnp.logical_and(inside, jnp.logical_or(own, end)), near, -1)
        rest = jnp.where(jnp.logical_and(usable, near < 0), rest, -1)
        w = jnp.transpose(w_key_value, (1, 0, 2))
        first_half, second_half, edge_rows = cuts
        first_half = other(first_half)
        near_spots, last_spots, wanted = distinct_slots(place, exp_cols, tiles, groups)
        edge_rows, *wanted = lax.optimization_barrier((edge_rows, *wanted))
        wanted = [swap(wanted[m], m) for m in range(MATCH)]
        inward = [(2 * i, 2 * i - 2) for i in range(1, blocks)]
        inward += [(2 * i + 1, 2 * i + 3) for i in range(blocks - 1)]
        halo = lax.ppermute(edge_rows, ("node", "head"), inward)
        scales = jnp.where(
            here == 0,
            jnp.concatenate([scales, beside], axis=1),
            jnp.concatenate([beside, scales], axis=1),
        )
        scales, halo, w, *wanted = lax.optimization_barrier((scales, halo, w, *wanted))
        keys, values, local_q, expand_q = project_own(features, w, w_query, scales)
        first_half, second_half, keys, near, rest = lax.optimization_barrier(
            (first_half, second_half, keys, near, rest)
        )
        second_half = other(second_half)
        share = edges // groups
        sources = [features, first_half]
        jobs = ((3, 2, (0,), 0), (2, 3, (0,), 16), (1, 1, (0,), 0), (0, 0, (0,), 0))
        *chosen, edge_rows = select(place, jobs, share, wanted, sources, margin)
        near, edge_rows, *chosen = lax.optimization_barrier((near, edge_rows, *chosen))
        outward = [(2 * i, 2 * i + 2) for i in range(blocks - 1)]
        outward += [(2 * i + 1, 2 * i - 1) for i in range(1, blocks)]
        other_halo = lax.ppermute(edge_rows, ("node", "head"), outward)
        first = swap(chosen[0], 3, 2)
        second = swap(chosen[1], 2, 3)
        early = swap(chosen[2], 1)
        pair = swap(chosen[3], 0)
        near, other_halo = lax.optimization_barrier((near, other_halo))
        num, den = local_attention(
            (place, local_cols, near), [first_half], w, local_q, (keys, values), True
        )
        second_half, num, den = lax.optimization_barrier((second_half, num, den))
        sources = [features, first_half, second_half]
        chosen = select(place, ((1, 1, (1,), 0), (0, 0, (1,), 0)), share, wanted, sources)
        rest, first, early, pair, *chosen = lax.optimization_barrier(
            (rest, first, early, pair, *chosen)
        )
        first_beside = other(first)
        late = swap(chosen[0], 1)
        late_pair = swap(chosen[1], 0)
        num, den = local_attention(
            (place, local_cols, rest),
            [first_half, second_half, halo, other_halo],
            w,
            local_q,
            (num, den),
            False,
        )
        second, num, den = lax.optimization_barrier((second, num, den))
        last_sources = [other(second)]
        near_sources = [pair, late_pair, early, late, first, second, first_beside]
    else:
        w = jnp.transpose(w_key_value, (1, 0, 2))
        gather = lambda x: lax.all_gather(x, "head", axis=0, tiled=True)
        scales = lax.all_gather(scales, "head", axis=1, tiled=True)
        full = gather(features)
        before = lax.ppermute(full[-margin:], "node", [(i, i + 1) for i in range(blocks - 1)])
        after = lax.ppermute(full[:margin], "node", [(i + 1, i) for i in range(blocks - 1)])
        received = [gather(swap(features, m)) for m in range(MATCH)]
        near_sources, last_sources = received[:2], received[2:]
        matching = jnp.arange(MATCH, dtype=jnp.int32)[:, None]
        near_spots = jnp.where(matching < 2, matching * tiles + exp_cols, -1)
        last_spots = jnp.where(matching < 2, -1, (matching - 2) * tiles + exp_cols)
        where_own = jnp.where(own, own_place, -1)
        where_rest = jnp.where(jnp.logical_and(usable, jnp.logical_not(own)), column + HT, -1)
        keys, values, local_q, expand_q = project_own(features, w, w_query, scales)
        num, den = local_attention(
            (place, local_cols, where_own), [], w, local_q, (keys, values), True
        )
        num, den = local_attention(
            (place, local_cols, where_rest), [before, full, after], w, local_q, (num, den), False
        )
    num, den, out = expand_attention(
        place, exp_rows, near_spots, near_sources, expand_q, num, den, w, None
    )
    return expand_attention(
        place, exp_rows, last_spots, last_sources, expand_q, num, den, w, out
    )


def solution(mesh):
    return jax.shard_map(
        local,
        mesh=mesh,
        in_specs=(
            P(("node", "head"), None),
            P(),
            P(),
            P("head"),
            P("head"),
            P("node", None),
            P("node", None, None),
            P("node", None, None),
        ),
        out_specs=P(("node", "head"), None),
        check_vma=False,
    )
```

```python
import functools
import math

import jax
import jax.numpy as jnp
from jax import lax
from jax.experimental import pallas as pl
from jax.experimental.pallas import tpu as pltpu
from jax.sharding import PartitionSpec as P

HEADS = 8
TILE = 128
HT = 2
MATCH = 4
LANES = 128
GROUP = 4
MIB = 1024 * 1024

ANY = pl.BlockSpec(memory_space=pl.ANY)
SMEM = pl.BlockSpec(memory_space=pltpu.SMEM)
VMEM = pl.BlockSpec(memory_space=pltpu.VMEM)
HBM = pl.BlockSpec(memory_space=pltpu.HBM)


def lane_masks():
    lane = lax.broadcasted_iota(jnp.int32, (TILE, LANES), 1)
    return lane < LANES // 2, lane % (LANES // 2)


def pack_denominators(pieces):
    _, within = lane_masks()
    size = LANES // 2 // len(pieces)
    packed = pieces[-1]
    for pair in range(len(pieces) - 2, -1, -1):
        packed = jnp.where(within < (pair + 1) * size, pieces[pair], packed)
    return packed


def denominator_chooser(pairs):
    size = LANES // 2 // pairs
    shape = (2 * LANES, pairs * LANES)
    source = lax.broadcasted_iota(jnp.int32, shape, 0) % LANES
    target = lax.broadcasted_iota(jnp.int32, shape, 1)
    wanted = target // LANES * size + (target % LANES) // (LANES // 2) * (LANES // 2)
    return jnp.where(source == wanted, 1.0, 0.0).astype(jnp.bfloat16)


def spread_reciprocals(packed, chooser):
    inverse = 1.0 / packed
    coarse = inverse.astype(jnp.bfloat16)
    fine = (inverse - coarse.astype(jnp.float32)).astype(jnp.bfloat16)
    return jnp.dot(
        jnp.concatenate([coarse, fine], axis=1), chooser, preferred_element_type=jnp.float32
    )


def project(rows, w, keys, values, first):
    new_keys = jnp.dot(rows, w[0], preferred_element_type=jnp.float32).astype(jnp.bfloat16).T
    new_values = jnp.dot(rows, w[1], preferred_element_type=jnp.float32).astype(jnp.bfloat16)
    for index in range(rows.shape[0] // TILE):
        span = slice(index * TILE, (index + 1) * TILE)
        keys[first + index] = new_keys[:, span]
        values[first + index] = new_values[span, :]


def attend_chunks(queries, keys, values, ones, num, den, units):
    low, _ = lane_masks()
    low_mask = jnp.where(low, 1.0, 0.0).astype(jnp.bfloat16)
    high_mask = jnp.where(low, 0.0, 1.0).astype(jnp.bfloat16)
    rows = [pl.ds(pl.multiple_of(unit[0] * TILE, TILE), TILE) for unit in units]
    last = queries.shape[0] // TILE - 1
    query_rows = [
        pl.ds(pl.multiple_of(jnp.minimum(unit[0], last) * TILE, TILE), TILE) for unit in units
    ]
    denominators = [[] for _ in units]
    for pair in range(queries.shape[1] // LANES):
        part = slice(pair * LANES, (pair + 1) * LANES)
        weights = []
        for row, (_, one, two, _) in zip(query_rows, units):
            some = queries[row, part]
            scores = jnp.dot(
                jnp.concatenate([some * low_mask, some * high_mask], axis=0),
                jnp.concatenate([keys[one, part, :], keys[two, part, :]], axis=1),
                preferred_element_type=jnp.float32,
            )
            weights.append(jnp.exp(jnp.clip(scores, -5.0, 5.0)).astype(jnp.bfloat16))
        sums = []
        for weight, (_, one, two, fills) in zip(weights, units):
            counts = ones[fills]
            wide = [
                jnp.concatenate([values[one, :, part], ones[0]], axis=1),
                jnp.concatenate([values[two, :, part] * counts, counts], axis=1),
            ]
            sums.append(
                jnp.dot(
                    weight, jnp.concatenate(wide, axis=0), preferred_element_type=jnp.float32
                )
            )
        for row, both, listed in zip(rows, sums, denominators):
            num[row, part] += jnp.where(low, both[:TILE, :LANES], both[TILE:, :LANES])
            listed.append(jnp.where(low, both[:TILE, LANES:], both[TILE:, LANES:]))
    for row, listed in zip(rows, denominators):
        den[row, :] += pack_denominators(listed)


def attend_units(queries, keys, values, num, den, units):
    low_lanes, _ = lane_masks()
    low = jnp.where(low_lanes, 1.0, 0.0).astype(jnp.bfloat16)
    high = jnp.where(low_lanes, 0.0, 1.0).astype(jnp.bfloat16)
    nothing = jnp.zeros((LANES // 2, TILE), jnp.bfloat16)
    rows = [pl.ds(pl.multiple_of(row * TILE, TILE), TILE) for row, _ in units]
    last = queries.shape[0] // TILE - 1
    query_rows = [
        pl.ds(pl.multiple_of(jnp.minimum(row, last) * TILE, TILE), TILE) for row, _ in units
    ]
    denominators = [[] for _ in units]
    for pair in range(queries.shape[1] // LANES):
        part = slice(pair * LANES, (pair + 1) * LANES)
        middle = pair * LANES + LANES // 2
        weights = []
        for row, (_, tile) in zip(query_rows, units):
            first = jnp.concatenate([keys[tile, pair * LANES : middle, :], nothing], axis=0)
            second = jnp.concatenate([nothing, keys[tile, middle : (pair + 1) * LANES, :]], axis=0)
            scores = jnp.dot(
                queries[row, part],
                jnp.concatenate([first, second], axis=1),
                preferred_element_type=jnp.float32,
            )
            weights.append(jnp.exp(jnp.clip(scores, -5.0, 5.0)).astype(jnp.bfloat16))
        sums = []
        for weight, (_, tile) in zip(weights, units):
            value = values[tile, :, part]
            wide = jnp.concatenate(
                [
                    jnp.concatenate([value * low, low], axis=1),
                    jnp.concatenate([value * high, high], axis=1),
                ],
                axis=0,
            )
            sums.append(jnp.dot(weight, wide, preferred_element_type=jnp.float32))
        for row, both, listed in zip(rows, sums, denominators):
            num[row, part] += both[:, :LANES]
            listed.append(both[:, LANES:])
    for row, listed in zip(rows, denominators):
        den[row, :] += pack_denominators(listed)


def project_pieces(pieces, w, keys, values, at):
    for piece in pieces:
        tiles = piece.shape[0] // TILE
        size = math.gcd(tiles, GROUP)

        def some_tiles(index, carry, piece=piece, at=at, size=size):
            some = piece[pl.ds(pl.multiple_of(index * size * TILE, TILE), size * TILE), :]
            project(some, w, keys, values, at + index * size)
            return carry

        lax.fori_loop(0, tiles // size, some_tiles, 0)
        at += tiles


def attend_listed(
    steps, split, place_ref, cols_ref, where_ref, queries, keys, values, num, den, scratch
):
    ones, row_list, tile_list, fill_list = scratch
    tiles_here = queries.shape[0] // TILE
    slots = tile_list.shape[0] - 2 * row_list.shape[0]
    ones[0] = jnp.ones(ones.shape[1:], ones.dtype)
    ones[1] = jnp.zeros(ones.shape[1:], ones.dtype)

    def visit(row, found):
        part = jnp.where(row < split, 0, 1)
        at = 2 * found
        for slot in range(slots):
            tile = where_ref[part, cols_ref[(place_ref[0] * tiles_here + row) * slots + slot]]
            tile_list[at] = tile
            at = at + (tile >= 0).astype(jnp.int32)
        tile_list[at] = 0
        units = (at - 2 * found + 1) // 2
        odd = lax.rem(at, 2)
        for unit in range(slots // 2):
            row_list[found + unit] = row
            fill_list[found + unit] = jnp.where(unit == units - 1, odd, 0)
        return found + units

    found = lax.fori_loop(0, steps, visit, jnp.int32(0))
    for inner in range(GROUP):
        row_list[found + inner] = tiles_here
        fill_list[found + inner] = 0
        tile_list[2 * (found + inner)] = 0
        tile_list[2 * (found + inner) + 1] = 0

    def group(index, carry):
        units = []
        for inner in range(GROUP):
            unit = index * GROUP + inner
            units.append(
                (row_list[unit], tile_list[2 * unit], tile_list[2 * unit + 1], fill_list[unit])
            )
        attend_chunks(queries, keys, values, ones, num, den, units)
        return carry

    lax.fori_loop(0, (found + GROUP - 1) // GROUP, group, 0)


def each_tile(tiles, action):
    def visit(tile, carry):
        action(pl.ds(pl.multiple_of(tile * TILE, TILE), TILE))
        return carry

    lax.fori_loop(0, tiles, visit, 0)


def own_kernel(split, place_ref, cols_ref, where_ref, rows, w, wq, scales, *refs):
    (num, den, keys, values, local_ref, expand_ref) = refs[:6]
    width = rows.shape[1]
    tiles = rows.shape[0] // TILE
    size = min(GROUP, tiles)
    project_pieces([rows], w, keys, values, 0)

    def some_queries(index, carry):
        target = pl.ds(pl.multiple_of(index * size * TILE, TILE), size * TILE)
        queries = jnp.dot(rows[target, :], wq[...], preferred_element_type=jnp.float32)
        queries = queries.astype(jnp.bfloat16).astype(jnp.float32)
        scale = 1.0 / math.sqrt(width // HEADS)
        local_ref[target, :] = (queries * scales[0:1, :] * scale).astype(jnp.bfloat16)
        expand_ref[target, :] = (queries * scales[1:2, :] * scale).astype(jnp.bfloat16)
        return carry

    lax.fori_loop(0, tiles // size, some_queries, 0)

    def clear(target):
        num[target, :] = jnp.zeros((TILE, width), jnp.float32)
        den[target, :] = jnp.zeros((TILE, LANES), jnp.float32)

    each_tile(tiles + 1, clear)
    attend_listed(
        split, split, place_ref, cols_ref, where_ref, local_ref, keys, values, num, den, refs[6:]
    )


def more_kernel(count, from_own, split, place_ref, cols_ref, where_ref, *refs):
    pieces = refs[:count]
    (w, local_ref, num_in, den_in) = refs[count : count + 4]
    refs = refs[count + 4 :]
    if from_own:
        (own_keys, own_values, num, den, *scratch, keys, values) = refs
        first = own_keys.shape[0]

        def bring(tile, carry):
            keys[tile] = own_keys[tile]
            values[tile] = own_values[tile]
            return carry

        lax.fori_loop(0, first, bring, 0)
    else:
        (num, den, *scratch, keys, values) = refs
        first = 0
    project_pieces(pieces, w, keys, values, first)

    def begin(target):
        num[target, :] = num_in[target, :]
        den[target, :] = den_in[target, :]

    tiles = local_ref.shape[0] // TILE
    each_tile(tiles + 1, begin)
    attend_listed(
        tiles, split, place_ref, cols_ref, where_ref, local_ref, keys, values, num, den, scratch
    )


def sums_shapes(own_rows, width):
    return [
        jax.ShapeDtypeStruct((own_rows + TILE, width), jnp.float32),
        jax.ShapeDtypeStruct((own_rows + TILE, LANES), jnp.float32),
    ]


def list_scratch(own_rows, slots):
    units = own_rows // TILE * (slots // 2) + GROUP
    return [
        pltpu.VMEM((2, TILE, LANES), jnp.bfloat16),
        pltpu.SMEM((units,), jnp.int32),
        pltpu.SMEM((2 * units + slots,), jnp.int32),
        pltpu.SMEM((units,), jnp.int32),
    ]


def own_attention(tables, rows, w, wq, scales, split, slots):
    own_rows, width = rows.shape
    tiles = own_rows // TILE
    shapes = [(tiles, width, TILE), (tiles, TILE, width), rows.shape, rows.shape]
    return pl.pallas_call(
        functools.partial(own_kernel, split),
        in_specs=[SMEM] * 3 + [VMEM] * 4,
        out_specs=[VMEM] * 6,
        out_shape=sums_shapes(own_rows, width)
        + [jax.ShapeDtypeStruct(shape, jnp.bfloat16) for shape in shapes],
        scratch_shapes=list_scratch(own_rows, slots),
        compiler_params=pltpu.CompilerParams(vmem_limit_bytes=24 * MIB),
        cost_estimate=pl.CostEstimate(flops=10**8, bytes_accessed=10**5, transcendentals=0),
    )(*tables, rows, w, wq, scales)


def more_attention(tables, pieces, w, local_q, num, den, own, split, slots):
    own_rows, width = local_q.shape
    tiles = sum(piece.shape[0] // TILE for piece in pieces) + (own_rows // TILE if own else 0)
    return pl.pallas_call(
        functools.partial(more_kernel, len(pieces), bool(own), split),
        in_specs=[SMEM] * 3 + [VMEM] * (len(pieces) + 4 + len(own)),
        out_specs=[VMEM] * 2,
        out_shape=sums_shapes(own_rows, width),
        scratch_shapes=list_scratch(own_rows, slots)
        + [
            pltpu.VMEM((tiles, width, TILE), jnp.bfloat16),
            pltpu.VMEM((tiles, TILE, width), jnp.bfloat16),
        ],
        compiler_params=pltpu.CompilerParams(vmem_limit_bytes=24 * MIB),
        cost_estimate=pl.CostEstimate(
            flops=10**12 if own else 10**8, bytes_accessed=10**5, transcendentals=0
        ),
    )(*tables, *pieces, w, local_q, num, den, *own)


def expand_kernel(count, gives_out, last, place_ref, rows_ref, spots_ref, *refs):
    sources = refs[:count]
    (expand_q, num_in, den_in, w) = refs[count : count + 4]
    refs = refs[count + 4 :]
    if last:
        (_, out_ref, features, keys, values, num, den, row_list, tile_list, mark) = refs[:-3]
        (results, result_sems) = refs[-3:-1]
    else:
        if gives_out:
            (num, den, out_ref) = refs[:3]
        else:
            (num, den) = refs[:2]
        (features, keys, values, row_list, tile_list, mark) = refs[-7:-1]
    chooser = refs[-1]
    own_rows, width = expand_q.shape
    tiles_here = own_rows // TILE
    matchings, edges = rows_ref.shape
    if gives_out:
        chooser[...] = denominator_chooser(width // LANES)
    for tile in range(tiles_here):
        mark[tile] = 0 if last else 1

    def visit(edge, found):
        for matching in range(matchings):
            row = rows_ref[matching, edge] - place_ref[0] * tiles_here
            spot = spots_ref[matching, edge]
            mine = jnp.logical_and(jnp.logical_and(row >= 0, row < tiles_here), spot >= 0)
            row_list[found] = row
            tile_list[found] = spot
            found = found + mine.astype(jnp.int32)
            if last:

                @pl.when(mine)
                def _():
                    mark[row] = 1

        return found

    found = lax.fori_loop(0, edges, visit, jnp.int32(0))
    for inner in range(GROUP):
        row_list[found + inner] = tiles_here
        tile_list[found + inner] = 0

    def each_marked(action):
        def visit_tile(tile, carry):
            target = pl.ds(pl.multiple_of(tile * TILE, TILE), TILE)
            pl.when(mark[tile] == 1)(lambda: action(tile, target))
            return carry

        lax.fori_loop(0, tiles_here, visit_tile, 0)

    def begin(tile, target):
        num[target, :] = num_in[target, :]
        den[target, :] = den_in[target, :]

    each_marked(begin)
    spare = pl.ds(own_rows, TILE)
    num[spare, :] = jnp.zeros((TILE, width), jnp.float32)
    den[spare, :] = jnp.zeros((TILE, LANES), jnp.float32)

    def group(index, carry):
        first = index * GROUP
        for i in range(GROUP):
            spot = tile_list[first + i]
            for source in sources:
                tiles = source.shape[0] // TILE

                @pl.when(jnp.logical_and(spot >= 0, spot < tiles))
                def _(source=source, spot=spot):
                    rows = pl.ds(pl.multiple_of(spot * TILE, TILE), TILE)
                    features[i * TILE : (i + 1) * TILE, :] = source[rows, :]

                spot = spot - tiles
        project(features[...], w, keys, values, 0)
        units = [(row_list[first + i], i) for i in range(GROUP)]
        attend_units(expand_q, keys, values, num, den, units)
        return carry

    lax.fori_loop(0, (found + GROUP - 1) // GROUP, group, 0)

    def finish(tile, target):
        inverse = spread_reciprocals(den[target, :], chooser[...])
        result = (num[target, :] * inverse).astype(jnp.bfloat16)
        if last:
            results[target, :] = result
            copy_out(tile, target).start()
        else:
            out_ref[target, :] = result

    def copy_out(tile, target):
        return pltpu.make_async_copy(results.at[target], out_ref.at[target], result_sems.at[tile])

    if gives_out:
        each_marked(finish)
    if last:
        each_marked(lambda tile, target: copy_out(tile, target).wait())


def expand_attention(place, exp_rows, spots, sources, expand_q, num, den, w, gives_out, out):
    width = w.shape[2]
    own_rows = expand_q.shape[0]
    last = out is not None
    most = exp_rows.shape[0] * exp_rows.shape[1] + GROUP
    sums = sums_shapes(own_rows, width)
    result = jax.ShapeDtypeStruct((own_rows, width), jnp.bfloat16)
    sums_scratch = [pltpu.VMEM(array.shape, array.dtype) for array in sums]
    arguments = [place, exp_rows, spots, *sources, expand_q, num, den, w]
    return pl.pallas_call(
        functools.partial(expand_kernel, len(sources), gives_out, last),
        in_specs=[SMEM] * 3 + [VMEM] * (len(sources) + 4) + [ANY] * last,
        out_specs=ANY if last else [VMEM] * (2 + gives_out),
        out_shape=result if last else sums + [result] * gives_out,
        input_output_aliases={len(arguments): 0} if last else {},
        scratch_shapes=[
            pltpu.VMEM((GROUP * TILE, width), jnp.bfloat16),
            pltpu.VMEM((GROUP, width, TILE), jnp.bfloat16),
            pltpu.VMEM((GROUP, TILE, width), jnp.bfloat16),
        ]
        + (sums_scratch if last else [])
        + [
            pltpu.SMEM((most,), jnp.int32),
            pltpu.SMEM((most,), jnp.int32),
            pltpu.SMEM((own_rows // TILE,), jnp.int32),
        ]
        + (
            [
                pltpu.VMEM((own_rows, width), jnp.bfloat16),
                pltpu.SemaphoreType.DMA((own_rows // TILE,)),
            ]
            if last
            else []
        )
        + [pltpu.VMEM((2 * LANES, width), jnp.bfloat16)],
        compiler_params=pltpu.CompilerParams(vmem_limit_bytes=24 * MIB),
        cost_estimate=pl.CostEstimate(
            flops=own_rows * width * 256, bytes_accessed=own_rows * width, transcendentals=0
        ),
    )(*arguments, *([out] if last else []))


def cut_half_kernel(here_ref, features, half_ref, buffer, sem):
    rows = half_ref.shape[0]
    start = pl.multiple_of(here_ref[0] * rows, TILE)
    inward = pltpu.make_async_copy(features.at[pl.ds(start, rows)], buffer, sem)
    inward.start()
    inward.wait()
    outward = pltpu.make_async_copy(buffer, half_ref, sem)
    outward.start()
    outward.wait()


def cut_half(here, features):
    half = (features.shape[0] // 2, features.shape[1])
    return pl.pallas_call(
        cut_half_kernel,
        in_specs=[SMEM, ANY],
        out_specs=ANY,
        out_shape=jax.ShapeDtypeStruct(half, jnp.bfloat16),
        scratch_shapes=[pltpu.VMEM(half, jnp.bfloat16), pltpu.SemaphoreType.DMA],
        compiler_params=pltpu.CompilerParams(vmem_limit_bytes=60 * MIB),
    )(here, features)


def cut_rest_kernel(here_ref, features, half_ref, edge_ref, sems):
    here = here_ref[0]
    half, margin = half_ref.shape[0], edge_ref.shape[0]
    copies = []
    for index, (start, target) in enumerate(
        [((1 - here) * half, half_ref), (here * (2 * half - margin), edge_ref)]
    ):
        rows = pl.ds(pl.multiple_of(start, TILE), target.shape[0])
        copies.append(pltpu.make_async_copy(features.at[rows], target, sems.at[index]))
    for copy in copies:
        copy.start()
    for copy in copies:
        copy.wait()


def cut_rest(here, features, margin):
    rows, width = features.shape
    return pl.pallas_call(
        cut_rest_kernel,
        in_specs=[SMEM, ANY],
        out_specs=[VMEM] * 2,
        out_shape=[
            jax.ShapeDtypeStruct((rows // 2, width), jnp.bfloat16),
            jax.ShapeDtypeStruct((margin, width), jnp.bfloat16),
        ],
        scratch_shapes=[pltpu.SemaphoreType.DMA((2,))],
        compiler_params=pltpu.CompilerParams(vmem_limit_bytes=8 * MIB),
        cost_estimate=pl.CostEstimate(flops=10**11, bytes_accessed=4096, transcendentals=0),
    )(here, features)


def select_kernel(jobs, share, sources, margin, place_ref, *refs):
    matchings = len(refs) - sources - len(jobs) - (margin > 0)
    wanted = refs[:matchings]
    parts = refs[matchings : matchings + sources]
    outs = refs[matchings + sources :]
    here = place_ref[0]
    even = lax.rem(place_ref[1], 2) == 0
    quarter = parts[1].shape[0] // TILE
    if margin:
        start = pl.multiple_of((1 - here) * (quarter * TILE - margin), TILE)
        outs[-1][...] = parts[1][pl.ds(start, margin), :]
    per_part = 2 * quarter
    flat = []
    for (of_even, of_odd, lines), out in zip(jobs, outs):
        at = 0
        for line in lines:
            start = (here if line == 0 else 1 - here) * share
            for slot in range(share):
                tile = wanted[of_even][0, start + slot]
                if of_odd != of_even:
                    tile = jnp.where(even, tile, wanted[of_odd][0, start + slot])
                flat.append((tile, out, at))
                at += 1
    for tile, out, slot in flat:
        own = tile // per_part == here
        place = tile // quarter
        end = jnp.logical_or(place == 0, place == 3)
        target = slice(slot * TILE, (slot + 1) * TILE)

        @pl.when(own)
        def _():
            start = pl.multiple_of(lax.rem(tile, per_part) * TILE, TILE)
            out[target, :] = parts[0][pl.ds(start, TILE), :]

        start = pl.multiple_of(lax.rem(tile, quarter) * TILE, TILE)

        @pl.when(jnp.logical_and(jnp.logical_not(own), end))
        def _():
            out[target, :] = parts[1][pl.ds(start, TILE), :]

        if sources > 2:

            @pl.when(jnp.logical_not(jnp.logical_or(own, end)))
            def _():
                out[target, :] = parts[2][pl.ds(start, TILE), :]


def select(place, jobs, share, wanted, parts, margin=0):
    width = parts[0].shape[1]
    sizes = [share * len(lines) * TILE for _, _, lines in jobs]
    sizes += [margin] * (margin > 0)
    return pl.pallas_call(
        functools.partial(select_kernel, jobs, share, len(parts), margin),
        in_specs=[SMEM] * (1 + len(wanted)) + [VMEM] * len(parts),
        out_specs=[VMEM] * len(sizes),
        out_shape=[jax.ShapeDtypeStruct((size, width), jnp.bfloat16) for size in sizes],
        compiler_params=pltpu.CompilerParams(vmem_limit_bytes=16 * MIB),
        cost_estimate=pl.CostEstimate(flops=1000, bytes_accessed=1000, transcendentals=0),
    )(place, *wanted, *parts)


def rank_tiles(tiles, edges, column_of, mark, on_tile):
    every = range(mark.shape[0])
    quarter = tiles // 4
    for tile in range(tiles):
        for matching in every:
            mark[matching, tile] = 0
    missing = [jnp.int32(edges)] * len(every)
    for edge in range(edges):
        for matching in every:
            tile = column_of(matching, edge)
            missing[matching] = missing[matching] - (1 - mark[matching, tile])
            mark[matching, tile] = 1
    rank = [jnp.int32(0)] * len(every)
    for at in range(tiles):
        tile = at + (quarter if at // quarter % 2 == 0 else -quarter)
        for matching in every:
            present = mark[matching, tile]
            added = jnp.where(jnp.logical_and(present == 0, missing[matching] > 0), 1, 0)
            on_tile(matching, tile, rank[matching])
            rank[matching] = rank[matching] + present + added
            missing[matching] = missing[matching] - added


def spots_kernel(tiles, lines, blocks, here_ref, block_ref, cols_ref, *refs):
    (place_ref, own_ref, near_table, rest_table) = refs[:4]
    spots_refs = refs[4:7]
    wanted_refs = refs[7:-2]
    mark, rank_of = refs[-2:]
    matchings, edges = cols_ref.shape
    share = edges // lines
    here, block = here_ref[0], block_ref[0]
    odd = lax.rem(block, 2)
    place_ref[0] = here
    place_ref[1] = block
    per_part = tiles // lines
    quarter = per_part // 2
    for index in range(tiles + 2 * HT):
        column = index - HT
        if 0 <= column < tiles:
            own = here == column // per_part
            own_place = jnp.where(own, column % per_part, -1)
            within = column % quarter
            end = column // quarter in (0, 3)
            near = jnp.where(own, -1, per_part + within if end else -1)
            rest = jnp.where(own, -1, -1 if end else within)
        else:
            after = column >= tiles
            own_place = near = jnp.int32(-1)
            ours = here == (0 if after else 1)
            rest = (column - tiles if after else column + HT) + jnp.where(ours, quarter + HT, quarter)
            rest = jnp.where(block < blocks - 1 if after else block > 0, rest, -1)
        own_ref[0, index] = own_place
        own_ref[1, index] = -1
        near_table[0, index] = near
        near_table[1, index] = jnp.maximum(near, own_place)
        rest_table[0, index] = rest
        rest_table[1, index] = rest

    def on_tile(matching, tile, slot):
        rank_of[matching, tile] = slot
        wanted_refs[matching][0, slot] = tile

    rank_tiles(tiles, edges, lambda matching, edge: cols_ref[matching, edge], mark, on_tile)
    for edge in range(edges):
        for matching in range(matchings):
            slot = rank_of[matching, cols_ref[matching, edge]]
            away = jnp.where(slot // share == here, 0, 1)
            within = lax.rem(slot, share)
            if matching == 0:
                when, spot = 0, away * share + within
            elif matching == 1:
                when, spot = away, within + jnp.where(away == 0, 3 * share, 0)
            else:
                second = odd if matching == matchings - 1 else 1 - odd
                when = jnp.where(away == 0, second, 1 + second)
                spot = within + share * jnp.where(second == 0, 2, jnp.where(away == 0, 1, odd))
            for index, spots_ref in enumerate(spots_refs):
                spots_ref[matching, edge] = jnp.where(when == index, spot, -1)


def arrival_spots(here, block, blocks, cols, tiles, lines):
    wanted = jax.ShapeDtypeStruct((1, 2 * cols.shape[1]), jnp.int32)
    spots = jax.ShapeDtypeStruct(cols.shape, jnp.int32)
    table = jax.ShapeDtypeStruct((2, tiles + 2 * HT), jnp.int32)
    place = jax.ShapeDtypeStruct((2,), jnp.int32)
    place, *rest = pl.pallas_call(
        functools.partial(spots_kernel, tiles, lines, blocks),
        in_specs=[SMEM] * 3,
        out_specs=[SMEM] * (7 + cols.shape[0]),
        out_shape=[place] + [table] * 3 + [spots] * 3 + [wanted] * cols.shape[0],
        scratch_shapes=[pltpu.SMEM((cols.shape[0], tiles), jnp.int32)] * 2,
        compiler_params=pltpu.CompilerParams(vmem_limit_bytes=8 * MIB),
        cost_estimate=pl.CostEstimate(flops=10**11, bytes_accessed=4096, transcendentals=0),
    )(here, block, cols)
    return place, rest[:3], rest[3:6], rest[6:]


def local(features, w_query, w_key_value, edge_local, edge_expand, local_cols, exp_rows, exp_cols):
    groups = lax.axis_size("head")
    blocks = lax.axis_size("node")
    own_rows, width = features.shape
    here = lax.axis_index("head")
    block = lax.axis_index("node")
    edges = exp_cols.shape[2]
    tiles = local_cols.shape[0]
    own_tiles = own_rows // TILE
    margin = HT * TILE
    exp_rows, exp_cols = exp_rows[0], exp_cols[0]
    log_count = blocks.bit_length() - 1
    flips = [1 << matching * log_count // MATCH for matching in range(MATCH)]

    def swap(x, matching, of_odd=None):
        flip = [flips[matching], flips[matching if of_odd is None else of_odd]]
        return lax.ppermute(x, "node", [(i, i ^ flip[i % 2]) for i in range(blocks)])

    def other(x):
        return lax.ppermute(x, "head", [(0, 1), (1, 0)])

    scales = jnp.stack([edge_local, edge_expand])
    listed = local_cols.shape[1]
    split = own_tiles
    two = groups == 2 and min(flips[2:]) > 1

    if two:
        split = own_tiles // 4
        here_array = jnp.reshape(here, (1,)).astype(jnp.int32)
        block_array = jnp.reshape(block, (1,)).astype(jnp.int32)
        first_half = cut_half(here_array, features)
        beside = other(scales)
        first_half, features, exp_cols, local_cols, beside, w_query, w_key_value = (
            lax.optimization_barrier(
                (first_half, features, exp_cols, local_cols, beside, w_query, w_key_value)
            )
        )
        local_cols = local_cols.reshape(-1)
        w = jnp.transpose(w_key_value, (1, 0, 2))
        first_half = other(first_half)
        second_half, edge_rows = cut_rest(here_array, features, margin)
        place, tables, spots, wanted = arrival_spots(
            here_array, block_array, blocks, exp_cols, tiles, groups
        )
        edge_rows, *wanted = lax.optimization_barrier((edge_rows, *wanted))
        wanted_pair, *wanted = wanted
        wanted = [swap(wanted[m - 1], m) for m in range(1, MATCH)]
        inward = [(2 * i, 2 * i - 2) for i in range(1, blocks)]
        inward += [(2 * i + 1, 2 * i + 3) for i in range(blocks - 1)]
        halo = lax.ppermute(edge_rows, ("node", "head"), inward)
        scales = jnp.where(
            here == 0,
            jnp.concatenate([scales, beside], axis=1),
            jnp.concatenate([beside, scales], axis=1),
        )
        scales, w, local_cols, halo, *wanted = lax.optimization_barrier(
            (scales, w, local_cols, halo, *wanted)
        )
        num, den, keys, values, local_q, expand_q = own_attention(
            (place, local_cols, tables[0]), features, w, w_query, scales, split, listed
        )
        first_half, second_half, num = lax.optimization_barrier((first_half, second_half, num))
        second_half = other(second_half)
        share = edges // groups
        sources = [features, first_half]
        jobs = ((2, 1, (0,)), (1, 2, (0,)), (0, 0, (0,)))
        *chosen, edge_rows = select(place, jobs, share, wanted, sources, margin)
        num, *chosen = lax.optimization_barrier((num, *chosen))
        first = swap(chosen[0], 3, 2)
        early = swap(chosen[2], 1)
        num, den = more_attention(
            (place, local_cols, tables[1]),
            [first_half],
            w,
            local_q,
            num,
            den,
            (keys, values),
            split,
            listed,
        )
        second_half, num, den, edge_rows, wanted_pair, second = lax.optimization_barrier(
            (second_half, num, den, edge_rows, wanted_pair, chosen[1])
        )
        outward = [(2 * i, 2 * i + 2) for i in range(blocks - 1)]
        outward += [(2 * i + 1, 2 * i - 1) for i in range(1, blocks)]
        other_halo = lax.ppermute(edge_rows, ("node", "head"), outward)
        wanted_pair = swap(wanted_pair, 0)
        sources = [features, first_half, second_half]
        late, direct = select(place, ((0, 0, (1,)), (1, 1, (1,))), share, wanted, sources)
        num, first, early, late = lax.optimization_barrier((num, first, early, late))
        second = swap(second, 2, 3)
        first_beside = other(first)
        late = swap(late, 1)
        (pair,) = select(place, ((0, 0, (0, 1)),), share, [wanted_pair], sources)
        num, pair, other_halo = lax.optimization_barrier((num, pair, other_halo))
        pair = swap(pair, 0)
        num, den = more_attention(
            (place, local_cols, tables[2]),
            [second_half, other_halo, halo],
            w,
            local_q,
            num,
            den,
            (),
            split,
            listed,
        )
        num, den = expand_attention(
            place, exp_rows, spots[0], [pair, first, early], expand_q, num, den, w, False, None
        )
        second, direct, num, den = lax.optimization_barrier((second, direct, num, den))
        direct = lax.ppermute(direct, "node", [(i, i ^ flips[2]) for i in range(0, blocks, 2)])
        sides = [(4 * i + 2 + side, 4 * i + 3 - side) for i in range(blocks // 2) for side in (0, 1)]
        second_beside = lax.ppermute(second, ("node", "head"), sides)
        sources = [None, [late, second, first_beside], [direct, second_beside]]
    else:
        place = jnp.stack([here, block]).astype(jnp.int32)
        column = jnp.arange(tiles + 2 * HT, dtype=jnp.int32) - HT
        usable = block * tiles + column
        usable = jnp.logical_and(usable >= 0, usable < blocks * tiles)
        own = column // own_tiles == here
        w = jnp.transpose(w_key_value, (1, 0, 2))
        gather = lambda x: lax.all_gather(x, "head", axis=0, tiled=True)
        scales = lax.all_gather(scales, "head", axis=1, tiled=True)
        full = gather(features)
        before = lax.ppermute(full[-margin:], "node", [(i, i + 1) for i in range(blocks - 1)])
        after = lax.ppermute(full[:margin], "node", [(i + 1, i) for i in range(blocks - 1)])
        received = [gather(swap(features, m)) for m in range(MATCH)]
        sources = [None, received[:2], received[2:]]
        matching = jnp.arange(MATCH, dtype=jnp.int32)[:, None]
        spots = [
            None,
            jnp.where(matching < 2, matching * tiles + exp_cols, -1),
            jnp.where(matching < 2, -1, (matching - 2) * tiles + exp_cols),
        ]
        where_own = jnp.where(own, column - here * own_tiles, -1)
        where_rest = jnp.where(jnp.logical_and(usable, jnp.logical_not(own)), column + HT, -1)
        local_cols = local_cols.reshape(-1)
        num, den, keys, values, local_q, expand_q = own_attention(
            (place, local_cols, jnp.stack([where_own] * 2)),
            features,
            w,
            w_query,
            scales,
            split,
            listed,
        )
        num, den = more_attention(
            (place, local_cols, jnp.stack([where_rest] * 2)),
            [before, full, after],
            w,
            local_q,
            num,
            den,
            (),
            split,
            listed,
        )
    num, den, out = expand_attention(
        place, exp_rows, spots[1], sources[1], expand_q, num, den, w, True, None
    )
    return expand_attention(
        place, exp_rows, spots[2], sources[2], expand_q, num, den, w, True, out
    )


def solution(mesh):
    return jax.shard_map(
        local,
        mesh=mesh,
        in_specs=(
            P(("node", "head"), None),
            P(),
            P(),
            P("head"),
            P("head"),
            P("node", None),
            P("node", None, None),
            P("node", None, None),
        ),
        out_specs=P(("node", "head"), None),
        check_vma=False,
    )
```

```python
import functools
import math

import jax
import jax.numpy as jnp
from jax import lax
from jax.experimental import pallas as pl
from jax.experimental.pallas import tpu as pltpu
from jax.sharding import PartitionSpec as P

HEADS = 8
TILE = 128
HT = 2
MATCH = 4
LANES = 128
GROUP = 4
MIB = 1024 * 1024

ANY = pl.BlockSpec(memory_space=pl.ANY)
SMEM = pl.BlockSpec(memory_space=pltpu.SMEM)
VMEM = pl.BlockSpec(memory_space=pltpu.VMEM)
HBM = pl.BlockSpec(memory_space=pltpu.HBM)


def lane_masks():
    lane = lax.broadcasted_iota(jnp.int32, (TILE, LANES), 1)
    return lane < LANES // 2, lane % (LANES // 2)


def pack_denominators(pieces):
    _, within = lane_masks()
    size = LANES // 2 // len(pieces)
    packed = pieces[-1]
    for pair in range(len(pieces) - 2, -1, -1):
        packed = jnp.where(within < (pair + 1) * size, pieces[pair], packed)
    return packed


def denominator_chooser(pairs):
    size = LANES // 2 // pairs
    shape = (2 * LANES, pairs * LANES)
    source = lax.broadcasted_iota(jnp.int32, shape, 0) % LANES
    target = lax.broadcasted_iota(jnp.int32, shape, 1)
    wanted = target // LANES * size + (target % LANES) // (LANES // 2) * (LANES // 2)
    return jnp.where(source == wanted, 1.0, 0.0).astype(jnp.bfloat16)


def spread_reciprocals(packed, chooser):
    inverse = 1.0 / packed
    coarse = inverse.astype(jnp.bfloat16)
    fine = (inverse - coarse.astype(jnp.float32)).astype(jnp.bfloat16)
    return jnp.dot(
        jnp.concatenate([coarse, fine], axis=1), chooser, preferred_element_type=jnp.float32
    )


def project(rows, w, keys, values, first):
    new_keys = jnp.dot(rows, w[0], preferred_element_type=jnp.float32).astype(jnp.bfloat16).T
    new_values = jnp.dot(rows, w[1], preferred_element_type=jnp.float32).astype(jnp.bfloat16)
    for index in range(rows.shape[0] // TILE):
        span = slice(index * TILE, (index + 1) * TILE)
        keys[first + index] = new_keys[:, span]
        values[first + index] = new_values[span, :]


def attend_chunks(queries, keys, values, ones, num, den, units):
    low, _ = lane_masks()
    low_mask = jnp.where(low, 1.0, 0.0).astype(jnp.bfloat16)
    high_mask = jnp.where(low, 0.0, 1.0).astype(jnp.bfloat16)
    rows = [pl.ds(pl.multiple_of(unit[0] * TILE, TILE), TILE) for unit in units]
    last = queries.shape[0] // TILE - 1
    query_rows = [
        pl.ds(pl.multiple_of(jnp.minimum(unit[0], last) * TILE, TILE), TILE) for unit in units
    ]
    denominators = [[] for _ in units]
    for pair in range(queries.shape[1] // LANES):
        part = slice(pair * LANES, (pair + 1) * LANES)
        weights = []
        for row, (_, one, two, _) in zip(query_rows, units):
            some = queries[row, part]
            scores = jnp.dot(
                jnp.concatenate([some * low_mask, some * high_mask], axis=0),
                jnp.concatenate([keys[one, part, :], keys[two, part, :]], axis=1),
                preferred_element_type=jnp.float32,
            )
            weights.append(jnp.exp(jnp.clip(scores, -5.0, 5.0)).astype(jnp.bfloat16))
        sums = []
        for weight, (_, one, two, fills) in zip(weights, units):
            counts = ones[fills]
            wide = [
                jnp.concatenate([values[one, :, part], ones[0]], axis=1),
                jnp.concatenate([values[two, :, part] * counts, counts], axis=1),
            ]
            sums.append(
                jnp.dot(
                    weight, jnp.concatenate(wide, axis=0), preferred_element_type=jnp.float32
                )
            )
        for row, both, listed in zip(rows, sums, denominators):
            num[row, part] += jnp.where(low, both[:TILE, :LANES], both[TILE:, :LANES])
            listed.append(jnp.where(low, both[:TILE, LANES:], both[TILE:, LANES:]))
    for row, listed in zip(rows, denominators):
        den[row, :] += pack_denominators(listed)


def attend_units(queries, rows_here, w, num, den, rows):
    keys = jnp.dot(rows_here, w[0], preferred_element_type=jnp.float32).astype(jnp.bfloat16)
    values = jnp.dot(rows_here, w[1], preferred_element_type=jnp.float32).astype(jnp.bfloat16)
    low_lanes, _ = lane_masks()
    low = jnp.where(low_lanes, 1.0, 0.0).astype(jnp.bfloat16)
    high = jnp.where(low_lanes, 0.0, 1.0).astype(jnp.bfloat16)
    last = queries.shape[0] // TILE - 1
    query_rows = [
        pl.ds(pl.multiple_of(jnp.minimum(row, last) * TILE, TILE), TILE) for row in rows
    ]
    rows = [pl.ds(pl.multiple_of(row * TILE, TILE), TILE) for row in rows]
    spans = [slice(index * TILE, (index + 1) * TILE) for index in range(len(rows))]
    denominators = [[] for _ in rows]
    for pair in range(queries.shape[1] // LANES):
        part = slice(pair * LANES, (pair + 1) * LANES)
        weights = []
        for row, span in zip(query_rows, spans):
            key = keys[span, part]
            scores = lax.dot_general(
                queries[row, part],
                jnp.concatenate([key * low, key * high], axis=0),
                (((1,), (1,)), ((), ())),
                preferred_element_type=jnp.float32,
            )
            weights.append(jnp.exp(jnp.clip(scores, -5.0, 5.0)).astype(jnp.bfloat16))
        sums = []
        for weight, span in zip(weights, spans):
            value = values[span, part]
            wide = jnp.concatenate(
                [
                    jnp.concatenate([value * low, low], axis=1),
                    jnp.concatenate([value * high, high], axis=1),
                ],
                axis=0,
            )
            sums.append(jnp.dot(weight, wide, preferred_element_type=jnp.float32))
        for row, both, listed in zip(rows, sums, denominators):
            num[row, part] += both[:, :LANES]
            listed.append(both[:, LANES:])
    for row, listed in zip(rows, denominators):
        den[row, :] += pack_denominators(listed)


def project_pieces(pieces, w, keys, values, at):
    for piece in pieces:
        tiles = piece.shape[0] // TILE
        size = math.gcd(tiles, GROUP)

        def some_tiles(index, carry, piece=piece, at=at, size=size):
            some = piece[pl.ds(pl.multiple_of(index * size * TILE, TILE), size * TILE), :]
            project(some, w, keys, values, at + index * size)
            return carry

        lax.fori_loop(0, tiles // size, some_tiles, 0)
        at += tiles


def attend_listed(
    steps, split, place_ref, cols_ref, where_ref, queries, keys, values, num, den, scratch
):
    ones, row_list, tile_list, fill_list = scratch
    tiles_here = queries.shape[0] // TILE
    slots = tile_list.shape[0] - 2 * row_list.shape[0]
    ones[0] = jnp.ones(ones.shape[1:], ones.dtype)
    ones[1] = jnp.zeros(ones.shape[1:], ones.dtype)

    def visit(row, found):
        part = jnp.where(row < split, 0, 1)
        at = 2 * found
        for slot in range(slots):
            tile = where_ref[part, cols_ref[(place_ref[0] * tiles_here + row) * slots + slot]]
            tile_list[at] = tile
            at = at + (tile >= 0).astype(jnp.int32)
        tile_list[at] = 0
        units = (at - 2 * found + 1) // 2
        odd = lax.rem(at, 2)
        for unit in range(slots // 2):
            row_list[found + unit] = row
            fill_list[found + unit] = jnp.where(unit == units - 1, odd, 0)
        return found + units

    found = lax.fori_loop(0, steps, visit, jnp.int32(0))
    for inner in range(GROUP):
        row_list[found + inner] = tiles_here
        fill_list[found + inner] = 0
        tile_list[2 * (found + inner)] = 0
        tile_list[2 * (found + inner) + 1] = 0

    def group(first, size):
        units = []
        for inner in range(size):
            unit = first + inner
            units.append(
                (row_list[unit], tile_list[2 * unit], tile_list[2 * unit + 1], fill_list[unit])
            )
        attend_chunks(queries, keys, values, ones, num, den, units)

    in_groups(found, group)


def in_groups(found, group):
    whole = found // GROUP

    def visit(index, carry):
        group(index * GROUP, GROUP)
        return carry

    lax.fori_loop(0, whole, visit, 0)
    left = found - whole * GROUP
    half = GROUP // 2
    pl.when(left > half)(lambda: group(whole * GROUP, GROUP))
    pl.when(jnp.logical_and(left > 0, left <= half))(lambda: group(whole * GROUP, half))


def each_tile(tiles, action):
    def visit(tile, carry):
        action(pl.ds(pl.multiple_of(tile * TILE, TILE), TILE))
        return carry

    lax.fori_loop(0, tiles, visit, 0)


def own_kernel(split, place_ref, cols_ref, where_ref, rows, w, wq, scales, *refs):
    (num, den, keys, values, local_ref, expand_ref) = refs[:6]
    width = rows.shape[1]
    tiles = rows.shape[0] // TILE
    size = min(GROUP, tiles)
    project_pieces([rows], w, keys, values, 0)

    def some_queries(index, carry):
        target = pl.ds(pl.multiple_of(index * size * TILE, TILE), size * TILE)
        queries = jnp.dot(rows[target, :], wq[...], preferred_element_type=jnp.float32)
        queries = queries.astype(jnp.bfloat16).astype(jnp.float32)
        scale = 1.0 / math.sqrt(width // HEADS)
        local_ref[target, :] = (queries * scales[0:1, :] * scale).astype(jnp.bfloat16)
        expand_ref[target, :] = (queries * scales[1:2, :] * scale).astype(jnp.bfloat16)
        return carry

    lax.fori_loop(0, tiles // size, some_queries, 0)

    def clear(target):
        num[target, :] = jnp.zeros((TILE, width), jnp.float32)
        den[target, :] = jnp.zeros((TILE, LANES), jnp.float32)

    each_tile(tiles + 1, clear)
    attend_listed(
        split, split, place_ref, cols_ref, where_ref, local_ref, keys, values, num, den, refs[6:]
    )


def more_kernel(count, from_own, split, place_ref, cols_ref, where_ref, *refs):
    pieces = refs[:count]
    (w, local_ref, num_in, den_in) = refs[count : count + 4]
    refs = refs[count + 4 :]
    if from_own:
        (own_keys, own_values, num, den, *scratch, keys, values) = refs
        first = own_keys.shape[0]

        def bring(tile, carry):
            keys[tile] = own_keys[tile]
            values[tile] = own_values[tile]
            return carry

        lax.fori_loop(0, first, bring, 0)
    else:
        (num, den, *scratch, keys, values) = refs
        first = 0
    project_pieces(pieces, w, keys, values, first)

    def begin(target):
        num[target, :] = num_in[target, :]
        den[target, :] = den_in[target, :]

    tiles = local_ref.shape[0] // TILE
    each_tile(tiles + 1, begin)
    attend_listed(
        tiles, split, place_ref, cols_ref, where_ref, local_ref, keys, values, num, den, scratch
    )


def sums_shapes(own_rows, width):
    return [
        jax.ShapeDtypeStruct((own_rows + TILE, width), jnp.float32),
        jax.ShapeDtypeStruct((own_rows + TILE, LANES), jnp.float32),
    ]


def list_scratch(own_rows, slots):
    units = own_rows // TILE * (slots // 2) + GROUP
    return [
        pltpu.VMEM((2, TILE, LANES), jnp.bfloat16),
        pltpu.SMEM((units,), jnp.int32),
        pltpu.SMEM((2 * units + slots,), jnp.int32),
        pltpu.SMEM((units,), jnp.int32),
    ]


def own_attention(tables, rows, w, wq, scales, split, slots):
    own_rows, width = rows.shape
    tiles = own_rows // TILE
    shapes = [(tiles, width, TILE), (tiles, TILE, width), rows.shape, rows.shape]
    return pl.pallas_call(
        functools.partial(own_kernel, split),
        in_specs=[SMEM] * 3 + [VMEM] * 4,
        out_specs=[VMEM] * 6,
        out_shape=sums_shapes(own_rows, width)
        + [jax.ShapeDtypeStruct(shape, jnp.bfloat16) for shape in shapes],
        scratch_shapes=list_scratch(own_rows, slots),
        compiler_params=pltpu.CompilerParams(vmem_limit_bytes=24 * MIB),
        cost_estimate=pl.CostEstimate(flops=10**8, bytes_accessed=10**5, transcendentals=0),
    )(*tables, rows, w, wq, scales)


def more_attention(tables, pieces, w, local_q, num, den, own, split, slots):
    own_rows, width = local_q.shape
    tiles = sum(piece.shape[0] // TILE for piece in pieces) + (own_rows // TILE if own else 0)
    return pl.pallas_call(
        functools.partial(more_kernel, len(pieces), bool(own), split),
        in_specs=[SMEM] * 3 + [VMEM] * (len(pieces) + 4 + len(own)),
        out_specs=[VMEM] * 2,
        out_shape=sums_shapes(own_rows, width),
        scratch_shapes=list_scratch(own_rows, slots)
        + [
            pltpu.VMEM((tiles, width, TILE), jnp.bfloat16),
            pltpu.VMEM((tiles, TILE, width), jnp.bfloat16),
        ],
        compiler_params=pltpu.CompilerParams(vmem_limit_bytes=24 * MIB),
        cost_estimate=pl.CostEstimate(
            flops=10**12 if own else 10**8, bytes_accessed=10**5, transcendentals=0
        ),
    )(*tables, *pieces, w, local_q, num, den, *own)


def expand_kernel(count, gives_out, last, place_ref, rows_ref, spots_ref, *refs):
    sources = refs[:count]
    (expand_q, num_in, den_in, w) = refs[count : count + 4]
    refs = refs[count + 4 :]
    if last:
        (_, out_ref, features, num, den, row_list, tile_list, mark) = refs[:-3]
        (results, result_sems) = refs[-3:-1]
    else:
        if gives_out:
            (num, den, out_ref) = refs[:3]
        else:
            (num, den) = refs[:2]
        (features, row_list, tile_list, mark) = refs[-5:-1]
    chooser = refs[-1]
    own_rows, width = expand_q.shape
    tiles_here = own_rows // TILE
    matchings, edges = rows_ref.shape
    if gives_out:
        chooser[...] = denominator_chooser(width // LANES)
    for tile in range(tiles_here):
        mark[tile] = 0 if last else 1

    def visit(edge, found):
        for matching in range(matchings):
            row = rows_ref[matching, edge] - place_ref[0] * tiles_here
            spot = spots_ref[matching, edge]
            mine = jnp.logical_and(jnp.logical_and(row >= 0, row < tiles_here), spot >= 0)
            row_list[found] = row
            tile_list[found] = spot
            found = found + mine.astype(jnp.int32)
            if last:

                @pl.when(mine)
                def _():
                    mark[row] = 1

        return found

    found = lax.fori_loop(0, edges, visit, jnp.int32(0))
    for inner in range(GROUP):
        row_list[found + inner] = tiles_here
        tile_list[found + inner] = 0

    def each_marked(action):
        def visit_tile(tile, carry):
            target = pl.ds(pl.multiple_of(tile * TILE, TILE), TILE)
            pl.when(mark[tile] == 1)(lambda: action(tile, target))
            return carry

        lax.fori_loop(0, tiles_here, visit_tile, 0)

    def begin(tile, target):
        num[target, :] = num_in[target, :]
        den[target, :] = den_in[target, :]

    each_marked(begin)
    spare = pl.ds(own_rows, TILE)
    num[spare, :] = jnp.zeros((TILE, width), jnp.float32)
    den[spare, :] = jnp.zeros((TILE, LANES), jnp.float32)

    def group(first, size):
        for i in range(size):
            spot = tile_list[first + i]
            for source in sources:
                tiles = source.shape[0] // TILE

                @pl.when(jnp.logical_and(spot >= 0, spot < tiles))
                def _(source=source, spot=spot):
                    rows = pl.ds(pl.multiple_of(spot * TILE, TILE), TILE)
                    features[i * TILE : (i + 1) * TILE, :] = source[rows, :]

                spot = spot - tiles
        rows = [row_list[first + i] for i in range(size)]
        attend_units(expand_q, features[: size * TILE, :], w, num, den, rows)

    in_groups(found, group)

    def finish(tile, target):
        inverse = spread_reciprocals(den[target, :], chooser[...])
        result = (num[target, :] * inverse).astype(jnp.bfloat16)
        if last:
            results[target, :] = result
            copy_out(tile, target).start()
        else:
            out_ref[target, :] = result

    def copy_out(tile, target):
        return pltpu.make_async_copy(results.at[target], out_ref.at[target], result_sems.at[tile])

    if gives_out:
        each_marked(finish)
    if last:
        each_marked(lambda tile, target: copy_out(tile, target).wait())


def expand_attention(place, exp_rows, spots, sources, expand_q, num, den, w, gives_out, out):
    width = w.shape[2]
    own_rows = expand_q.shape[0]
    last = out is not None
    most = exp_rows.shape[0] * exp_rows.shape[1] + GROUP
    sums = sums_shapes(own_rows, width)
    result = jax.ShapeDtypeStruct((own_rows, width), jnp.bfloat16)
    sums_scratch = [pltpu.VMEM(array.shape, array.dtype) for array in sums]
    arguments = [place, exp_rows, spots, *sources, expand_q, num, den, w]
    return pl.pallas_call(
        functools.partial(expand_kernel, len(sources), gives_out, last),
        in_specs=[SMEM] * 3 + [VMEM] * (len(sources) + 4) + [ANY] * last,
        out_specs=ANY if last else [VMEM] * (2 + gives_out),
        out_shape=result if last else sums + [result] * gives_out,
        input_output_aliases={len(arguments): 0} if last else {},
        scratch_shapes=[
            pltpu.VMEM((GROUP * TILE, width), jnp.bfloat16),
        ]
        + (sums_scratch if last else [])
        + [
            pltpu.SMEM((most,), jnp.int32),
            pltpu.SMEM((most,), jnp.int32),
            pltpu.SMEM((own_rows // TILE,), jnp.int32),
        ]
        + (
            [
                pltpu.VMEM((own_rows, width), jnp.bfloat16),
                pltpu.SemaphoreType.DMA((own_rows // TILE,)),
            ]
            if last
            else []
        )
        + [pltpu.VMEM((2 * LANES, width), jnp.bfloat16)],
        compiler_params=pltpu.CompilerParams(vmem_limit_bytes=24 * MIB),
        cost_estimate=pl.CostEstimate(
            flops=own_rows * width * 256, bytes_accessed=own_rows * width, transcendentals=0
        ),
    )(*arguments, *([out] if last else []))


def cut_half_kernel(here_ref, features, half_ref, buffer, sem):
    rows = half_ref.shape[0]
    start = pl.multiple_of(here_ref[0] * rows, TILE)
    inward = pltpu.make_async_copy(features.at[pl.ds(start, rows)], buffer, sem)
    inward.start()
    inward.wait()
    outward = pltpu.make_async_copy(buffer, half_ref, sem)
    outward.start()
    outward.wait()


def cut_half(here, features):
    half = (features.shape[0] // 2, features.shape[1])
    return pl.pallas_call(
        cut_half_kernel,
        in_specs=[SMEM, ANY],
        out_specs=ANY,
        out_shape=jax.ShapeDtypeStruct(half, jnp.bfloat16),
        scratch_shapes=[pltpu.VMEM(half, jnp.bfloat16), pltpu.SemaphoreType.DMA],
        compiler_params=pltpu.CompilerParams(vmem_limit_bytes=60 * MIB),
    )(here, features)


def cut_rest_kernel(here_ref, features, half_ref, edge_ref, sems):
    here = here_ref[0]
    half, margin = half_ref.shape[0], edge_ref.shape[0]
    copies = []
    for index, (start, target) in enumerate(
        [((1 - here) * half, half_ref), (here * (2 * half - margin), edge_ref)]
    ):
        rows = pl.ds(pl.multiple_of(start, TILE), target.shape[0])
        copies.append(pltpu.make_async_copy(features.at[rows], target, sems.at[index]))
    for copy in copies:
        copy.start()
    for copy in copies:
        copy.wait()


def cut_rest(here, features, margin):
    rows, width = features.shape
    return pl.pallas_call(
        cut_rest_kernel,
        in_specs=[SMEM, ANY],
        out_specs=[VMEM] * 2,
        out_shape=[
            jax.ShapeDtypeStruct((rows // 2, width), jnp.bfloat16),
            jax.ShapeDtypeStruct((margin, width), jnp.bfloat16),
        ],
        scratch_shapes=[pltpu.SemaphoreType.DMA((2,))],
        compiler_params=pltpu.CompilerParams(vmem_limit_bytes=8 * MIB),
        cost_estimate=pl.CostEstimate(flops=10**11, bytes_accessed=4096, transcendentals=0),
    )(here, features)


def select_kernel(jobs, share, sources, margin, place_ref, *refs):
    matchings = len(refs) - sources - len(jobs) - (margin > 0)
    wanted = refs[:matchings]
    parts = refs[matchings : matchings + sources]
    outs = refs[matchings + sources :]
    here = place_ref[0]
    even = lax.rem(place_ref[1], 2) == 0
    quarter = parts[1].shape[0] // TILE
    if margin:
        start = pl.multiple_of((1 - here) * (quarter * TILE - margin), TILE)
        outs[-1][...] = parts[1][pl.ds(start, margin), :]
    per_part = 2 * quarter
    flat = []
    for (of_even, of_odd, lines), out in zip(jobs, outs):
        at = 0
        for line in lines:
            start = (here if line == 0 else 1 - here) * share
            for slot in range(share):
                tile = wanted[of_even][0, start + slot]
                if of_odd != of_even:
                    tile = jnp.where(even, tile, wanted[of_odd][0, start + slot])
                flat.append((tile, out, at))
                at += 1
    for tile, out, slot in flat:
        own = tile // per_part == here
        place = tile // quarter
        end = jnp.logical_or(place == 0, place == 3)
        target = slice(slot * TILE, (slot + 1) * TILE)

        @pl.when(own)
        def _():
            start = pl.multiple_of(lax.rem(tile, per_part) * TILE, TILE)
            out[target, :] = parts[0][pl.ds(start, TILE), :]

        start = pl.multiple_of(lax.rem(tile, quarter) * TILE, TILE)

        @pl.when(jnp.logical_and(jnp.logical_not(own), end))
        def _():
            out[target, :] = parts[1][pl.ds(start, TILE), :]

        if sources > 2:

            @pl.when(jnp.logical_not(jnp.logical_or(own, end)))
            def _():
                out[target, :] = parts[2][pl.ds(start, TILE), :]


def select(place, jobs, share, wanted, parts, margin=0):
    width = parts[0].shape[1]
    sizes = [share * len(lines) * TILE for _, _, lines in jobs]
    sizes += [margin] * (margin > 0)
    return pl.pallas_call(
        functools.partial(select_kernel, jobs, share, len(parts), margin),
        in_specs=[SMEM] * (1 + len(wanted)) + [VMEM] * len(parts),
        out_specs=[VMEM] * len(sizes),
        out_shape=[jax.ShapeDtypeStruct((size, width), jnp.bfloat16) for size in sizes],
        compiler_params=pltpu.CompilerParams(vmem_limit_bytes=16 * MIB),
        cost_estimate=pl.CostEstimate(flops=1000, bytes_accessed=1000, transcendentals=0),
    )(place, *wanted, *parts)


def rank_tiles(tiles, edges, column_of, mark, on_tile):
    every = range(mark.shape[0])
    quarter = tiles // 4
    for tile in range(tiles):
        for matching in every:
            mark[matching, tile] = 0
    missing = [jnp.int32(edges)] * len(every)
    for edge in range(edges):
        for matching in every:
            tile = column_of(matching, edge)
            missing[matching] = missing[matching] - (1 - mark[matching, tile])
            mark[matching, tile] = 1
    rank = [jnp.int32(0)] * len(every)
    for at in range(tiles):
        tile = at + (quarter if at // quarter % 2 == 0 else -quarter)
        for matching in every:
            present = mark[matching, tile]
            added = jnp.where(jnp.logical_and(present == 0, missing[matching] > 0), 1, 0)
            on_tile(matching, tile, rank[matching])
            rank[matching] = rank[matching] + present + added
            missing[matching] = missing[matching] - added


def spots_kernel(tiles, lines, blocks, here_ref, block_ref, cols_ref, *refs):
    (place_ref, own_ref, near_table, rest_table) = refs[:4]
    spots_refs = refs[4:7]
    wanted_refs = refs[7:-2]
    mark, rank_of = refs[-2:]
    matchings, edges = cols_ref.shape
    share = edges // lines
    here, block = here_ref[0], block_ref[0]
    odd = lax.rem(block, 2)
    place_ref[0] = here
    place_ref[1] = block
    per_part = tiles // lines
    quarter = per_part // 2
    for index in range(tiles + 2 * HT):
        column = index - HT
        if 0 <= column < tiles:
            own = here == column // per_part
            own_place = jnp.where(own, column % per_part, -1)
            within = column % quarter
            end = column // quarter in (0, 3)
            near = jnp.where(own, -1, per_part + within if end else -1)
            rest = jnp.where(own, -1, -1 if end else within)
        else:
            after = column >= tiles
            own_place = near = jnp.int32(-1)
            ours = here == (0 if after else 1)
            rest = (column - tiles if after else column + HT) + jnp.where(ours, quarter + HT, quarter)
            rest = jnp.where(block < blocks - 1 if after else block > 0, rest, -1)
        own_ref[0, index] = own_place
        own_ref[1, index] = -1
        near_table[0, index] = near
        near_table[1, index] = jnp.maximum(near, own_place)
        rest_table[0, index] = rest
        rest_table[1, index] = rest

    def on_tile(matching, tile, slot):
        rank_of[matching, tile] = slot
        wanted_refs[matching][0, slot] = tile

    rank_tiles(tiles, edges, lambda matching, edge: cols_ref[matching, edge], mark, on_tile)
    for edge in range(edges):
        for matching in range(matchings):
            slot = rank_of[matching, cols_ref[matching, edge]]
            away = jnp.where(slot // share == here, 0, 1)
            within = lax.rem(slot, share)
            if matching == 0:
                when, spot = 0, away * share + within
            elif matching == 1:
                when, spot = away, within + jnp.where(away == 0, 3 * share, 0)
            else:
                second = odd if matching == matchings - 1 else 1 - odd
                when = jnp.where(away == 0, second, 1 + second)
                spot = within + share * jnp.where(second == 0, 2, jnp.where(away == 0, 1, odd))
            for index, spots_ref in enumerate(spots_refs):
                spots_ref[matching, edge] = jnp.where(when == index, spot, -1)


def arrival_spots(here, block, blocks, cols, tiles, lines):
    wanted = jax.ShapeDtypeStruct((1, 2 * cols.shape[1]), jnp.int32)
    spots = jax.ShapeDtypeStruct(cols.shape, jnp.int32)
    table = jax.ShapeDtypeStruct((2, tiles + 2 * HT), jnp.int32)
    place = jax.ShapeDtypeStruct((2,), jnp.int32)
    place, *rest = pl.pallas_call(
        functools.partial(spots_kernel, tiles, lines, blocks),
        in_specs=[SMEM] * 3,
        out_specs=[SMEM] * (7 + cols.shape[0]),
        out_shape=[place] + [table] * 3 + [spots] * 3 + [wanted] * cols.shape[0],
        scratch_shapes=[pltpu.SMEM((cols.shape[0], tiles), jnp.int32)] * 2,
        compiler_params=pltpu.CompilerParams(vmem_limit_bytes=8 * MIB),
        cost_estimate=pl.CostEstimate(flops=10**11, bytes_accessed=4096, transcendentals=0),
    )(here, block, cols)
    return place, rest[:3], rest[3:6], rest[6:]


def local(features, w_query, w_key_value, edge_local, edge_expand, local_cols, exp_rows, exp_cols):
    groups = lax.axis_size("head")
    blocks = lax.axis_size("node")
    own_rows, width = features.shape
    here = lax.axis_index("head")
    block = lax.axis_index("node")
    edges = exp_cols.shape[2]
    tiles = local_cols.shape[0]
    own_tiles = own_rows // TILE
    margin = HT * TILE
    exp_rows, exp_cols = exp_rows[0], exp_cols[0]
    log_count = blocks.bit_length() - 1
    flips = [1 << matching * log_count // MATCH for matching in range(MATCH)]

    def swap(x, matching, of_odd=None):
        flip = [flips[matching], flips[matching if of_odd is None else of_odd]]
        return lax.ppermute(x, "node", [(i, i ^ flip[i % 2]) for i in range(blocks)])

    def other(x):
        return lax.ppermute(x, "head", [(0, 1), (1, 0)])

    scales = jnp.stack([edge_local, edge_expand])
    listed = local_cols.shape[1]
    split = own_tiles
    two = groups == 2 and min(flips[2:]) > 1

    if two:
        split = own_tiles // 4
        here_array = jnp.reshape(here, (1,)).astype(jnp.int32)
        block_array = jnp.reshape(block, (1,)).astype(jnp.int32)
        first_half = cut_half(here_array, features)
        beside = other(scales)
        first_half, features, exp_cols, local_cols, beside, w_query, w_key_value = (
            lax.optimization_barrier(
                (first_half, features, exp_cols, local_cols, beside, w_query, w_key_value)
            )
        )
        local_cols = local_cols.reshape(-1)
        w = jnp.transpose(w_key_value, (1, 0, 2))
        first_half = other(first_half)
        second_half, edge_rows = cut_rest(here_array, features, margin)
        place, tables, spots, wanted = arrival_spots(
            here_array, block_array, blocks, exp_cols, tiles, groups
        )
        edge_rows, *wanted = lax.optimization_barrier((edge_rows, *wanted))
        wanted_pair, *wanted = wanted
        wanted = [swap(wanted[m - 1], m) for m in range(1, MATCH)]
        inward = [(2 * i, 2 * i - 2) for i in range(1, blocks)]
        inward += [(2 * i + 1, 2 * i + 3) for i in range(blocks - 1)]
        halo = lax.ppermute(edge_rows, ("node", "head"), inward)
        scales = jnp.where(
            here == 0,
            jnp.concatenate([scales, beside], axis=1),
            jnp.concatenate([beside, scales], axis=1),
        )
        scales, w, local_cols, halo, *wanted = lax.optimization_barrier(
            (scales, w, local_cols, halo, *wanted)
        )
        num, den, keys, values, local_q, expand_q = own_attention(
            (place, local_cols, tables[0]), features, w, w_query, scales, split, listed
        )
        first_half, second_half, num = lax.optimization_barrier((first_half, second_half, num))
        second_half = other(second_half)
        share = edges // groups
        sources = [features, first_half]
        jobs = ((2, 1, (0,)), (1, 2, (0,)), (0, 0, (0,)))
        *chosen, edge_rows = select(place, jobs, share, wanted, sources, margin)
        num, *chosen = lax.optimization_barrier((num, *chosen))
        first = swap(chosen[0], 3, 2)
        early = swap(chosen[2], 1)
        num, den = more_attention(
            (place, local_cols, tables[1]),
            [first_half],
            w,
            local_q,
            num,
            den,
            (keys, values),
            split,
            listed,
        )
        second_half, num, den, edge_rows, wanted_pair, second = lax.optimization_barrier(
            (second_half, num, den, edge_rows, wanted_pair, chosen[1])
        )
        outward = [(2 * i, 2 * i + 2) for i in range(blocks - 1)]
        outward += [(2 * i + 1, 2 * i - 1) for i in range(1, blocks)]
        other_halo = lax.ppermute(edge_rows, ("node", "head"), outward)
        wanted_pair = swap(wanted_pair, 0)
        sources = [features, first_half, second_half]
        late, direct = select(place, ((0, 0, (1,)), (1, 1, (1,))), share, wanted, sources)
        num, first, early, late = lax.optimization_barrier((num, first, early, late))
        second = swap(second, 2, 3)
        first_beside = other(first)
        late = swap(late, 1)
        (pair,) = select(place, ((0, 0, (0, 1)),), share, [wanted_pair], sources)
        num, pair, other_halo = lax.optimization_barrier((num, pair, other_halo))
        pair = swap(pair, 0)
        num, den = more_attention(
            (place, local_cols, tables[2]),
            [second_half, other_halo, halo],
            w,
            local_q,
            num,
            den,
            (),
            split,
            listed,
        )
        num, den = expand_attention(
            place, exp_rows, spots[0], [pair, first, early], expand_q, num, den, w, False, None
        )
        second, direct, num, den = lax.optimization_barrier((second, direct, num, den))
        direct = lax.ppermute(direct, "node", [(i, i ^ flips[2]) for i in range(0, blocks, 2)])
        sides = [(4 * i + 2 + side, 4 * i + 3 - side) for i in range(blocks // 2) for side in (0, 1)]
        second_beside = lax.ppermute(second, ("node", "head"), sides)
        sources = [None, [late, second, first_beside], [direct, second_beside]]
    else:
        place = jnp.stack([here, block]).astype(jnp.int32)
        column = jnp.arange(tiles + 2 * HT, dtype=jnp.int32) - HT
        usable = block * tiles + column
        usable = jnp.logical_and(usable >= 0, usable < blocks * tiles)
        own = column // own_tiles == here
        w = jnp.transpose(w_key_value, (1, 0, 2))
        gather = lambda x: lax.all_gather(x, "head", axis=0, tiled=True)
        scales = lax.all_gather(scales, "head", axis=1, tiled=True)
        full = gather(features)
        before = lax.ppermute(full[-margin:], "node", [(i, i + 1) for i in range(blocks - 1)])
        after = lax.ppermute(full[:margin], "node", [(i + 1, i) for i in range(blocks - 1)])
        received = [gather(swap(features, m)) for m in range(MATCH)]
        sources = [None, received[:2], received[2:]]
        matching = jnp.arange(MATCH, dtype=jnp.int32)[:, None]
        spots = [
            None,
            jnp.where(matching < 2, matching * tiles + exp_cols, -1),
            jnp.where(matching < 2, -1, (matching - 2) * tiles + exp_cols),
        ]
        where_own = jnp.where(own, column - here * own_tiles, -1)
        where_rest = jnp.where(jnp.logical_and(usable, jnp.logical_not(own)), column + HT, -1)
        local_cols = local_cols.reshape(-1)
        num, den, keys, values, local_q, expand_q = own_attention(
            (place, local_cols, jnp.stack([where_own] * 2)),
            features,
            w,
            w_query,
            scales,
            split,
            listed,
        )
        num, den = more_attention(
            (place, local_cols, jnp.stack([where_rest] * 2)),
            [before, full, after],
            w,
            local_q,
            num,
            den,
            (),
            split,
            listed,
        )
    num, den, out = expand_attention(
        place, exp_rows, spots[1], sources[1], expand_q, num, den, w, True, None
    )
    return expand_attention(
        place, exp_rows, spots[2], sources[2], expand_q, num, den, w, True, out
    )


def solution(mesh):
    return jax.shard_map(
        local,
        mesh=mesh,
        in_specs=(
            P(("node", "head"), None),
            P(),
            P(),
            P("head"),
            P("head"),
            P("node", None),
            P("node", None, None),
            P("node", None, None),
        ),
        out_specs=P(("node", "head"), None),
        check_vma=False,
    )
```

```python
import functools
import math

import jax
import jax.numpy as jnp
from jax import lax
from jax.experimental import pallas as pl
from jax.experimental.pallas import tpu as pltpu
from jax.sharding import PartitionSpec as P

HEADS = 8
TILE = 128
HT = 2
MATCH = 4
LANES = 128
GROUP = 4
MIB = 1024 * 1024

ANY = pl.BlockSpec(memory_space=pl.ANY)
SMEM = pl.BlockSpec(memory_space=pltpu.SMEM)
VMEM = pl.BlockSpec(memory_space=pltpu.VMEM)
HBM = pl.BlockSpec(memory_space=pltpu.HBM)


def lane_masks():
    lane = lax.broadcasted_iota(jnp.int32, (TILE, LANES), 1)
    return lane < LANES // 2, lane % (LANES // 2)


def pack_denominators(pieces):
    _, within = lane_masks()
    size = LANES // 2 // len(pieces)
    packed = pieces[-1]
    for pair in range(len(pieces) - 2, -1, -1):
        packed = jnp.where(within < (pair + 1) * size, pieces[pair], packed)
    return packed


def denominator_chooser(pairs):
    size = LANES // 2 // pairs
    shape = (2 * LANES, pairs * LANES)
    source = lax.broadcasted_iota(jnp.int32, shape, 0) % LANES
    target = lax.broadcasted_iota(jnp.int32, shape, 1)
    wanted = target // LANES * size + (target % LANES) // (LANES // 2) * (LANES // 2)
    return jnp.where(source == wanted, 1.0, 0.0).astype(jnp.bfloat16)


def spread_reciprocals(packed, chooser):
    inverse = 1.0 / packed
    coarse = inverse.astype(jnp.bfloat16)
    fine = (inverse - coarse.astype(jnp.float32)).astype(jnp.bfloat16)
    return jnp.dot(
        jnp.concatenate([coarse, fine], axis=1), chooser, preferred_element_type=jnp.float32
    )


def project(rows, w, keys, values, first):
    new_keys = jnp.dot(rows, w[0], preferred_element_type=jnp.float32).astype(jnp.bfloat16).T
    new_values = jnp.dot(rows, w[1], preferred_element_type=jnp.float32).astype(jnp.bfloat16)
    for index in range(rows.shape[0] // TILE):
        span = slice(index * TILE, (index + 1) * TILE)
        keys[first + index] = new_keys[:, span]
        values[first + index] = new_values[span, :]


def attend_chunks(queries, keys, values, ones, num, den, units):
    low, _ = lane_masks()
    low_mask = jnp.where(low, 1.0, 0.0).astype(jnp.bfloat16)
    high_mask = jnp.where(low, 0.0, 1.0).astype(jnp.bfloat16)
    rows = [pl.ds(pl.multiple_of(unit[0] * TILE, TILE), TILE) for unit in units]
    last = queries.shape[0] // TILE - 1
    query_rows = [
        pl.ds(pl.multiple_of(jnp.minimum(unit[0], last) * TILE, TILE), TILE) for unit in units
    ]
    denominators = [[] for _ in units]
    for pair in range(queries.shape[1] // LANES):
        part = slice(pair * LANES, (pair + 1) * LANES)
        weights = []
        for row, (_, one, two, _) in zip(query_rows, units):
            some = queries[row, part]
            scores = jnp.dot(
                jnp.concatenate([some * low_mask, some * high_mask], axis=0),
                jnp.concatenate([keys[one, part, :], keys[two, part, :]], axis=1),
                preferred_element_type=jnp.float32,
            )
            weights.append(jnp.exp(jnp.clip(scores, -5.0, 5.0)).astype(jnp.bfloat16))
        sums = []
        for weight, (_, one, two, fills) in zip(weights, units):
            counts = ones[fills]
            wide = [
                jnp.concatenate([values[one, :, part], ones[0]], axis=1),
                jnp.concatenate([values[two, :, part] * counts, counts], axis=1),
            ]
            sums.append(
                jnp.dot(
                    weight, jnp.concatenate(wide, axis=0), preferred_element_type=jnp.float32
                )
            )
        for row, both, listed in zip(rows, sums, denominators):
            num[row, part] += jnp.where(low, both[:TILE, :LANES], both[TILE:, :LANES])
            listed.append(jnp.where(low, both[:TILE, LANES:], both[TILE:, LANES:]))
    for row, listed in zip(rows, denominators):
        den[row, :] += pack_denominators(listed)


def attend_units(queries, rows_here, w, num, den, rows):
    keys = jnp.dot(rows_here, w[0], preferred_element_type=jnp.float32).astype(jnp.bfloat16)
    values = jnp.dot(rows_here, w[1], preferred_element_type=jnp.float32).astype(jnp.bfloat16)
    low_lanes, _ = lane_masks()
    low = jnp.where(low_lanes, 1.0, 0.0).astype(jnp.bfloat16)
    high = jnp.where(low_lanes, 0.0, 1.0).astype(jnp.bfloat16)
    last = queries.shape[0] // TILE - 1
    query_rows = [
        pl.ds(pl.multiple_of(jnp.minimum(row, last) * TILE, TILE), TILE) for row in rows
    ]
    rows = [pl.ds(pl.multiple_of(row * TILE, TILE), TILE) for row in rows]
    spans = [slice(index * TILE, (index + 1) * TILE) for index in range(len(rows))]
    denominators = [[] for _ in rows]
    for pair in range(queries.shape[1] // LANES):
        part = slice(pair * LANES, (pair + 1) * LANES)
        weights = []
        for row, span in zip(query_rows, spans):
            key = keys[span, part]
            scores = lax.dot_general(
                queries[row, part],
                jnp.concatenate([key * low, key * high], axis=0),
                (((1,), (1,)), ((), ())),
                preferred_element_type=jnp.float32,
            )
            weights.append(jnp.exp(jnp.clip(scores, -5.0, 5.0)).astype(jnp.bfloat16))
        sums = []
        for weight, span in zip(weights, spans):
            value = values[span, part]
            wide = jnp.concatenate(
                [
                    jnp.concatenate([value * low, low], axis=1),
                    jnp.concatenate([value * high, high], axis=1),
                ],
                axis=0,
            )
            sums.append(jnp.dot(weight, wide, preferred_element_type=jnp.float32))
        for row, both, listed in zip(rows, sums, denominators):
            num[row, part] += both[:, :LANES]
            listed.append(both[:, LANES:])
    for row, listed in zip(rows, denominators):
        den[row, :] += pack_denominators(listed)


def project_pieces(pieces, w, keys, values, at):
    for piece in pieces:
        tiles = piece.shape[0] // TILE
        size = math.gcd(tiles, GROUP)

        def some_tiles(index, carry, piece=piece, at=at, size=size):
            some = piece[pl.ds(pl.multiple_of(index * size * TILE, TILE), size * TILE), :]
            project(some, w, keys, values, at + index * size)
            return carry

        lax.fori_loop(0, tiles // size, some_tiles, 0)
        at += tiles


def attend_listed(
    steps, split, place_ref, cols_ref, where_ref, queries, keys, values, num, den, scratch
):
    ones, row_list, tile_list, fill_list = scratch
    tiles_here = queries.shape[0] // TILE
    slots = tile_list.shape[0] - 2 * row_list.shape[0]
    ones[0] = jnp.ones(ones.shape[1:], ones.dtype)
    ones[1] = jnp.zeros(ones.shape[1:], ones.dtype)

    def visit(row, found):
        part = jnp.where(row < split, 0, 1)
        at = 2 * found
        for slot in range(slots):
            tile = where_ref[part, cols_ref[(place_ref[0] * tiles_here + row) * slots + slot]]
            tile_list[at] = tile
            at = at + (tile >= 0).astype(jnp.int32)
        tile_list[at] = 0
        units = (at - 2 * found + 1) // 2
        odd = lax.rem(at, 2)
        for unit in range(slots // 2):
            row_list[found + unit] = row
            fill_list[found + unit] = jnp.where(unit == units - 1, odd, 0)
        return found + units

    found = lax.fori_loop(0, steps, visit, jnp.int32(0))
    for inner in range(GROUP):
        row_list[found + inner] = tiles_here
        fill_list[found + inner] = 0
        tile_list[2 * (found + inner)] = 0
        tile_list[2 * (found + inner) + 1] = 0

    def group(first, size):
        units = []
        for inner in range(size):
            unit = first + inner
            units.append(
                (row_list[unit], tile_list[2 * unit], tile_list[2 * unit + 1], fill_list[unit])
            )
        attend_chunks(queries, keys, values, ones, num, den, units)

    in_groups(found, group)


def in_groups(found, group):
    whole = found // GROUP

    def visit(index, carry):
        group(index * GROUP, GROUP)
        return carry

    lax.fori_loop(0, whole, visit, 0)
    left = found - whole * GROUP
    half = GROUP // 2
    pl.when(left > half)(lambda: group(whole * GROUP, GROUP))
    pl.when(jnp.logical_and(left > 0, left <= half))(lambda: group(whole * GROUP, half))


def each_tile(tiles, action):
    def visit(tile, carry):
        action(pl.ds(pl.multiple_of(tile * TILE, TILE), TILE))
        return carry

    lax.fori_loop(0, tiles, visit, 0)


def own_kernel(split, place_ref, cols_ref, where_ref, rows, w, wq, scales, *refs):
    (num, den, keys, values, local_ref, expand_ref) = refs[:6]
    width = rows.shape[1]
    tiles = rows.shape[0] // TILE
    size = min(GROUP, tiles)
    project_pieces([rows], w, keys, values, 0)

    def some_queries(index, carry):
        target = pl.ds(pl.multiple_of(index * size * TILE, TILE), size * TILE)
        queries = jnp.dot(rows[target, :], wq[...], preferred_element_type=jnp.float32)
        queries = queries.astype(jnp.bfloat16).astype(jnp.float32)
        scale = 1.0 / math.sqrt(width // HEADS)
        local_ref[target, :] = (queries * scales[0:1, :] * scale).astype(jnp.bfloat16)
        expand_ref[target, :] = (queries * scales[1:2, :] * scale).astype(jnp.bfloat16)
        return carry

    lax.fori_loop(0, tiles // size, some_queries, 0)

    def clear(target):
        num[target, :] = jnp.zeros((TILE, width), jnp.float32)
        den[target, :] = jnp.zeros((TILE, LANES), jnp.float32)

    each_tile(tiles + 1, clear)
    attend_listed(
        split, split, place_ref, cols_ref, where_ref, local_ref, keys, values, num, den, refs[6:]
    )


def more_kernel(count, from_own, split, place_ref, cols_ref, where_ref, *refs):
    pieces = refs[:count]
    (w, local_ref, num_in, den_in) = refs[count : count + 4]
    refs = refs[count + 4 :]
    if from_own:
        (own_keys, own_values, num, den, *scratch, keys, values) = refs
        first = own_keys.shape[0]

        def bring(tile, carry):
            keys[tile] = own_keys[tile]
            values[tile] = own_values[tile]
            return carry

        lax.fori_loop(0, first, bring, 0)
    else:
        (num, den, *scratch, keys, values) = refs
        first = 0
    project_pieces(pieces, w, keys, values, first)

    def begin(target):
        num[target, :] = num_in[target, :]
        den[target, :] = den_in[target, :]

    tiles = local_ref.shape[0] // TILE
    each_tile(tiles + 1, begin)
    attend_listed(
        tiles, split, place_ref, cols_ref, where_ref, local_ref, keys, values, num, den, scratch
    )


def sums_shapes(own_rows, width):
    return [
        jax.ShapeDtypeStruct((own_rows + TILE, width), jnp.float32),
        jax.ShapeDtypeStruct((own_rows + TILE, LANES), jnp.float32),
    ]


def list_scratch(own_rows, slots):
    units = own_rows // TILE * (slots // 2) + GROUP
    return [
        pltpu.VMEM((2, TILE, LANES), jnp.bfloat16),
        pltpu.SMEM((units,), jnp.int32),
        pltpu.SMEM((2 * units + slots,), jnp.int32),
        pltpu.SMEM((units,), jnp.int32),
    ]


def own_attention(tables, rows, w, wq, scales, split, slots):
    own_rows, width = rows.shape
    tiles = own_rows // TILE
    shapes = [(tiles, width, TILE), (tiles, TILE, width), rows.shape, rows.shape]
    return pl.pallas_call(
        functools.partial(own_kernel, split),
        in_specs=[SMEM] * 3 + [VMEM] * 4,
        out_specs=[VMEM] * 6,
        out_shape=sums_shapes(own_rows, width)
        + [jax.ShapeDtypeStruct(shape, jnp.bfloat16) for shape in shapes],
        scratch_shapes=list_scratch(own_rows, slots),
        compiler_params=pltpu.CompilerParams(vmem_limit_bytes=24 * MIB),
        cost_estimate=pl.CostEstimate(flops=10**8, bytes_accessed=10**5, transcendentals=0),
    )(*tables, rows, w, wq, scales)


def more_attention(tables, pieces, w, local_q, num, den, own, split, slots):
    own_rows, width = local_q.shape
    tiles = sum(piece.shape[0] // TILE for piece in pieces) + (own_rows // TILE if own else 0)
    return pl.pallas_call(
        functools.partial(more_kernel, len(pieces), bool(own), split),
        in_specs=[SMEM] * 3 + [VMEM] * (len(pieces) + 4 + len(own)),
        out_specs=[VMEM] * 2,
        out_shape=sums_shapes(own_rows, width),
        scratch_shapes=list_scratch(own_rows, slots)
        + [
            pltpu.VMEM((tiles, width, TILE), jnp.bfloat16),
            pltpu.VMEM((tiles, TILE, width), jnp.bfloat16),
        ],
        compiler_params=pltpu.CompilerParams(vmem_limit_bytes=24 * MIB),
        cost_estimate=pl.CostEstimate(
            flops=10**12, bytes_accessed=10**5, transcendentals=0
        ),
    )(*tables, *pieces, w, local_q, num, den, *own)


def expand_kernel(count, gives_out, last, place_ref, rows_ref, spots_ref, *refs):
    sources = refs[:count]
    (expand_q, num_in, den_in, w) = refs[count : count + 4]
    refs = refs[count + 4 :]
    if last:
        (_, out_ref, features, num, den, row_list, tile_list, mark) = refs[:-3]
        (results, result_sems) = refs[-3:-1]
    else:
        if gives_out:
            (num, den, out_ref) = refs[:3]
        else:
            (num, den) = refs[:2]
        (features, row_list, tile_list, mark) = refs[-5:-1]
    chooser = refs[-1]
    own_rows, width = expand_q.shape
    tiles_here = own_rows // TILE
    matchings, edges = rows_ref.shape
    if gives_out:
        chooser[...] = denominator_chooser(width // LANES)
    for tile in range(tiles_here):
        mark[tile] = 0 if last else 1

    def visit(edge, found):
        for matching in range(matchings):
            row = rows_ref[matching, edge] - place_ref[0] * tiles_here
            spot = spots_ref[matching, edge]
            mine = jnp.logical_and(jnp.logical_and(row >= 0, row < tiles_here), spot >= 0)
            row_list[found] = row
            tile_list[found] = spot
            found = found + mine.astype(jnp.int32)
            if last:

                @pl.when(mine)
                def _():
                    mark[row] = 1

        return found

    found = lax.fori_loop(0, edges, visit, jnp.int32(0))
    for inner in range(GROUP):
        row_list[found + inner] = tiles_here
        tile_list[found + inner] = 0

    def each_marked(action):
        def visit_tile(tile, carry):
            target = pl.ds(pl.multiple_of(tile * TILE, TILE), TILE)
            pl.when(mark[tile] == 1)(lambda: action(tile, target))
            return carry

        lax.fori_loop(0, tiles_here, visit_tile, 0)

    def begin(tile, target):
        num[target, :] = num_in[target, :]
        den[target, :] = den_in[target, :]

    each_marked(begin)
    spare = pl.ds(own_rows, TILE)
    num[spare, :] = jnp.zeros((TILE, width), jnp.float32)
    den[spare, :] = jnp.zeros((TILE, LANES), jnp.float32)

    def group(first, size):
        for i in range(size):
            spot = tile_list[first + i]
            for source in sources:
                tiles = source.shape[0] // TILE

                @pl.when(jnp.logical_and(spot >= 0, spot < tiles))
                def _(source=source, spot=spot):
                    rows = pl.ds(pl.multiple_of(spot * TILE, TILE), TILE)
                    features[i * TILE : (i + 1) * TILE, :] = source[rows, :]

                spot = spot - tiles
        rows = [row_list[first + i] for i in range(size)]
        attend_units(expand_q, features[: size * TILE, :], w, num, den, rows)

    in_groups(found, group)

    def outputs(target):
        inverse = spread_reciprocals(den[target, :], chooser[...])
        return (num[target, :] * inverse).astype(jnp.bfloat16)

    def finish(tile, target):
        results[target, :] = outputs(target)
        copy_out(tile, target).start()

    def finish_some(index, carry):
        size = math.gcd(GROUP, tiles_here) * TILE
        target = pl.ds(pl.multiple_of(index * size, TILE), size)
        out_ref[target, :] = outputs(target)
        return carry

    def copy_out(tile, target):
        return pltpu.make_async_copy(results.at[target], out_ref.at[target], result_sems.at[tile])

    if last:
        each_marked(finish)
    elif gives_out:
        lax.fori_loop(0, tiles_here // math.gcd(GROUP, tiles_here), finish_some, 0)
    if last:
        each_marked(lambda tile, target: copy_out(tile, target).wait())


def expand_attention(place, exp_rows, spots, sources, expand_q, num, den, w, gives_out, out):
    width = w.shape[2]
    own_rows = expand_q.shape[0]
    last = out is not None
    most = exp_rows.shape[0] * exp_rows.shape[1] + GROUP
    sums = sums_shapes(own_rows, width)
    result = jax.ShapeDtypeStruct((own_rows, width), jnp.bfloat16)
    sums_scratch = [pltpu.VMEM(array.shape, array.dtype) for array in sums]
    arguments = [place, exp_rows, spots, *sources, expand_q, num, den, w]
    return pl.pallas_call(
        functools.partial(expand_kernel, len(sources), gives_out, last),
        in_specs=[SMEM] * 3 + [VMEM] * (len(sources) + 4) + [ANY] * last,
        out_specs=ANY if last else [VMEM] * (2 + gives_out),
        out_shape=result if last else sums + [result] * gives_out,
        input_output_aliases={len(arguments): 0} if last else {},
        scratch_shapes=[
            pltpu.VMEM((GROUP * TILE, width), jnp.bfloat16),
        ]
        + (sums_scratch if last else [])
        + [
            pltpu.SMEM((most,), jnp.int32),
            pltpu.SMEM((most,), jnp.int32),
            pltpu.SMEM((own_rows // TILE,), jnp.int32),
        ]
        + (
            [
                pltpu.VMEM((own_rows, width), jnp.bfloat16),
                pltpu.SemaphoreType.DMA((own_rows // TILE,)),
            ]
            if last
            else []
        )
        + [pltpu.VMEM((2 * LANES, width), jnp.bfloat16)],
        compiler_params=pltpu.CompilerParams(vmem_limit_bytes=24 * MIB),
        cost_estimate=pl.CostEstimate(
            flops=10**8 if gives_out else 10**12, bytes_accessed=own_rows * width, transcendentals=0
        ),
    )(*arguments, *([out] if last else []))


def cut_half_kernel(here_ref, features, half_ref, buffer, sems):
    rows = half_ref.shape[0]
    start = here_ref[0] * rows
    pieces = sems.shape[1]
    size = rows // pieces
    inward, outward = [], []
    for index in range(pieces):
        source = pl.ds(pl.multiple_of(start + index * size, TILE), size)
        target = pl.ds(index * size, size)
        inward.append(
            pltpu.make_async_copy(features.at[source], buffer.at[target], sems.at[0, index])
        )
        outward.append(
            pltpu.make_async_copy(buffer.at[target], half_ref.at[target], sems.at[1, index])
        )
    for copy in inward:
        copy.start()
    for first, second in zip(inward, outward):
        first.wait()
        second.start()
    for copy in outward:
        copy.wait()


def cut_half(here, features):
    half = (features.shape[0] // 2, features.shape[1])
    return pl.pallas_call(
        cut_half_kernel,
        in_specs=[SMEM, ANY],
        out_specs=ANY,
        out_shape=jax.ShapeDtypeStruct(half, jnp.bfloat16),
        scratch_shapes=[pltpu.VMEM(half, jnp.bfloat16), pltpu.SemaphoreType.DMA((2, 4))],
        compiler_params=pltpu.CompilerParams(vmem_limit_bytes=60 * MIB),
    )(here, features)


def cut_rest_kernel(here_ref, features, half_ref, edge_ref, sems):
    here = here_ref[0]
    half, margin = half_ref.shape[0], edge_ref.shape[0]
    copies = []
    for index, (start, target) in enumerate(
        [((1 - here) * half, half_ref), (here * (2 * half - margin), edge_ref)]
    ):
        rows = pl.ds(pl.multiple_of(start, TILE), target.shape[0])
        copies.append(pltpu.make_async_copy(features.at[rows], target, sems.at[index]))
    for copy in copies:
        copy.start()
    for copy in copies:
        copy.wait()


def cut_rest(here, features, margin):
    rows, width = features.shape
    return pl.pallas_call(
        cut_rest_kernel,
        in_specs=[SMEM, ANY],
        out_specs=[VMEM] * 2,
        out_shape=[
            jax.ShapeDtypeStruct((rows // 2, width), jnp.bfloat16),
            jax.ShapeDtypeStruct((margin, width), jnp.bfloat16),
        ],
        scratch_shapes=[pltpu.SemaphoreType.DMA((2,))],
        compiler_params=pltpu.CompilerParams(vmem_limit_bytes=8 * MIB),
        cost_estimate=pl.CostEstimate(flops=10**11, bytes_accessed=4096, transcendentals=0),
    )(here, features)


def select_kernel(jobs, share, sources, margin, place_ref, *refs):
    matchings = len(refs) - sources - len(jobs) - (margin > 0)
    wanted = refs[:matchings]
    parts = refs[matchings : matchings + sources]
    outs = refs[matchings + sources :]
    here = place_ref[0]
    even = lax.rem(place_ref[1], 2) == 0
    quarter = parts[1].shape[0] // TILE
    if margin:
        start = pl.multiple_of((1 - here) * (quarter * TILE - margin), TILE)
        outs[-1][...] = parts[1][pl.ds(start, margin), :]
    per_part = 2 * quarter
    flat = []
    for (of_even, of_odd, lines), out in zip(jobs, outs):
        at = 0
        for line in lines:
            start = (here if line == 0 else 1 - here) * share
            for slot in range(share):
                tile = wanted[of_even][0, start + slot]
                if of_odd != of_even:
                    tile = jnp.where(even, tile, wanted[of_odd][0, start + slot])
                flat.append((tile, out, at))
                at += 1
    for tile, out, slot in flat:
        own = tile // per_part == here
        place = tile // quarter
        end = jnp.logical_or(place == 0, place == 3)
        target = slice(slot * TILE, (slot + 1) * TILE)

        @pl.when(own)
        def _():
            start = pl.multiple_of(lax.rem(tile, per_part) * TILE, TILE)
            out[target, :] = parts[0][pl.ds(start, TILE), :]

        start = pl.multiple_of(lax.rem(tile, quarter) * TILE, TILE)

        @pl.when(jnp.logical_and(jnp.logical_not(own), end))
        def _():
            out[target, :] = parts[1][pl.ds(start, TILE), :]

        if sources > 2:

            @pl.when(jnp.logical_not(jnp.logical_or(own, end)))
            def _():
                out[target, :] = parts[2][pl.ds(start, TILE), :]


def select(place, jobs, share, wanted, parts, margin=0):
    width = parts[0].shape[1]
    sizes = [share * len(lines) * TILE for _, _, lines in jobs]
    sizes += [margin] * (margin > 0)
    return pl.pallas_call(
        functools.partial(select_kernel, jobs, share, len(parts), margin),
        in_specs=[SMEM] * (1 + len(wanted)) + [VMEM] * len(parts),
        out_specs=[VMEM] * len(sizes),
        out_shape=[jax.ShapeDtypeStruct((size, width), jnp.bfloat16) for size in sizes],
        compiler_params=pltpu.CompilerParams(vmem_limit_bytes=16 * MIB),
        cost_estimate=pl.CostEstimate(flops=1000, bytes_accessed=1000, transcendentals=0),
    )(place, *wanted, *parts)


def rank_tiles(tiles, edges, column_of, mark, on_tile):
    every = range(mark.shape[0])
    quarter = tiles // 4
    for tile in range(tiles):
        for matching in every:
            mark[matching, tile] = 0
    missing = [jnp.int32(edges)] * len(every)
    for edge in range(edges):
        for matching in every:
            tile = column_of(matching, edge)
            missing[matching] = missing[matching] - (1 - mark[matching, tile])
            mark[matching, tile] = 1
    rank = [jnp.int32(0)] * len(every)
    for at in range(tiles):
        tile = at + (quarter if at // quarter % 2 == 0 else -quarter)
        for matching in every:
            present = mark[matching, tile]
            added = jnp.where(jnp.logical_and(present == 0, missing[matching] > 0), 1, 0)
            on_tile(matching, tile, rank[matching])
            rank[matching] = rank[matching] + present + added
            missing[matching] = missing[matching] - added


def spots_kernel(tiles, lines, blocks, here_ref, block_ref, cols_ref, *refs):
    (place_ref, own_ref, near_table, rest_table) = refs[:4]
    spots_refs = refs[4:7]
    wanted_refs = refs[7:-2]
    mark, rank_of = refs[-2:]
    matchings, edges = cols_ref.shape
    share = edges // lines
    here, block = here_ref[0], block_ref[0]
    odd = lax.rem(block, 2)
    place_ref[0] = here
    place_ref[1] = block
    per_part = tiles // lines
    quarter = per_part // 2
    for index in range(tiles + 2 * HT):
        column = index - HT
        if 0 <= column < tiles:
            own = here == column // per_part
            own_place = jnp.where(own, column % per_part, -1)
            within = column % quarter
            end = column // quarter in (0, 3)
            near = jnp.where(own, -1, per_part + within if end else -1)
            rest = jnp.where(own, -1, -1 if end else within)
        else:
            after = column >= tiles
            own_place = near = jnp.int32(-1)
            ours = here == (0 if after else 1)
            rest = (column - tiles if after else column + HT) + jnp.where(ours, quarter + HT, quarter)
            rest = jnp.where(block < blocks - 1 if after else block > 0, rest, -1)
        own_ref[0, index] = own_place
        own_ref[1, index] = -1
        near_table[0, index] = near
        near_table[1, index] = jnp.maximum(near, own_place)
        rest_table[0, index] = rest
        rest_table[1, index] = rest

    def on_tile(matching, tile, slot):
        rank_of[matching, tile] = slot
        wanted_refs[matching][0, slot] = tile

    rank_tiles(tiles, edges, lambda matching, edge: cols_ref[matching, edge], mark, on_tile)
    for edge in range(edges):
        for matching in range(matchings):
            slot = rank_of[matching, cols_ref[matching, edge]]
            away = jnp.where(slot // share == here, 0, 1)
            within = lax.rem(slot, share)
            if matching == 0:
                when, spot = 0, away * share + within
            elif matching == 1:
                when, spot = away, within + jnp.where(away == 0, 3 * share, 0)
            else:
                second = odd if matching == matchings - 1 else 1 - odd
                when = jnp.where(away == 0, second, 1 + second)
                spot = within + share * jnp.where(second == 0, 2, jnp.where(away == 0, 1, odd))
            for index, spots_ref in enumerate(spots_refs):
                spots_ref[matching, edge] = jnp.where(when == index, spot, -1)


def arrival_spots(here, block, blocks, cols, tiles, lines):
    wanted = jax.ShapeDtypeStruct((1, 2 * cols.shape[1]), jnp.int32)
    spots = jax.ShapeDtypeStruct(cols.shape, jnp.int32)
    table = jax.ShapeDtypeStruct((2, tiles + 2 * HT), jnp.int32)
    place = jax.ShapeDtypeStruct((2,), jnp.int32)
    place, *rest = pl.pallas_call(
        functools.partial(spots_kernel, tiles, lines, blocks),
        in_specs=[SMEM] * 3,
        out_specs=[SMEM] * (7 + cols.shape[0]),
        out_shape=[place] + [table] * 3 + [spots] * 3 + [wanted] * cols.shape[0],
        scratch_shapes=[pltpu.SMEM((cols.shape[0], tiles), jnp.int32)] * 2,
        compiler_params=pltpu.CompilerParams(vmem_limit_bytes=8 * MIB),
        cost_estimate=pl.CostEstimate(flops=10**11, bytes_accessed=4096, transcendentals=0),
    )(here, block, cols)
    return place, rest[:3], rest[3:6], rest[6:]


def local(features, w_query, w_key_value, edge_local, edge_expand, local_cols, exp_rows, exp_cols):
    groups = lax.axis_size("head")
    blocks = lax.axis_size("node")
    own_rows, width = features.shape
    here = lax.axis_index("head")
    block = lax.axis_index("node")
    edges = exp_cols.shape[2]
    tiles = local_cols.shape[0]
    own_tiles = own_rows // TILE
    margin = HT * TILE
    exp_rows, exp_cols = exp_rows[0], exp_cols[0]
    log_count = blocks.bit_length() - 1
    flips = [1 << matching * log_count // MATCH for matching in range(MATCH)]

    def swap(x, matching, of_odd=None):
        flip = [flips[matching], flips[matching if of_odd is None else of_odd]]
        return lax.ppermute(x, "node", [(i, i ^ flip[i % 2]) for i in range(blocks)])

    def other(x):
        return lax.ppermute(x, "head", [(0, 1), (1, 0)])

    scales = jnp.stack([edge_local, edge_expand])
    listed = local_cols.shape[1]
    split = own_tiles
    two = groups == 2 and min(flips[2:]) > 1

    if two:
        split = own_tiles // 4
        here_array = jnp.reshape(here, (1,)).astype(jnp.int32)
        block_array = jnp.reshape(block, (1,)).astype(jnp.int32)
        first_half = cut_half(here_array, features)
        beside = other(scales)
        first_half, features, exp_cols, local_cols, beside, w_query, w_key_value = (
            lax.optimization_barrier(
                (first_half, features, exp_cols, local_cols, beside, w_query, w_key_value)
            )
        )
        local_cols = local_cols.reshape(-1)
        w = jnp.transpose(w_key_value, (1, 0, 2))
        first_half = other(first_half)
        second_half, edge_rows = cut_rest(here_array, features, margin)
        place, tables, spots, wanted = arrival_spots(
            here_array, block_array, blocks, exp_cols, tiles, groups
        )
        edge_rows, *wanted = lax.optimization_barrier((edge_rows, *wanted))
        wanted_pair, *wanted = wanted
        wanted = [swap(wanted[m - 1], m) for m in range(1, MATCH)]
        inward = [(2 * i, 2 * i - 2) for i in range(1, blocks)]
        inward += [(2 * i + 1, 2 * i + 3) for i in range(blocks - 1)]
        halo = lax.ppermute(edge_rows, ("node", "head"), inward)
        scales = jnp.where(
            here == 0,
            jnp.concatenate([scales, beside], axis=1),
            jnp.concatenate([beside, scales], axis=1),
        )
        scales, w, local_cols, halo, *wanted = lax.optimization_barrier(
            (scales, w, local_cols, halo, *wanted)
        )
        num, den, keys, values, local_q, expand_q = own_attention(
            (place, local_cols, tables[0]), features, w, w_query, scales, split, listed
        )
        first_half, second_half, num = lax.optimization_barrier((first_half, second_half, num))
        second_half = other(second_half)
        share = edges // groups
        sources = [features, first_half]
        jobs = ((2, 1, (0,)), (1, 2, (0,)), (0, 0, (0,)))
        *chosen, edge_rows = select(place, jobs, share, wanted, sources, margin)
        num, *chosen = lax.optimization_barrier((num, *chosen))
        first = swap(chosen[0], 3, 2)
        early = swap(chosen[2], 1)
        num, den = more_attention(
            (place, local_cols, tables[1]),
            [first_half],
            w,
            local_q,
            num,
            den,
            (keys, values),
            split,
            listed,
        )
        second_half, num, den, edge_rows, wanted_pair, second = lax.optimization_barrier(
            (second_half, num, den, edge_rows, wanted_pair, chosen[1])
        )
        outward = [(2 * i, 2 * i + 2) for i in range(blocks - 1)]
        outward += [(2 * i + 1, 2 * i - 1) for i in range(1, blocks)]
        other_halo = lax.ppermute(edge_rows, ("node", "head"), outward)
        wanted_pair = swap(wanted_pair, 0)
        sources = [features, first_half, second_half]
        late, direct = select(place, ((0, 0, (1,)), (1, 1, (1,))), share, wanted, sources)
        num, first, early, late = lax.optimization_barrier((num, first, early, late))
        second = swap(second, 2, 3)
        first_beside = other(first)
        late = swap(late, 1)
        (pair,) = select(place, ((0, 0, (0, 1)),), share, [wanted_pair], sources)
        num, pair, other_halo = lax.optimization_barrier((num, pair, other_halo))
        pair = swap(pair, 0)
        num, den = more_attention(
            (place, local_cols, tables[2]),
            [second_half, other_halo, halo],
            w,
            local_q,
            num,
            den,
            (),
            split,
            listed,
        )
        num, den = expand_attention(
            place, exp_rows, spots[0], [pair, first, early], expand_q, num, den, w, False, None
        )
        second, direct, num, den = lax.optimization_barrier((second, direct, num, den))
        direct = lax.ppermute(direct, "node", [(i, i ^ flips[2]) for i in range(0, blocks, 2)])
        sides = [(4 * i + 2 + side, 4 * i + 3 - side) for i in range(blocks // 2) for side in (0, 1)]
        second_beside = lax.ppermute(second, ("node", "head"), sides)
        sources = [None, [late, second, first_beside], [direct, second_beside]]
    else:
        place = jnp.stack([here, block]).astype(jnp.int32)
        column = jnp.arange(tiles + 2 * HT, dtype=jnp.int32) - HT
        usable = block * tiles + column
        usable = jnp.logical_and(usable >= 0, usable < blocks * tiles)
        own = column // own_tiles == here
        w = jnp.transpose(w_key_value, (1, 0, 2))
        gather = lambda x: lax.all_gather(x, "head", axis=0, tiled=True)
        scales = lax.all_gather(scales, "head", axis=1, tiled=True)
        full = gather(features)
        before = lax.ppermute(full[-margin:], "node", [(i, i + 1) for i in range(blocks - 1)])
        after = lax.ppermute(full[:margin], "node", [(i + 1, i) for i in range(blocks - 1)])
        received = [gather(swap(features, m)) for m in range(MATCH)]
        sources = [None, received[:2], received[2:]]
        matching = jnp.arange(MATCH, dtype=jnp.int32)[:, None]
        spots = [
            None,
            jnp.where(matching < 2, matching * tiles + exp_cols, -1),
            jnp.where(matching < 2, -1, (matching - 2) * tiles + exp_cols),
        ]
        where_own = jnp.where(own, column - here * own_tiles, -1)
        where_rest = jnp.where(jnp.logical_and(usable, jnp.logical_not(own)), column + HT, -1)
        local_cols = local_cols.reshape(-1)
        num, den, keys, values, local_q, expand_q = own_attention(
            (place, local_cols, jnp.stack([where_own] * 2)),
            features,
            w,
            w_query,
            scales,
            split,
            listed,
        )
        num, den = more_attention(
            (place, local_cols, jnp.stack([where_rest] * 2)),
            [before, full, after],
            w,
            local_q,
            num,
            den,
            (),
            split,
            listed,
        )
    num, den, out = expand_attention(
        place, exp_rows, spots[1], sources[1], expand_q, num, den, w, True, None
    )
    return expand_attention(
        place, exp_rows, spots[2], sources[2], expand_q, num, den, w, True, out
    )


def solution(mesh):
    return jax.shard_map(
        local,
        mesh=mesh,
        in_specs=(
            P(("node", "head"), None),
            P(),
            P(),
            P("head"),
            P("head"),
            P("node", None),
            P("node", None, None),
            P("node", None, None),
        ),
        out_specs=P(("node", "head"), None),
        check_vma=False,
    )
```

```python
import functools
import math

import jax
import jax.numpy as jnp
from jax import lax
from jax.experimental import pallas as pl
from jax.experimental.pallas import tpu as pltpu
from jax.sharding import PartitionSpec as P

HEADS = 8
TILE = 128
HT = 2
MATCH = 4
LANES = 128
GROUP = 4
MIB = 1024 * 1024

ANY = pl.BlockSpec(memory_space=pl.ANY)
SMEM = pl.BlockSpec(memory_space=pltpu.SMEM)
VMEM = pl.BlockSpec(memory_space=pltpu.VMEM)
HBM = pl.BlockSpec(memory_space=pltpu.HBM)


def lane_masks():
    lane = lax.broadcasted_iota(jnp.int32, (TILE, LANES), 1)
    return lane < LANES // 2, lane % (LANES // 2)


def pack_denominators(pieces):
    _, within = lane_masks()
    size = LANES // 2 // len(pieces)
    packed = pieces[-1]
    for pair in range(len(pieces) - 2, -1, -1):
        packed = jnp.where(within < (pair + 1) * size, pieces[pair], packed)
    return packed


def denominator_chooser(pairs):
    size = LANES // 2 // pairs
    shape = (2 * LANES, pairs * LANES)
    source = lax.broadcasted_iota(jnp.int32, shape, 0) % LANES
    target = lax.broadcasted_iota(jnp.int32, shape, 1)
    wanted = target // LANES * size + (target % LANES) // (LANES // 2) * (LANES // 2)
    return jnp.where(source == wanted, 1.0, 0.0).astype(jnp.bfloat16)


def spread_reciprocals(packed, chooser):
    inverse = 1.0 / packed
    coarse = inverse.astype(jnp.bfloat16)
    fine = (inverse - coarse.astype(jnp.float32)).astype(jnp.bfloat16)
    return jnp.dot(
        jnp.concatenate([coarse, fine], axis=1), chooser, preferred_element_type=jnp.float32
    )


def project(rows, w, keys, values, first):
    new_keys = jnp.dot(rows, w[0], preferred_element_type=jnp.float32).astype(jnp.bfloat16).T
    new_values = jnp.dot(rows, w[1], preferred_element_type=jnp.float32).astype(jnp.bfloat16)
    for index in range(rows.shape[0] // TILE):
        span = slice(index * TILE, (index + 1) * TILE)
        keys[first + index] = new_keys[:, span]
        values[first + index] = new_values[span, :]


def attend_chunks(queries, keys, values, ones, num, den, units):
    low, _ = lane_masks()
    low_mask = jnp.where(low, 1.0, 0.0).astype(jnp.bfloat16)
    high_mask = jnp.where(low, 0.0, 1.0).astype(jnp.bfloat16)
    rows = [pl.ds(pl.multiple_of(unit[0] * TILE, TILE), TILE) for unit in units]
    last = queries.shape[0] // TILE - 1
    query_rows = [
        pl.ds(pl.multiple_of(jnp.minimum(unit[0], last) * TILE, TILE), TILE) for unit in units
    ]
    denominators = [[] for _ in units]
    for pair in range(queries.shape[1] // LANES):
        part = slice(pair * LANES, (pair + 1) * LANES)
        weights = []
        for row, (_, one, two, _) in zip(query_rows, units):
            some = queries[row, part]
            scores = jnp.dot(
                jnp.concatenate([some * low_mask, some * high_mask], axis=0),
                jnp.concatenate([keys[one, part, :], keys[two, part, :]], axis=1),
                preferred_element_type=jnp.float32,
            )
            weights.append(jnp.exp(jnp.clip(scores, -5.0, 5.0)).astype(jnp.bfloat16))
        sums = []
        for weight, (_, one, two, fills) in zip(weights, units):
            counts = ones[fills]
            wide = [
                jnp.concatenate([values[one, :, part], ones[0]], axis=1),
                jnp.concatenate([values[two, :, part] * counts, counts], axis=1),
            ]
            sums.append(
                jnp.dot(
                    weight, jnp.concatenate(wide, axis=0), preferred_element_type=jnp.float32
                )
            )
        for row, both, listed in zip(rows, sums, denominators):
            num[row, part] += jnp.where(low, both[:TILE, :LANES], both[TILE:, :LANES])
            listed.append(jnp.where(low, both[:TILE, LANES:], both[TILE:, LANES:]))
    for row, listed in zip(rows, denominators):
        den[row, :] += pack_denominators(listed)


def attend_units(queries, rows_here, w, num, den, rows):
    keys = jnp.dot(rows_here, w[0], preferred_element_type=jnp.float32).astype(jnp.bfloat16)
    values = jnp.dot(rows_here, w[1], preferred_element_type=jnp.float32).astype(jnp.bfloat16)
    low_lanes, _ = lane_masks()
    low = jnp.where(low_lanes, 1.0, 0.0).astype(jnp.bfloat16)
    high = jnp.where(low_lanes, 0.0, 1.0).astype(jnp.bfloat16)
    last = queries.shape[0] // TILE - 1
    query_rows = [
        pl.ds(pl.multiple_of(jnp.minimum(row, last) * TILE, TILE), TILE) for row in rows
    ]
    rows = [pl.ds(pl.multiple_of(row * TILE, TILE), TILE) for row in rows]
    spans = [slice(index * TILE, (index + 1) * TILE) for index in range(len(rows))]
    denominators = [[] for _ in rows]
    for pair in range(queries.shape[1] // LANES):
        part = slice(pair * LANES, (pair + 1) * LANES)
        weights = []
        for row, span in zip(query_rows, spans):
            key = keys[span, part]
            scores = lax.dot_general(
                queries[row, part],
                jnp.concatenate([key * low, key * high], axis=0),
                (((1,), (1,)), ((), ())),
                preferred_element_type=jnp.float32,
            )
            weights.append(jnp.exp(jnp.clip(scores, -5.0, 5.0)).astype(jnp.bfloat16))
        sums = []
        for weight, span in zip(weights, spans):
            value = values[span, part]
            wide = jnp.concatenate(
                [
                    jnp.concatenate([value * low, low], axis=1),
                    jnp.concatenate([value * high, high], axis=1),
                ],
                axis=0,
            )
            sums.append(jnp.dot(weight, wide, preferred_element_type=jnp.float32))
        for row, both, listed in zip(rows, sums, denominators):
            num[row, part] += both[:, :LANES]
            listed.append(both[:, LANES:])
    for row, listed in zip(rows, denominators):
        den[row, :] += pack_denominators(listed)


def project_pieces(pieces, w, keys, values, at):
    for piece in pieces:
        tiles = piece.shape[0] // TILE
        size = math.gcd(tiles, GROUP)

        def some_tiles(index, carry, piece=piece, at=at, size=size):
            some = piece[pl.ds(pl.multiple_of(index * size * TILE, TILE), size * TILE), :]
            project(some, w, keys, values, at + index * size)
            return carry

        lax.fori_loop(0, tiles // size, some_tiles, 0)
        at += tiles


def attend_listed(
    steps, split, place_ref, cols_ref, where_ref, queries, keys, values, num, den, scratch
):
    ones, row_list, tile_list, fill_list = scratch
    tiles_here = queries.shape[0] // TILE
    slots = tile_list.shape[0] - 2 * row_list.shape[0]
    ones[0] = jnp.ones(ones.shape[1:], ones.dtype)
    ones[1] = jnp.zeros(ones.shape[1:], ones.dtype)

    def visit(row, found):
        part = jnp.where(row < split, 0, 1)
        at = 2 * found
        for slot in range(slots):
            tile = where_ref[part, cols_ref[(place_ref[0] * tiles_here + row) * slots + slot]]
            tile_list[at] = tile
            at = at + (tile >= 0).astype(jnp.int32)
        tile_list[at] = 0
        units = (at - 2 * found + 1) // 2
        odd = lax.rem(at, 2)
        for unit in range(slots // 2):
            row_list[found + unit] = row
            fill_list[found + unit] = jnp.where(unit == units - 1, odd, 0)
        return found + units

    found = lax.fori_loop(0, steps, visit, jnp.int32(0))
    for inner in range(GROUP):
        row_list[found + inner] = tiles_here
        fill_list[found + inner] = 0
        tile_list[2 * (found + inner)] = 0
        tile_list[2 * (found + inner) + 1] = 0

    def group(first, size):
        units = []
        for inner in range(size):
            unit = first + inner
            units.append(
                (row_list[unit], tile_list[2 * unit], tile_list[2 * unit + 1], fill_list[unit])
            )
        attend_chunks(queries, keys, values, ones, num, den, units)

    in_groups(found, group)


def in_groups(found, group):
    whole = found // GROUP

    def visit(index, carry):
        group(index * GROUP, GROUP)
        return carry

    lax.fori_loop(0, whole, visit, 0)
    left = found - whole * GROUP
    half = GROUP // 2
    pl.when(left > half)(lambda: group(whole * GROUP, GROUP))
    pl.when(jnp.logical_and(left > 0, left <= half))(lambda: group(whole * GROUP, half))


def each_tile(tiles, action):
    def visit(tile, carry):
        action(pl.ds(pl.multiple_of(tile * TILE, TILE), TILE))
        return carry

    lax.fori_loop(0, tiles, visit, 0)


def own_kernel(split, place_ref, cols_ref, where_ref, rows, w, wq, scales, *refs):
    (num, den, keys, values, local_ref, expand_ref) = refs[:6]
    width = rows.shape[1]
    tiles = rows.shape[0] // TILE
    size = min(GROUP, tiles)
    project_pieces([rows], w, keys, values, 0)

    def some_queries(index, carry):
        target = pl.ds(pl.multiple_of(index * size * TILE, TILE), size * TILE)
        queries = jnp.dot(rows[target, :], wq[...], preferred_element_type=jnp.float32)
        queries = queries.astype(jnp.bfloat16).astype(jnp.float32)
        scale = 1.0 / math.sqrt(width // HEADS)
        local_ref[target, :] = (queries * scales[0:1, :] * scale).astype(jnp.bfloat16)
        expand_ref[target, :] = (queries * scales[1:2, :] * scale).astype(jnp.bfloat16)
        return carry

    lax.fori_loop(0, tiles // size, some_queries, 0)

    def clear(target):
        num[target, :] = jnp.zeros((TILE, width), jnp.float32)
        den[target, :] = jnp.zeros((TILE, LANES), jnp.float32)

    each_tile(tiles + 1, clear)
    attend_listed(
        split, split, place_ref, cols_ref, where_ref, local_ref, keys, values, num, den, refs[6:]
    )


def more_kernel(count, from_own, split, place_ref, cols_ref, where_ref, *refs):
    pieces = refs[:count]
    (w, local_ref, num_in, den_in) = refs[count : count + 4]
    refs = refs[count + 4 :]
    if from_own:
        (own_keys, own_values, num, den, *scratch, keys, values) = refs
        first = own_keys.shape[0]

        def bring(tile, carry):
            keys[tile] = own_keys[tile]
            values[tile] = own_values[tile]
            return carry

        lax.fori_loop(0, first, bring, 0)
    else:
        (num, den, *scratch, keys, values) = refs
        first = 0
    project_pieces(pieces, w, keys, values, first)

    def begin(target):
        num[target, :] = num_in[target, :]
        den[target, :] = den_in[target, :]

    tiles = local_ref.shape[0] // TILE
    each_tile(tiles + 1, begin)
    attend_listed(
        tiles, split, place_ref, cols_ref, where_ref, local_ref, keys, values, num, den, scratch
    )


def sums_shapes(own_rows, width):
    return [
        jax.ShapeDtypeStruct((own_rows + TILE, width), jnp.float32),
        jax.ShapeDtypeStruct((own_rows + TILE, LANES), jnp.float32),
    ]


def list_scratch(own_rows, slots):
    units = own_rows // TILE * (slots // 2) + GROUP
    return [
        pltpu.VMEM((2, TILE, LANES), jnp.bfloat16),
        pltpu.SMEM((units,), jnp.int32),
        pltpu.SMEM((2 * units + slots,), jnp.int32),
        pltpu.SMEM((units,), jnp.int32),
    ]


def own_attention(tables, rows, w, wq, scales, split, slots):
    own_rows, width = rows.shape
    tiles = own_rows // TILE
    shapes = [(tiles, width, TILE), (tiles, TILE, width), rows.shape, rows.shape]
    return pl.pallas_call(
        functools.partial(own_kernel, split),
        in_specs=[SMEM] * 3 + [VMEM] * 4,
        out_specs=[VMEM] * 6,
        out_shape=sums_shapes(own_rows, width)
        + [jax.ShapeDtypeStruct(shape, jnp.bfloat16) for shape in shapes],
        scratch_shapes=list_scratch(own_rows, slots),
        compiler_params=pltpu.CompilerParams(vmem_limit_bytes=24 * MIB),
        cost_estimate=pl.CostEstimate(flops=10**8, bytes_accessed=10**5, transcendentals=0),
    )(*tables, rows, w, wq, scales)


def more_attention(tables, pieces, w, local_q, num, den, own, split, slots):
    own_rows, width = local_q.shape
    tiles = sum(piece.shape[0] // TILE for piece in pieces) + (own_rows // TILE if own else 0)
    return pl.pallas_call(
        functools.partial(more_kernel, len(pieces), bool(own), split),
        in_specs=[SMEM] * 3 + [VMEM] * (len(pieces) + 4 + len(own)),
        out_specs=[VMEM] * 2,
        out_shape=sums_shapes(own_rows, width),
        scratch_shapes=list_scratch(own_rows, slots)
        + [
            pltpu.VMEM((tiles, width, TILE), jnp.bfloat16),
            pltpu.VMEM((tiles, TILE, width), jnp.bfloat16),
        ],
        compiler_params=pltpu.CompilerParams(vmem_limit_bytes=24 * MIB),
        cost_estimate=pl.CostEstimate(
            flops=10**12 if own else 10**8, bytes_accessed=10**5, transcendentals=0
        ),
    )(*tables, *pieces, w, local_q, num, den, *own)


def expand_kernel(count, gives_out, last, place_ref, rows_ref, spots_ref, *refs):
    sources = refs[:count]
    (expand_q, num_in, den_in, w) = refs[count : count + 4]
    refs = refs[count + 4 :]
    if last:
        (_, out_ref, features, num, den, row_list, tile_list, mark) = refs[:-3]
        (results, result_sems) = refs[-3:-1]
    else:
        if gives_out:
            (num, den, out_ref) = refs[:3]
        else:
            (num, den) = refs[:2]
        (features, row_list, tile_list, mark) = refs[-5:-1]
    chooser = refs[-1]
    own_rows, width = expand_q.shape
    tiles_here = own_rows // TILE
    matchings, edges = rows_ref.shape
    if gives_out:
        chooser[...] = denominator_chooser(width // LANES)
    for tile in range(tiles_here):
        mark[tile] = 0 if last else 1

    def visit(edge, found):
        for matching in range(matchings):
            row = rows_ref[matching, edge] - place_ref[0] * tiles_here
            spot = spots_ref[matching, edge]
            mine = jnp.logical_and(jnp.logical_and(row >= 0, row < tiles_here), spot >= 0)
            row_list[found] = row
            tile_list[found] = spot
            found = found + mine.astype(jnp.int32)
            if last:

                @pl.when(mine)
                def _():
                    mark[row] = 1

        return found

    found = lax.fori_loop(0, edges, visit, jnp.int32(0))
    for inner in range(GROUP):
        row_list[found + inner] = tiles_here
        tile_list[found + inner] = 0

    def each_marked(action):
        def visit_tile(tile, carry):
            target = pl.ds(pl.multiple_of(tile * TILE, TILE), TILE)
            pl.when(mark[tile] == 1)(lambda: action(tile, target))
            return carry

        lax.fori_loop(0, tiles_here, visit_tile, 0)

    def begin(tile, target):
        num[target, :] = num_in[target, :]
        den[target, :] = den_in[target, :]

    each_marked(begin)
    spare = pl.ds(own_rows, TILE)
    num[spare, :] = jnp.zeros((TILE, width), jnp.float32)
    den[spare, :] = jnp.zeros((TILE, LANES), jnp.float32)

    def group(first, size):
        for i in range(size):
            spot = tile_list[first + i]
            for source in sources:
                tiles = source.shape[0] // TILE

                @pl.when(jnp.logical_and(spot >= 0, spot < tiles))
                def _(source=source, spot=spot):
                    rows = pl.ds(pl.multiple_of(spot * TILE, TILE), TILE)
                    features[i * TILE : (i + 1) * TILE, :] = source[rows, :]

                spot = spot - tiles
        rows = [row_list[first + i] for i in range(size)]
        attend_units(expand_q, features[: size * TILE, :], w, num, den, rows)

    in_groups(found, group)

    def outputs(target):
        inverse = spread_reciprocals(den[target, :], chooser[...])
        return (num[target, :] * inverse).astype(jnp.bfloat16)

    def finish(tile, target):
        results[target, :] = outputs(target)
        copy_out(tile, target).start()

    def finish_some(index, carry):
        size = math.gcd(GROUP, tiles_here) * TILE
        target = pl.ds(pl.multiple_of(index * size, TILE), size)
        out_ref[target, :] = outputs(target)
        return carry

    def copy_out(tile, target):
        return pltpu.make_async_copy(results.at[target], out_ref.at[target], result_sems.at[tile])

    if last:
        each_marked(finish)
    elif gives_out:
        lax.fori_loop(0, tiles_here // math.gcd(GROUP, tiles_here), finish_some, 0)
    if last:
        each_marked(lambda tile, target: copy_out(tile, target).wait())


def expand_attention(place, exp_rows, spots, sources, expand_q, num, den, w, gives_out, out):
    width = w.shape[2]
    own_rows = expand_q.shape[0]
    last = out is not None
    most = exp_rows.shape[0] * exp_rows.shape[1] + GROUP
    sums = sums_shapes(own_rows, width)
    result = jax.ShapeDtypeStruct((own_rows, width), jnp.bfloat16)
    sums_scratch = [pltpu.VMEM(array.shape, array.dtype) for array in sums]
    arguments = [place, exp_rows, spots, *sources, expand_q, num, den, w]
    return pl.pallas_call(
        functools.partial(expand_kernel, len(sources), gives_out, last),
        in_specs=[SMEM] * 3 + [VMEM] * (len(sources) + 4) + [ANY] * last,
        out_specs=ANY if last else [VMEM] * (2 + gives_out),
        out_shape=result if last else sums + [result] * gives_out,
        input_output_aliases={len(arguments): 0} if last else {},
        scratch_shapes=[
            pltpu.VMEM((GROUP * TILE, width), jnp.bfloat16),
        ]
        + (sums_scratch if last else [])
        + [
            pltpu.SMEM((most,), jnp.int32),
            pltpu.SMEM((most,), jnp.int32),
            pltpu.SMEM((own_rows // TILE,), jnp.int32),
        ]
        + (
            [
                pltpu.VMEM((own_rows, width), jnp.bfloat16),
                pltpu.SemaphoreType.DMA((own_rows // TILE,)),
            ]
            if last
            else []
        )
        + [pltpu.VMEM((2 * LANES, width), jnp.bfloat16)],
        compiler_params=pltpu.CompilerParams(vmem_limit_bytes=24 * MIB),
        cost_estimate=pl.CostEstimate(
            flops=own_rows * width * 256, bytes_accessed=own_rows * width, transcendentals=0
        ),
    )(*arguments, *([out] if last else []))


def cut_half_kernel(here_ref, features, half_ref, buffer, sems):
    rows = half_ref.shape[0]
    start = here_ref[0] * rows
    pieces = sems.shape[1]
    size = rows // pieces
    inward, outward = [], []
    for index in range(pieces):
        source = pl.ds(pl.multiple_of(start + index * size, TILE), size)
        target = pl.ds(index * size, size)
        inward.append(
            pltpu.make_async_copy(features.at[source], buffer.at[target], sems.at[0, index])
        )
        outward.append(
            pltpu.make_async_copy(buffer.at[target], half_ref.at[target], sems.at[1, index])
        )
    for copy in inward:
        copy.start()
    for first, second in zip(inward, outward):
        first.wait()
        second.start()
    for copy in outward:
        copy.wait()


def cut_half(here, features):
    half = (features.shape[0] // 2, features.shape[1])
    return pl.pallas_call(
        cut_half_kernel,
        in_specs=[SMEM, ANY],
        out_specs=ANY,
        out_shape=jax.ShapeDtypeStruct(half, jnp.bfloat16),
        scratch_shapes=[pltpu.VMEM(half, jnp.bfloat16), pltpu.SemaphoreType.DMA((2, 4))],
        compiler_params=pltpu.CompilerParams(vmem_limit_bytes=60 * MIB),
    )(here, features)


def cut_rest_kernel(here_ref, features, half_ref, edge_ref, sems):
    here = here_ref[0]
    half, margin = half_ref.shape[0], edge_ref.shape[0]
    copies = []
    for index, (start, target) in enumerate(
        [((1 - here) * half, half_ref), (here * (2 * half - margin), edge_ref)]
    ):
        rows = pl.ds(pl.multiple_of(start, TILE), target.shape[0])
        copies.append(pltpu.make_async_copy(features.at[rows], target, sems.at[index]))
    for copy in copies:
        copy.start()
    for copy in copies:
        copy.wait()


def cut_rest(here, features, margin):
    rows, width = features.shape
    return pl.pallas_call(
        cut_rest_kernel,
        in_specs=[SMEM, ANY],
        out_specs=[VMEM] * 2,
        out_shape=[
            jax.ShapeDtypeStruct((rows // 2, width), jnp.bfloat16),
            jax.ShapeDtypeStruct((margin, width), jnp.bfloat16),
        ],
        scratch_shapes=[pltpu.SemaphoreType.DMA((2,))],
        compiler_params=pltpu.CompilerParams(vmem_limit_bytes=8 * MIB),
        cost_estimate=pl.CostEstimate(flops=10**11, bytes_accessed=4096, transcendentals=0),
    )(here, features)


def select_kernel(jobs, share, sources, margin, place_ref, *refs):
    matchings = len(refs) - sources - len(jobs) - (margin > 0)
    wanted = refs[:matchings]
    parts = refs[matchings : matchings + sources]
    outs = refs[matchings + sources :]
    here = place_ref[0]
    even = lax.rem(place_ref[1], 2) == 0
    quarter = parts[1].shape[0] // TILE
    if margin:
        start = pl.multiple_of((1 - here) * (quarter * TILE - margin), TILE)
        outs[-1][...] = parts[1][pl.ds(start, margin), :]
    per_part = 2 * quarter
    flat = []
    for (of_even, of_odd, lines), out in zip(jobs, outs):
        at = 0
        for line in lines:
            start = (here if line == 0 else 1 - here) * share
            for slot in range(share):
                tile = wanted[of_even][0, start + slot]
                if of_odd != of_even:
                    tile = jnp.where(even, tile, wanted[of_odd][0, start + slot])
                flat.append((tile, out, at))
                at += 1
    for tile, out, slot in flat:
        own = tile // per_part == here
        place = tile // quarter
        end = jnp.logical_or(place == 0, place == 3)
        target = slice(slot * TILE, (slot + 1) * TILE)

        @pl.when(own)
        def _():
            start = pl.multiple_of(lax.rem(tile, per_part) * TILE, TILE)
            out[target, :] = parts[0][pl.ds(start, TILE), :]

        start = pl.multiple_of(lax.rem(tile, quarter) * TILE, TILE)

        @pl.when(jnp.logical_and(jnp.logical_not(own), end))
        def _():
            out[target, :] = parts[1][pl.ds(start, TILE), :]

        if sources > 2:

            @pl.when(jnp.logical_not(jnp.logical_or(own, end)))
            def _():
                out[target, :] = parts[2][pl.ds(start, TILE), :]


def select(place, jobs, share, wanted, parts, margin=0):
    width = parts[0].shape[1]
    sizes = [share * len(lines) * TILE for _, _, lines in jobs]
    sizes += [margin] * (margin > 0)
    return pl.pallas_call(
        functools.partial(select_kernel, jobs, share, len(parts), margin),
        in_specs=[SMEM] * (1 + len(wanted)) + [VMEM] * len(parts),
        out_specs=[VMEM] * len(sizes),
        out_shape=[jax.ShapeDtypeStruct((size, width), jnp.bfloat16) for size in sizes],
        compiler_params=pltpu.CompilerParams(vmem_limit_bytes=16 * MIB),
        cost_estimate=pl.CostEstimate(flops=1000, bytes_accessed=1000, transcendentals=0),
    )(place, *wanted, *parts)


def rank_tiles(tiles, edges, column_of, mark, on_tile):
    every = range(mark.shape[0])
    quarter = tiles // 4
    for tile in range(tiles):
        for matching in every:
            mark[matching, tile] = 0
    missing = [jnp.int32(edges)] * len(every)
    for edge in range(edges):
        for matching in every:
            tile = column_of(matching, edge)
            missing[matching] = missing[matching] - (1 - mark[matching, tile])
            mark[matching, tile] = 1
    rank = [jnp.int32(0)] * len(every)
    for at in range(tiles):
        tile = at + (quarter if at // quarter % 2 == 0 else -quarter)
        for matching in every:
            present = mark[matching, tile]
            added = jnp.where(jnp.logical_and(present == 0, missing[matching] > 0), 1, 0)
            on_tile(matching, tile, rank[matching])
            rank[matching] = rank[matching] + present + added
            missing[matching] = missing[matching] - added


def spots_kernel(tiles, lines, blocks, here_ref, block_ref, cols_ref, *refs):
    (place_ref, own_ref, near_table, rest_table) = refs[:4]
    spots_refs = refs[4:7]
    wanted_refs = refs[7:-2]
    mark, rank_of = refs[-2:]
    matchings, edges = cols_ref.shape
    share = edges // lines
    here, block = here_ref[0], block_ref[0]
    odd = lax.rem(block, 2)
    place_ref[0] = here
    place_ref[1] = block
    per_part = tiles // lines
    quarter = per_part // 2
    for index in range(tiles + 2 * HT):
        column = index - HT
        if 0 <= column < tiles:
            own = here == column // per_part
            own_place = jnp.where(own, column % per_part, -1)
            within = column % quarter
            end = column // quarter in (0, 3)
            near = jnp.where(own, -1, per_part + within if end else -1)
            rest = jnp.where(own, -1, -1 if end else within)
        else:
            after = column >= tiles
            own_place = near = jnp.int32(-1)
            ours = here == (0 if after else 1)
            rest = (column - tiles if after else column + HT) + jnp.where(ours, quarter + HT, quarter)
            rest = jnp.where(block < blocks - 1 if after else block > 0, rest, -1)
        own_ref[0, index] = own_place
        own_ref[1, index] = -1
        near_table[0, index] = near
        near_table[1, index] = jnp.maximum(near, own_place)
        rest_table[0, index] = rest
        rest_table[1, index] = rest

    def on_tile(matching, tile, slot):
        rank_of[matching, tile] = slot
        wanted_refs[matching][0, slot] = tile

    rank_tiles(tiles, edges, lambda matching, edge: cols_ref[matching, edge], mark, on_tile)
    for edge in range(edges):
        for matching in range(matchings):
            slot = rank_of[matching, cols_ref[matching, edge]]
            away = jnp.where(slot // share == here, 0, 1)
            within = lax.rem(slot, share)
            if matching == 0:
                when, spot = 0, away * share + within
            elif matching == 1:
                when, spot = away, within + jnp.where(away == 0, 3 * share, 0)
            else:
                second = odd if matching == matchings - 1 else 1 - odd
                when = jnp.where(away == 0, second, 1 + second)
                spot = within + share * jnp.where(second == 0, 2, jnp.where(away == 0, 1, odd))
            for index, spots_ref in enumerate(spots_refs):
                spots_ref[matching, edge] = jnp.where(when == index, spot, -1)


def arrival_spots(here, block, blocks, cols, tiles, lines):
    wanted = jax.ShapeDtypeStruct((1, 2 * cols.shape[1]), jnp.int32)
    spots = jax.ShapeDtypeStruct(cols.shape, jnp.int32)
    table = jax.ShapeDtypeStruct((2, tiles + 2 * HT), jnp.int32)
    place = jax.ShapeDtypeStruct((2,), jnp.int32)
    place, *rest = pl.pallas_call(
        functools.partial(spots_kernel, tiles, lines, blocks),
        in_specs=[SMEM] * 3,
        out_specs=[SMEM] * (7 + cols.shape[0]),
        out_shape=[place] + [table] * 3 + [spots] * 3 + [wanted] * cols.shape[0],
        scratch_shapes=[pltpu.SMEM((cols.shape[0], tiles), jnp.int32)] * 2,
        compiler_params=pltpu.CompilerParams(vmem_limit_bytes=8 * MIB),
        cost_estimate=pl.CostEstimate(flops=10**11, bytes_accessed=4096, transcendentals=0),
    )(here, block, cols)
    return place, rest[:3], rest[3:6], rest[6:]


def local(features, w_query, w_key_value, edge_local, edge_expand, local_cols, exp_rows, exp_cols):
    groups = lax.axis_size("head")
    blocks = lax.axis_size("node")
    own_rows, width = features.shape
    here = lax.axis_index("head")
    block = lax.axis_index("node")
    edges = exp_cols.shape[2]
    tiles = local_cols.shape[0]
    own_tiles = own_rows // TILE
    margin = HT * TILE
    exp_rows, exp_cols = exp_rows[0], exp_cols[0]
    log_count = blocks.bit_length() - 1
    flips = [1 << matching * log_count // MATCH for matching in range(MATCH)]

    def swap(x, matching, of_odd=None):
        flip = [flips[matching], flips[matching if of_odd is None else of_odd]]
        return lax.ppermute(x, "node", [(i, i ^ flip[i % 2]) for i in range(blocks)])

    def other(x):
        return lax.ppermute(x, "head", [(0, 1), (1, 0)])

    scales = jnp.stack([edge_local, edge_expand])
    listed = local_cols.shape[1]
    split = own_tiles
    two = groups == 2 and min(flips[2:]) > 1

    if two:
        split = own_tiles // 4
        here_array = jnp.reshape(here, (1,)).astype(jnp.int32)
        block_array = jnp.reshape(block, (1,)).astype(jnp.int32)
        first_half = cut_half(here_array, features)
        beside = other(scales)
        first_half, features, exp_cols, local_cols, beside, w_query, w_key_value = (
            lax.optimization_barrier(
                (first_half, features, exp_cols, local_cols, beside, w_query, w_key_value)
            )
        )
        local_cols = local_cols.reshape(-1)
        w = jnp.transpose(w_key_value, (1, 0, 2))
        first_half = other(first_half)
        second_half, edge_rows = cut_rest(here_array, features, margin)
        place, tables, spots, wanted = arrival_spots(
            here_array, block_array, blocks, exp_cols, tiles, groups
        )
        edge_rows, *wanted = lax.optimization_barrier((edge_rows, *wanted))
        wanted_pair, *wanted = wanted
        wanted = [swap(wanted[m - 1], m) for m in range(1, MATCH)]
        inward = [(2 * i, 2 * i - 2) for i in range(1, blocks)]
        inward += [(2 * i + 1, 2 * i + 3) for i in range(blocks - 1)]
        halo = lax.ppermute(edge_rows, ("node", "head"), inward)
        scales = jnp.where(
            here == 0,
            jnp.concatenate([scales, beside], axis=1),
            jnp.concatenate([beside, scales], axis=1),
        )
        scales, w, local_cols, halo, *wanted = lax.optimization_barrier(
            (scales, w, local_cols, halo, *wanted)
        )
        num, den, keys, values, local_q, expand_q = own_attention(
            (place, local_cols, tables[0]), features, w, w_query, scales, split, listed
        )
        first_half, second_half, num = lax.optimization_barrier((first_half, second_half, num))
        second_half = other(second_half)
        share = edges // groups
        sources = [features, first_half]
        jobs = ((2, 1, (0,)), (1, 2, (0,)), (0, 0, (0,)))
        *chosen, edge_rows = select(place, jobs, share, wanted, sources, margin)
        num, *chosen = lax.optimization_barrier((num, *chosen))
        first = swap(chosen[0], 3, 2)
        early = swap(chosen[2], 1)
        num, den = more_attention(
            (place, local_cols, tables[1]),
            [first_half],
            w,
            local_q,
            num,
            den,
            (keys, values),
            split,
            listed,
        )
        second_half, num, den, edge_rows, wanted_pair, second = lax.optimization_barrier(
            (second_half, num, den, edge_rows, wanted_pair, chosen[1])
        )
        outward = [(2 * i, 2 * i + 2) for i in range(blocks - 1)]
        outward += [(2 * i + 1, 2 * i - 1) for i in range(1, blocks)]
        other_halo = lax.ppermute(edge_rows, ("node", "head"), outward)
        wanted_pair = swap(wanted_pair, 0)
        sources = [features, first_half, second_half]
        jobs = ((1, 1, (1,)), (2, 2, (1,)), (0, 0, (0, 1)))
        late, direct, pair = select(place, jobs, share, [wanted_pair] + wanted, sources)
        num, first, early, late = lax.optimization_barrier((num, first, early, late))
        second = swap(second, 2, 3)
        first_beside = other(first)
        late = swap(late, 1)
        num, pair, other_halo = lax.optimization_barrier((num, pair, other_halo))
        pair = swap(pair, 0)
        num, den = more_attention(
            (place, local_cols, tables[2]),
            [second_half, other_halo, halo],
            w,
            local_q,
            num,
            den,
            (),
            split,
            listed,
        )
        num, den = expand_attention(
            place, exp_rows, spots[0], [pair, first, early], expand_q, num, den, w, False, None
        )
        second, direct, num, den = lax.optimization_barrier((second, direct, num, den))
        direct = lax.ppermute(direct, "node", [(i, i ^ flips[2]) for i in range(0, blocks, 2)])
        sides = [(4 * i + 2 + side, 4 * i + 3 - side) for i in range(blocks // 2) for side in (0, 1)]
        second_beside = lax.ppermute(second, ("node", "head"), sides)
        sources = [None, [late, second, first_beside], [direct, second_beside]]
    else:
        place = jnp.stack([here, block]).astype(jnp.int32)
        column = jnp.arange(tiles + 2 * HT, dtype=jnp.int32) - HT
        usable = block * tiles + column
        usable = jnp.logical_and(usable >= 0, usable < blocks * tiles)
        own = column // own_tiles == here
        w = jnp.transpose(w_key_value, (1, 0, 2))
        gather = lambda x: lax.all_gather(x, "head", axis=0, tiled=True)
        scales = lax.all_gather(scales, "head", axis=1, tiled=True)
        full = gather(features)
        before = lax.ppermute(full[-margin:], "node", [(i, i + 1) for i in range(blocks - 1)])
        after = lax.ppermute(full[:margin], "node", [(i + 1, i) for i in range(blocks - 1)])
        received = [gather(swap(features, m)) for m in range(MATCH)]
        sources = [None, received[:2], received[2:]]
        matching = jnp.arange(MATCH, dtype=jnp.int32)[:, None]
        spots = [
            None,
            jnp.where(matching < 2, matching * tiles + exp_cols, -1),
            jnp.where(matching < 2, -1, (matching - 2) * tiles + exp_cols),
        ]
        where_own = jnp.where(own, column - here * own_tiles, -1)
        where_rest = jnp.where(jnp.logical_and(usable, jnp.logical_not(own)), column + HT, -1)
        local_cols = local_cols.reshape(-1)
        num, den, keys, values, local_q, expand_q = own_attention(
            (place, local_cols, jnp.stack([where_own] * 2)),
            features,
            w,
            w_query,
            scales,
            split,
            listed,
        )
        num, den = more_attention(
            (place, local_cols, jnp.stack([where_rest] * 2)),
            [before, full, after],
            w,
            local_q,
            num,
            den,
            (),
            split,
            listed,
        )
    num, den, out = expand_attention(
        place, exp_rows, spots[1], sources[1], expand_q, num, den, w, True, None
    )
    return expand_attention(
        place, exp_rows, spots[2], sources[2], expand_q, num, den, w, True, out
    )


def solution(mesh):
    return jax.shard_map(
        local,
        mesh=mesh,
        in_specs=(
            P(("node", "head"), None),
            P(),
            P(),
            P("head"),
            P("head"),
            P("node", None),
            P("node", None, None),
            P("node", None, None),
        ),
        out_specs=P(("node", "head"), None),
        check_vma=False,
    )
```
